32 devices in a mesh: lat: 4 (over y, x), lon: 4 (over z), mem: 2 (over core).
Axes of the slice: x: 2, y: 2, z: 4, core: 2. Of those that a mesh axis runs over, the one named last changes fastest.
Arguments:
- velo: float32 [2, 4, 128, 2048], P(None, None, 'lat', 'lon'), may hold values from -6 to 6
- temp: float32 [4, 128, 2048], P(None, 'lat', 'lon'), may hold values from -6 to 6
- land: int32 [128, 2048], P('lat', 'lon'), may hold values 0 or 1
- target: bfloat16 [2, 4, 32, 512], P(None, None, 'lat', 'lon'), may hold values from -3 to 3
- w_first: bfloat16 [4, 9, 64, 3], P('mem'), may hold values from -1.25 to 1.25
- w_middle: bfloat16 [4, 9, 64, 64], P('mem'), may hold values from -0.25 to 0.25
- w_last: bfloat16 [4, 9, 2, 64], P('mem'), may hold values from -0.25 to 0.25
Outputs:
- velo_next: float32 [2, 4, 128, 2048], P(None, None, 'lat', 'lon')
- temp_next: float32 [4, 128, 2048], P(None, 'lat', 'lon')
- grad_first: float32 [4, 9, 64, 3], P('mem')
- grad_middle: float32 [4, 9, 64, 64], P('mem')
- grad_last: float32 [4, 9, 2, 64], P('mem')
The draws below stay inside these ranges and needn't reach their ends.
All inputs are finite; a program needn't handle non-finite values. No bound on the sum of `land` on one device may be relied on, other than what follows from the above.
Results may differ from the reference program's by a relative error of at most 0.0003.
Values may be sent and summed in bfloat16 or wider, within the bound.
No kernel may reach another device: no remote copies, remote signals or barrier semaphores. Data moves between devices by JAX's collectives and lax.ppermute only.
A program may use at most 128 MiB of HBM per device.

```python
import math
import jax
import jax.numpy as jnp
from jax import lax

LEV = 4
COARSE = 4
HID = 64
MEMBERS = 4
NY = 128
NX = 2048
NYC = 32
NXC = 512


def touch_ends(drawn, stream_key, least, largest):
    index_at = [jax.random.randint(jax.random.fold_in(stream_key, axis), (), 0, length) for axis, length in enumerate(drawn.shape)]
    longest = drawn.shape.index(max(drawn.shape))
    beside = index_at[:longest] + [(index_at[longest] + 1) % drawn.shape[longest]] + index_at[longest + 1:]
    return drawn.at[tuple(index_at)].set(least).at[tuple(beside)].set(largest)


def block_levels(own_key, extent, split, low, largest):
    level, own = 1.0, jax.random.fold_in(own_key, 6)
    for dim, shards_of in split:
        heights = jnp.exp(jax.random.uniform(jax.random.fold_in(own, dim), (shards_of,), jnp.float32, low / len(split), largest / len(split)))
        level = level * jnp.repeat(heights, extent[dim] // shards_of).reshape([-1 if axis == dim else 1 for axis in range(len(extent))])
    return level


def gaussian(stream_key, dims, scale, reach, split=(), held_as=jnp.bfloat16):
    drawn = jax.random.normal(stream_key, dims, jnp.float32) * scale
    if len(split) > 0:
        drawn = block_levels(stream_key, dims, split, -0.22, 0.18) * drawn
    return jnp.clip(drawn, min=-reach, max=reach).astype(held_as)


def setup_inputs(seed: int = 0) -> dict:
    seeds = jax.random.split(jax.random.key(seed), 8)
    return {
        "velo": gaussian(seeds[0], (2, LEV, NY, NX), 1.0, 6.0, ((2, 4), (3, 4)), jnp.float32),
        "temp": gaussian(seeds[1], (LEV, NY, NX), 1.0, 6.0, ((1, 4), (2, 4)), jnp.float32),
        "land": touch_ends((jax.random.randint(seeds[2], (NY, NX), 0, 5) < 4).astype(jnp.int32), jax.random.fold_in(seeds[2], 1), 0, 1),
        "target": gaussian(seeds[3], (2, LEV, NYC, NXC), 0.5, 3.0, ((2, 4), (3, 4))),
        "w_first": gaussian(seeds[4], (MEMBERS, 9, HID, 3), 27 ** -0.5, 1.25, ((0, 2),)),
        "w_middle": gaussian(seeds[5], (MEMBERS, 9, HID, HID), (9 * HID) ** -0.5, 0.25, ((0, 2),)),
        "w_last": gaussian(seeds[6], (MEMBERS, 9, 2, HID), (9 * HID) ** -0.5, 0.25, ((0, 2),)),
    }


def pad_coarse(x):
    x = jnp.pad(x, ((0, 0), (1, 1), (0, 0)))
    return jnp.concatenate([x[..., -1:], x, x[..., :1]], axis=-1)

def conv_sum(padded, weights, sign):
    height = padded.shape[-2] - 2
    width = padded.shape[-1] - 2
    total = None
    for a in (-1, 0, 1):
        for b in (-1, 0, 1):
            k = (a + 1) * 3 + (b + 1)
            piece = padded[:, 1 + sign * a:1 + sign * a + height, 1 + sign * b:1 + sign * b + width]
            if sign > 0:
                term = jnp.einsum('oc,cyx->oyx', weights[k].astype(jnp.float32), piece.astype(jnp.float32))
            else:
                term = jnp.einsum('oc,oyx->cyx', weights[k].astype(jnp.float32), piece.astype(jnp.float32))
            total = term if total is None else total + term
    return total

def weight_grad(cotangent, padded):
    height = cotangent.shape[-2]
    width = cotangent.shape[-1]
    result = []
    for a in (-1, 0, 1):
        for b in (-1, 0, 1):
            piece = padded[:, 1 + a:1 + a + height, 1 + b:1 + b + width]
            result.append(jnp.einsum('oyx,cyx->oc', cotangent.astype(jnp.float32), piece.astype(jnp.float32)))
    return jnp.stack(result, 0)

def reference(velo, temp, land, target, w_first, w_middle, w_last):
    fields = jnp.concatenate([velo, temp[None]], 0)
    rows = fields.shape[2]
    cols = fields.shape[3]
    coarse = fields.reshape(3, LEV, rows // COARSE, COARSE, cols // COARSE, COARSE).mean(axis=(3, 5)).astype(jnp.bfloat16)
    count = 2.0 * LEV * (rows // COARSE) * (cols // COARSE)
    coarse_levels = jnp.transpose(coarse, (1, 0, 2, 3))
    target_levels = jnp.transpose(target, (1, 0, 2, 3))

    def member_pass(weights):
        wf, wm, wl = weights

        def level_pass(inputs):
            x_level, goal = inputs
            xpad = pad_coarse(x_level)
            hidden_one = jnp.tanh(conv_sum(xpad, wf, 1)).astype(jnp.bfloat16)
            hpad_one = pad_coarse(hidden_one)
            hidden_two = jnp.tanh(conv_sum(hpad_one, wm, 1)).astype(jnp.bfloat16)
            hpad_two = pad_coarse(hidden_two)
            predict = conv_sum(hpad_two, wl, 1)
            cot_three = ((predict - goal.astype(jnp.float32)) * (2.0 / count)).astype(jnp.bfloat16)
            grad_three = weight_grad(cot_three, hpad_two)
            two_f = hidden_two.astype(jnp.float32)
            cot_two = (conv_sum(pad_coarse(cot_three), wl, -1) * (1.0 - two_f * two_f)).astype(jnp.bfloat16)
            grad_two = weight_grad(cot_two, hpad_one)
            one_f = hidden_one.astype(jnp.float32)
            cot_one = (conv_sum(pad_coarse(cot_two), wm, -1) * (1.0 - one_f * one_f)).astype(jnp.bfloat16)
            grad_one = weight_grad(cot_one, xpad)
            return (predict, grad_one, grad_two, grad_three)
        preds, g_one, g_two, g_three = lax.map(level_pass, (coarse_levels, target_levels))
        return (preds, lax.optimization_barrier(jnp.sum(g_one, 0)), lax.optimization_barrier(jnp.sum(g_two, 0)), lax.optimization_barrier(jnp.sum(g_three, 0)))
    preds, grad_first, grad_middle, grad_last = lax.map(member_pass, (w_first, w_middle, w_last))
    members = w_first.shape[0]
    mean_force = jnp.transpose(lax.optimization_barrier(jnp.sum(preds, 0)), (1, 0, 2, 3)) / members
    force = jnp.repeat(jnp.repeat(mean_force, COARSE, axis=2), COARSE, axis=3)
    padded = jnp.pad(fields, ((0, 0), (0, 0), (1, 1), (0, 0)))
    padded = jnp.concatenate([padded[..., -1:], padded, padded[..., :1]], axis=-1)
    centre = padded[:, :, 1:-1, 1:-1]
    east = padded[:, :, 1:-1, 2:]
    west = padded[:, :, 1:-1, :-2]
    north = padded[:, :, 2:, 1:-1]
    south = padded[:, :, :-2, 1:-1]
    laplace = east + west + north + south - 4.0 * centre
    press = -jnp.cumsum(0.5 * padded[2], axis=0)
    grad_x = (press[:, 1:-1, 2:] - press[:, 1:-1, :-2]) / 2.0
    grad_y = (press[:, 2:, 1:-1] - press[:, :-2, 1:-1]) / 2.0
    row_ids = jnp.arange(rows).astype(jnp.float32)
    coriolis = jnp.sin(-math.pi / 2 + math.pi * (row_ids + 0.5) / rows)[:, None]
    wet = land.astype(jnp.float32)
    u_now = centre[0]
    v_now = centre[1]
    t_now = centre[2]
    u_next = u_now + 0.1 * wet * (coriolis * v_now - grad_x + 0.5 * laplace[0] + force[0])
    v_next = v_now + 0.1 * wet * (-coriolis * u_now - grad_y + 0.5 * laplace[1] + force[1])
    advect = u_now * (east[2] - west[2]) / 2.0 + v_now * (north[2] - south[2]) / 2.0
    t_next = t_now + 0.1 * wet * (-advect + 0.3 * laplace[2])
    return (jnp.stack([u_next, v_next], 0), t_next, grad_first, grad_middle, grad_last)
```

```python
import functools
import itertools
import math

import jax
import jax.numpy as jnp
from jax import lax
from jax.experimental import pallas as pl
from jax.experimental.pallas import tpu as pltpu
from jax.sharding import PartitionSpec as P

COARSE = 4
HALO = 5
SIDE = 16
F32 = jnp.float32
BF16 = jnp.bfloat16
HIGH = lax.Precision.HIGHEST
VMEM_LIMIT = 48 * 1024 * 1024


def dot(a, b, **kw):
    return jnp.dot(a, b, preferred_element_type=F32, **kw)


def dot_nt(a, b):
    return lax.dot_general(a, b, (((1,), (1,)), ((), ())), preferred_element_type=F32)


def lanes_of(shape):
    return lax.broadcasted_iota(jnp.int32, shape, len(shape) - 1)


def subs_of(shape):
    return lax.broadcasted_iota(jnp.int32, shape, len(shape) - 2)


def heads_up(axis):
    return (lax.axis_index(axis) + lax.axis_index("mem")) % 2 == 0


def coarse_kernel(velo, temp, target, own, message, fine):
    levels, rows, cols = temp.shape
    height, width = rows // COARSE, cols // COARSE
    vregs = levels + 1
    pool_r = subs_of((cols, width)) // COARSE
    pool = jnp.where(pool_r == lanes_of((cols, width)), F32(1.0 / COARSE**2), F32(0.0))

    def field(f):
        return temp if f == 2 else velo.at[f]

    means = []
    for f in range(3):
        ref = field(f)
        pieces = []
        for j in range(cols // 128):
            fine[j] = ref[:, :, 128 * j : 128 * (j + 1)].reshape(levels * rows, 128)
            part = None
            for s in range(COARSE):
                piece = fine[j, pl.ds(s, levels * height, stride=COARSE), :]
                part = piece if part is None else part + piece
            pieces.append(part)
        means.append(jnp.concatenate(pieces, 1))
    mean = dot(jnp.concatenate(means, 0), pool, precision=HIGH)
    mean = mean.astype(BF16).astype(F32)

    lane = lanes_of((height, 128))

    def place(tiles):
        pieces = []
        for j in range(vregs):
            value = jnp.zeros((height, 128), F32)
            if j < levels:
                moved = pltpu.roll(tiles[j], 32 * j + SIDE, 1)
                value = jnp.where(lane >= 32 * j + SIDE, moved, value)
            if j > 0:
                moved = pltpu.roll(tiles[j - 1], 32 * (j - 1) + SIDE, 1)
                value = jnp.where(lane < 32 * (j - 1) + SIDE, moved, value)
            pieces.append(value)
        return pieces

    for ch in range(8):
        if ch < 4:
            tiles = [target[ch % 2, l].astype(F32) for l in range(levels)]
        elif ch < 7:
            base = (ch - 4) * levels * height
            tiles = [mean[base + l * height : base + (l + 1) * height] for l in range(levels)]
        if ch < 7:
            pieces = place(tiles)
        else:
            pieces = [jnp.zeros((height, 128), F32)] * vregs
        for j in range(vregs):
            own[j, pl.ds(ch, height, stride=8), :] = pieces[j]
    lane = lanes_of((8 * height, 128))
    to_west = jnp.zeros((8 * height, 128), F32)
    to_east = jnp.zeros((8 * height, 128), F32)
    for l in range(levels):
        here = (lane >= 32 * l) & (lane < 32 * (l + 1))
        to_west = jnp.where(here, own[l], to_west)
        to_east = jnp.where(here, own[l + 1], to_east)
    lane = lanes_of((rows, 128))
    first = jnp.zeros((rows, 128), F32)
    last = jnp.zeros((rows, 128), F32)
    for f in range(3):
        ref = field(f)
        for l in range(levels):
            n = f * levels + l
            first = jnp.where(lane == n, pltpu.roll(ref[l, :, 0:128], n, 1), first)
            last = jnp.where(lane == n, pltpu.roll(ref[l, :, cols - 128 :], n + 1, 1), last)
    to_east = jnp.concatenate([to_east, last], 0)
    to_west = jnp.concatenate([to_west, first], 0)
    message[...] = jnp.where(heads_up("lon"), to_east, to_west)


def merge_kernel(velo, temp, own, got, other, full, message):
    levels, rows, cols = temp.shape
    vregs, tall = own.shape[:2]
    ahead = heads_up("lon")
    right = jnp.where(ahead, got[0:tall, :], other[0:tall, :])
    left = jnp.where(ahead, other[0:tall, :], got[0:tall, :])
    lane = lanes_of((tall, 128))
    for j in range(vregs):
        value = own[j]
        if j < levels:
            at = 32 * j + SIDE
            value = jnp.where((lane >= at - HALO) & (lane < at), left, value)
        if j > 0:
            at = 32 * (j - 1) + SIDE
            value = jnp.where((lane >= at) & (lane < at + HALO), right, value)
        full[j] = value
    deep = 8 * HALO
    ahead = heads_up("lat")
    for j in range(vregs):
        message[deep * j : deep * (j + 1), :] = jnp.where(ahead, full[j, tall - deep :, :], full[j, :deep, :])
    for f in range(3):
        ref = temp if f == 2 else velo.at[f]
        edge = jnp.where(ahead, ref[:, rows - 1, :], ref[:, 0, :])
        for j in range(cols // 128):
            at = deep * vregs + 16 * j + levels * f
            message[at : at + levels, :] = edge[:, 128 * j : 128 * (j + 1)]


def closure_kernel(
    scale, total_rows,
    full, got, other, wf, wm, wb, wl, wlt,
    force, *rest,
):
    nlat = lax.axis_size("lat")
    sends, (mine, xf, xb, h1, h2, yl, gb, d2, pf, gm, gf, gl, packed) = rest[: nlat - 1], rest[nlat - 1 :]
    vregs = full.shape[0]
    height = full.shape[1] // 8
    wide = 128 * vregs
    span = height + 2 * HALO
    first_row = lax.axis_index("lat") * height

    def inside(row):
        at = first_row + row
        return jnp.where((at >= 0) & (at < total_rows), F32(1.0), F32(0.0))

    ahead = heads_up("lat")
    deep = 8 * HALO
    for j in range(vregs):
        cols = slice(128 * j, 128 * (j + 1))
        near, far = got[deep * j : deep * (j + 1), :], other[deep * j : deep * (j + 1), :]
        xf[0:deep, cols] = jnp.where(ahead, far, near)
        xf[deep : deep + 8 * height, cols] = full[j]
        xf[deep + 8 * height :, cols] = jnp.where(ahead, near, far)

    sub = subs_of((8, wide))
    lane = lanes_of((1, wide))
    within = lane % (128 + 2 * SIDE)
    tile = (within >= SIDE) & (within < SIDE + 128)
    tile_f = jnp.where(tile, F32(1.0), F32(0.0))
    tile_b = tile_f.astype(BF16)

    def rows_of(ref, start, size, step):
        return ref[pl.ds(pl.multiple_of(start * step, step), size), :]

    def build(r, _):
        x = rows_of(xf, r, 8, 8)
        one = jnp.where(sub < 4, pltpu.roll(pltpu.roll(x, 1, 1), 4, 0), x)
        two = pltpu.roll(pltpu.roll(x, wide - 1, 1), 4, 0)
        xb[pl.ds(pl.multiple_of(16 * r, 16), 16), :] = jnp.concatenate([one, two], 0).astype(BF16)
        return 0

    lax.fori_loop(0, span, build, 0, unroll=2)

    def stage_one(q, _):
        pre = dot(wf[...], rows_of(xb, q, 48, 16))
        h = jnp.tanh(pre) * inside(q - 4)
        h1[pl.ds(pl.multiple_of(128 * q, 128), 128), :] = h.astype(BF16)
        return 0

    lax.fori_loop(0, height + 8, stage_one, 0)

    def stack(ref, r, m):
        return jnp.concatenate(
            [ref[pl.ds(pl.multiple_of(128 * (r + a) + 64 * m, 64), 64), :] for a in range(3)], 0
        )

    def stage_two(p, _):
        ok = inside(p - 3)
        halves = []
        for m in range(2):
            y = dot(wm[m], stack(h1, p, m))
            pre = pltpu.roll(y[0:64], 1, 1) + y[64:128] + pltpu.roll(y[128:192], wide - 1, 1)
            halves.append((jnp.tanh(pre) * ok).astype(BF16))
        row = jnp.concatenate(halves, 0)
        h2[pl.ds(pl.multiple_of(128 * p, 128), 128), :] = row
        yl[pl.ds(pl.multiple_of(72 * p, 8), 72), :] = dot(wl[...], row)
        return 0

    lax.fori_loop(0, height + 6, stage_two, 0)

    def stage_three(s, _):
        def part(a):
            return yl[pl.ds(pl.multiple_of(72 * (s + a) + 24 * a, 8), 24), :]

        z = part(0) + part(1) + part(2)
        pred = pltpu.roll(z[0:8], 1, 1) + z[8:16] + pltpu.roll(z[16:24], wide - 1, 1)
        goal = rows_of(xf, s + 3, 8, 8)
        g = ((pred - goal) * scale * inside(s - 2)).astype(BF16).astype(F32)
        one = jnp.where(sub < 4, pltpu.roll(g, wide - 1, 1), pltpu.roll(g, 4, 0))
        two = pltpu.roll(g, 1, 1)
        gb[pl.ds(pl.multiple_of(16 * s, 16), 16), :] = jnp.concatenate([one, two], 0).astype(BF16)
        both = pred + pltpu.roll(pred, 6, 0)
        pf[pl.ds(pl.multiple_of(8 * s, 8), 8), :] = both
        return 0

    lax.fori_loop(0, height + 4, stage_three, 0)
    force[...] = jnp.concatenate(
        [pf[8 * (r + 2) : 8 * (r + 2) + 2, :] for r in range(height)], 0
    ).astype(BF16)

    gl[...] = jnp.zeros_like(gl)
    gf[...] = jnp.zeros_like(gf)
    gm[...] = jnp.zeros_like(gm)

    def stage_four(u, _):
        g48 = rows_of(gb, u, 48, 16)
        hidden = rows_of(h2, u + 2, 128, 128).astype(F32)
        d = dot(wlt[...], g48) * (1.0 - hidden * hidden) * inside(u - 1)
        d2[pl.ds(pl.multiple_of(128 * u, 128), 128), :] = d.astype(BF16)
        return 0

    lax.fori_loop(0, height + 2, stage_four, 0)

    def stage_five(j, _):
        g48 = rows_of(gb, j + 1, 48, 16) * tile_b
        gl[...] += dot_nt(g48, rows_of(h2, j + 3, 128, 128))
        halves = []
        for m in range(2):
            y = dot(wb[m], stack(d2, j, m))
            pre = pltpu.roll(y[0:64], wide - 1, 1) + y[64:128] + pltpu.roll(y[128:192], 1, 1)
            hidden = h1[pl.ds(pl.multiple_of(128 * (j + 4) + 64 * m, 64), 64), :].astype(F32)
            halves.append((pre * (1.0 - hidden * hidden) * tile_f).astype(BF16))
            d = d2[pl.ds(pl.multiple_of(128 * (j + 1) + 64 * m, 64), 64), :] * tile_b
            moved = jnp.concatenate([pltpu.roll(d, wide - 1, 1), d, pltpu.roll(d, 1, 1)], 0)
            gm[m] += dot_nt(moved, stack(h1, j + 3, m))
        gf[...] += dot_nt(rows_of(xb, j + 4, 48, 16), jnp.concatenate(halves, 0))
        return 0

    lax.fori_loop(0, height, stage_five, 0)
    for m in range(2):
        packed[192 * m : 192 * (m + 1), :] = gm[m, :, 0:128]
    packed[384:576, :] = jnp.concatenate([gm[0, :, 128:192], gm[1, :, 128:192]], 1)
    pieces = [gf[16 * a : 16 * a + 12, :] for a in range(3)]
    last = gl[...]
    last = jnp.where(lanes_of(last.shape) < 64, last, pltpu.roll(last, 46, 0))
    pieces += [last[16 * s + 4 * b : 16 * s + 4 * b + 2] for s in range(3) for b in range(3)]
    pieces.append(jnp.zeros((packed.shape[0] - 576 - 54, 128), F32))
    packed[576:, :] = jnp.concatenate(pieces, 0)
    part = packed.shape[0] // nlat
    me = lax.axis_index("lat")
    for k, ref in enumerate((mine, *sends)):
        ref[...] = packed[pl.ds(pl.multiple_of((me ^ k) * part, 8), part), :]


def finish_kernel(*refs):
    nlat = lax.axis_size("lat")
    parts, (first, middle, last, packed) = refs[:nlat], refs[nlat:]
    part = parts[0].shape[0]
    me = lax.axis_index("lat")
    for k, ref in enumerate(parts):
        packed[pl.ds(pl.multiple_of((me ^ k) * part, 8), part), :] = ref[...]
    for m in range(2):
        for b in range(3):
            two = packed[192 * m + 64 * b : 192 * m + 64 * (b + 1), :]
            third = packed[384 + 64 * b : 384 + 64 * (b + 1), :]
            middle[m, b] = two[:, 0:64]
            middle[m, 3 + b] = two[:, 64:128]
            middle[m, 6 + b] = third[:, 64 * m : 64 * (m + 1)]
    rows = packed[576:640, :]
    turned = rows.T
    for m in range(2):
        for k in range(9):
            first[m, k] = turned[64 * m : 64 * (m + 1), 4 * k : 4 * k + 3]
            at = 36 + 2 * (3 * (2 - k // 3) + k % 3)
            last[m, k] = rows[at : at + 2, 64 * m : 64 * (m + 1)]


def ocean_kernel(
    total_rows, members,
    velo, temp, land, mine, other, got_lon, other_lon, got_lat, other_lat,
    velo_next, temp_next,
):
    levels, rows, cols = temp.shape
    at = got_lon.shape[0] - rows
    ahead = heads_up("lon")
    ceast = jnp.where(ahead, got_lon[at:, :], other_lon[at:, :])
    cwest = jnp.where(ahead, other_lon[at:, :], got_lon[at:, :])
    ahead = heads_up("lat")
    at = got_lat.shape[0] - 16 * (cols // 128)
    near, far = (
        jnp.concatenate([ref[at + 16 * j : at + 16 * (j + 1), :] for j in range(cols // 128)], 1)
        for ref in (got_lat, other_lat)
    )
    rnorth, rsouth = jnp.where(ahead, near, far), jnp.where(ahead, far, near)
    height, width = rows // COARSE, cols // COARSE
    row = subs_of((rows, cols))
    lane = lanes_of((rows, cols))
    ids = (lax.axis_index("lat") * rows + subs_of((rows, 128))).astype(F32)
    coriolis = jnp.sin(F32(-math.pi / 2) + F32(math.pi) * (ids + 0.5) / F32(total_rows))
    coriolis = jnp.concatenate([coriolis] * (cols // 128), 1)
    wet = land[...].astype(F32) * 0.1
    up = [
        jnp.where(lanes_of((rows, 2 * height)) == subs_of((rows, 2 * height)) // COARSE * 2 + o, F32(1.0), F32(0.0)).astype(BF16)
        for o in range(2)
    ]
    tall = [[dot(u, ref[...]).astype(BF16) for ref in (mine, other)] for u in up]
    spread_k = subs_of((256, cols))
    spread_i = lanes_of((256, cols)) // COARSE

    def neighbours(q, n):
        east = jnp.where(lane == cols - 1, ceast[:, n : n + 1], pltpu.roll(q, cols - 1, 1))
        west = jnp.where(lane == 0, cwest[:, n : n + 1], pltpu.roll(q, 1, 1))
        north = jnp.where(row == rows - 1, rnorth[n : n + 1, :], pltpu.roll(q, rows - 1, 0))
        south = jnp.where(row == 0, rsouth[n : n + 1, :], pltpu.roll(q, 1, 0))
        return east, west, north, south

    cum_x = cum_y = None
    for l in range(levels):
        u, v, t = velo[0, l], velo[1, l], temp[l]
        ue, uw, un, us = neighbours(u, l)
        ve, vw, vn, vs = neighbours(v, levels + l)
        te, tw, tn, ts = neighbours(t, 2 * levels + l)
        dx, dy = te - tw, tn - ts
        cum_x = dx if cum_x is None else cum_x + dx
        cum_y = dy if cum_y is None else cum_y + dy
        spread = jnp.where(spread_k == spread_i + (32 * l + SIDE), F32(1.0), F32(0.0)).astype(BF16)
        f = []
        for o in range(2):
            total = None
            for part in tall[o]:
                term = dot(part[:, 128 * l : 128 * (l + 2)], spread)
                total = term if total is None else total + term
            f.append(total * (1.0 / members))
        lap_u = ue + uw + un + us - 4.0 * u
        lap_v = ve + vw + vn + vs - 4.0 * v
        lap_t = te + tw + tn + ts - 4.0 * t
        velo_next[0, l] = u + wet * (coriolis * v + 0.25 * cum_x + 0.5 * lap_u + f[0])
        velo_next[1, l] = v + wet * (0.25 * cum_y - coriolis * u + 0.5 * lap_v + f[1])
        temp_next[l] = t + wet * (0.3 * lap_t - 0.5 * (u * dx + v * dy))


def prepare(w_first, w_middle, w_last):
    m = w_first.shape[0]
    hid = w_middle.shape[-1]
    eye = jnp.eye(m, dtype=BF16)
    wf = w_first.reshape(m, 3, 3, hid, 3)
    wf = jnp.transpose(wf, (0, 3, 1, 2, 4)).reshape(m * hid, 3, 3, 3)
    wf = jnp.pad(wf, ((0, 0), (0, 0), (0, 0), (0, 1))).reshape(m * hid, 3, 12)
    wf = jnp.pad(wf, ((0, 0), (0, 0), (0, 4))).reshape(m * hid, 48)
    mid = w_middle.reshape(m, 3, 3, hid, hid)
    wm = jnp.transpose(mid, (0, 2, 3, 1, 4)).reshape(m, 3 * hid, 3 * hid)
    wb = jnp.transpose(mid[:, ::-1], (0, 2, 4, 1, 3)).reshape(m, 3 * hid, 3 * hid)
    last = w_last.reshape(m, 3, 3, 2, hid)
    wl = jnp.einsum("mn,maboc->abmonc", eye, last).reshape(3, 3, 2 * m, m * hid)
    wl = jnp.pad(wl, ((0, 0), (0, 0), (0, 8 - 2 * m), (0, 0))).reshape(72, m * hid)
    wlt = jnp.einsum("mn,maboc->mcabno", eye, last[:, ::-1]).reshape(m * hid, 3, 6 * m)
    wlt = jnp.pad(wlt, ((0, 0), (0, 0), (0, 16 - 6 * m))).reshape(m * hid, 48)
    return wf, wm, wb, wl, wlt


def swap_pairs(axis, wrap):
    names = ("lat", "lon", "mem")
    sizes = [lax.axis_size(name) for name in names]
    where = names.index(axis)
    pairs = []
    for index in itertools.product(*(range(n) for n in sizes)):
        place = list(index)
        place[where] += 1 if (index[where] + index[2]) % 2 == 0 else -1
        if wrap:
            place[where] %= sizes[where]
        if 0 <= place[where] < sizes[where]:
            flat = [(i[0] * sizes[1] + i[1]) * sizes[2] + i[2] for i in (index, place)]
            pairs.append(tuple(flat))
    return pairs


def swap(value, axis, wrap):
    got = lax.ppermute(value, ("lat", "lon", "mem"), swap_pairs(axis, wrap))
    return got, swap_cores(got)


def swap_cores(value):
    return lax.ppermute(value, "mem", [(i, i ^ 1) for i in range(lax.axis_size("mem"))])


def partner(value, axis, k):
    return lax.ppermute(value, axis, [(i, i ^ k) for i in range(lax.axis_size(axis))])


def tree_sum(values):
    while len(values) > 1:
        values = [sum(values[i : i + 2][1:], values[i]) for i in range(0, len(values), 2)]
    return values[0]


def per_device(velo, temp, land, target, w_first, w_middle, w_last):
    levels, rows, cols = temp.shape
    height, width = rows // COARSE, cols // COARSE
    wide = levels * (width + 2 * SIDE)
    vregs = wide // 128
    members = w_first.shape[0] * lax.axis_size("mem")
    nlat, nlon = lax.axis_size("lat"), lax.axis_size("lon")
    total_coarse = height * nlat
    count = 2.0 * levels * total_coarse * width * nlon
    params = pltpu.CompilerParams(vmem_limit_bytes=VMEM_LIMIT)
    vm = pltpu.VMEM

    def f32(*shape):
        return jax.ShapeDtypeStruct(shape, F32)

    own, message = pl.pallas_call(
        coarse_kernel,
        out_shape=(f32(vregs, 8 * height, 128), f32(8 * height + rows, 128)),
        scratch_shapes=[vm((cols // 128, levels * rows, 128), F32)],
        compiler_params=params,
        name="coarse",
    )(velo, temp, target)
    got_lon, other_lon = swap(message, "lon", True)
    full, message = pl.pallas_call(
        merge_kernel,
        out_shape=(f32(vregs, 8 * height, 128), f32(8 * HALO * vregs + 16 * (cols // 128), 128)),
        compiler_params=params,
        name="merge",
    )(velo, temp, own, got_lon, other_lon)
    got_lat, other_lat = swap(message, "lat", False)

    weights = prepare(w_first, w_middle, w_last)
    total = 640
    part = total // nlat
    force, *sends, mine = pl.pallas_call(
        functools.partial(closure_kernel, 2.0 / count, total_coarse),
        out_shape=(jax.ShapeDtypeStruct((2 * height, wide), BF16), *[f32(part, 128)] * nlat),
        scratch_shapes=[
            vm((8 * (height + 2 * HALO), wide), F32),
            vm((16 * (height + 2 * HALO), wide), BF16),
            vm((128 * (height + 8), wide), BF16),
            vm((128 * (height + 6), wide), BF16),
            vm((72 * (height + 6), wide), F32),
            vm((16 * (height + 4), wide), BF16),
            vm((128 * (height + 2), wide), BF16),
            vm((8 * (height + 4), wide), F32),
            vm((2, 192, 192), F32),
            vm((48, 128), F32),
            vm((48, 128), F32),
            vm((total, 128), F32),
        ],
        compiler_params=params,
        name="closure",
    )(full, got_lat, other_lat, *weights)

    parts = [partner(value, "lat", k + 1) for k, value in enumerate(sends)]
    other = swap_cores(force)
    velo_next, temp_next = pl.pallas_call(
        functools.partial(ocean_kernel, rows * nlat, members),
        out_shape=(jax.ShapeDtypeStruct(velo.shape, F32), jax.ShapeDtypeStruct(temp.shape, F32)),
        cost_estimate=pl.CostEstimate(flops=10**8, bytes_accessed=4 * 10**6, transcendentals=0),
        compiler_params=params,
        name="ocean",
    )(velo, temp, land, force, other, got_lon, other_lon, got_lat, other_lat)

    summed = tree_sum([mine, *parts])
    summed = tree_sum([summed] + [partner(summed, "lon", k) for k in range(1, nlon)])
    parts = [summed] + [partner(summed, "lat", k) for k in range(1, nlat)]
    grads = pl.pallas_call(
        finish_kernel,
        out_shape=tuple(f32(*w.shape) for w in (w_first, w_middle, w_last)),
        scratch_shapes=[vm((total, 128), F32)],
        compiler_params=params,
        name="finish",
    )(*parts)
    return (velo_next, temp_next, *grads)


def solution(mesh):
    return jax.shard_map(
        per_device,
        mesh=mesh,
        in_specs=(
            P(None, None, "lat", "lon"),
            P(None, "lat", "lon"),
            P("lat", "lon"),
            P(None, None, "lat", "lon"),
            P("mem", None, None, None),
            P("mem", None, None, None),
            P("mem", None, None, None),
        ),
        out_specs=(
            P(None, None, "lat", "lon"),
            P(None, "lat", "lon"),
            P("mem", None, None, None),
            P("mem", None, None, None),
            P("mem", None, None, None),
        ),
        check_vma=False,
    )
```

```python
import functools
import itertools
import math

import jax
import jax.numpy as jnp
from jax import lax
from jax.experimental import pallas as pl
from jax.experimental.pallas import tpu as pltpu
from jax.sharding import PartitionSpec as P

COARSE = 4
HALO = 5
GROUP = 16
LEVELS = 32000.0
H1_ROWS = 4
SIDE = 16
F32 = jnp.float32
BF16 = jnp.bfloat16
HIGH = lax.Precision.HIGHEST
VMEM_LIMIT = 48 * 1024 * 1024
COARSE_LIMIT = 64 * 1024 * 1024 - 512 * 1024


def dot(a, b, **kw):
    return jnp.dot(a, b, preferred_element_type=F32, **kw)


def dot_nt(a, b):
    return lax.dot_general(a, b, (((1,), (1,)), ((), ())), preferred_element_type=F32)


def lanes_of(shape):
    return lax.broadcasted_iota(jnp.int32, shape, len(shape) - 1)


def subs_of(shape):
    return lax.broadcasted_iota(jnp.int32, shape, len(shape) - 2)


def heads_up(axis):
    return (lax.axis_index(axis) + lax.axis_index("mem")) % 2 == 0


def halves(x):
    high = x.astype(BF16).astype(F32)
    return [high, x - high]


def encode(x):
    coded, exponents = [], []
    for at in range(0, x.shape[0], GROUP):
        part = x[at : at + GROUP]
        most = jnp.max(jnp.abs(part), axis=0, keepdims=True)
        exponent = jnp.ceil(jnp.log2(jnp.maximum(most, 1e-30)))
        coded.append(jnp.round(part * (jnp.exp2(-exponent) * LEVELS)))
        exponents.append(exponent)
    exponents.append(jnp.zeros((GROUP - len(exponents), x.shape[1]), F32))
    return jnp.concatenate(coded + exponents, 0).astype(jnp.int32).astype(jnp.int16)


def decode(ref):
    value = ref[...].astype(jnp.int32).astype(F32)
    rows = value.shape[0] - GROUP
    scale = jnp.exp2(value[rows:]) * (1.0 / LEVELS)
    pieces = [value[at : at + GROUP] * scale[i : i + 1] for i, at in enumerate(range(0, rows, GROUP))]
    return jnp.concatenate(pieces, 0)


def coarse_kernel(
    velo_hbm, temp_hbm, target_hbm, own, to_lon, edges, velo, temp, target, fine, sems
):
    copies = [
        pltpu.make_async_copy(velo_hbm.at[0], velo.at[0], sems.at[0]),
        pltpu.make_async_copy(velo_hbm.at[1], velo.at[1], sems.at[1]),
        pltpu.make_async_copy(temp_hbm, temp, sems.at[2]),
        pltpu.make_async_copy(target_hbm, target, sems.at[3]),
    ]
    for copy in copies:
        copy.start()
    levels, rows, cols = temp.shape
    height, width = rows // COARSE, cols // COARSE
    vregs = levels + 1
    pool_r = subs_of((cols, width)) // COARSE
    pool = jnp.where(pool_r == lanes_of((cols, width)), F32(1.0 / COARSE**2), F32(0.0))

    def field(f):
        return temp if f == 2 else velo.at[f]

    means = []
    for f in range(3):
        copies[f].wait()
        ref = field(f)
        pieces = []
        for j in range(cols // 128):
            fine[j] = ref[:, :, 128 * j : 128 * (j + 1)].reshape(levels * rows, 128)
            part = None
            for s in range(COARSE):
                piece = fine[j, pl.ds(s, levels * height, stride=COARSE), :]
                part = piece if part is None else part + piece
            pieces.append(part)
        means.append(jnp.concatenate(pieces, 1))
    mean = dot(jnp.concatenate(means, 0), pool, precision=HIGH)
    mean = mean.astype(BF16).astype(F32)

    copies[3].wait()
    lane = lanes_of((height, 128))

    def place(tiles):
        pieces = []
        for j in range(vregs):
            value = jnp.zeros((height, 128), F32)
            if j < levels:
                moved = pltpu.roll(tiles[j], 32 * j + SIDE, 1)
                value = jnp.where(lane >= 32 * j + SIDE, moved, value)
            if j > 0:
                moved = pltpu.roll(tiles[j - 1], 32 * (j - 1) + SIDE, 1)
                value = jnp.where(lane < 32 * (j - 1) + SIDE, moved, value)
            pieces.append(value)
        return pieces

    for ch in range(8):
        if ch < 4:
            tiles = [target[ch % 2, l].astype(F32) for l in range(levels)]
        elif ch < 7:
            base = (ch - 4) * levels * height
            tiles = [mean[base + l * height : base + (l + 1) * height] for l in range(levels)]
        if ch < 7:
            pieces = place(tiles)
        else:
            pieces = [jnp.zeros((height, 128), F32)] * vregs
        for j in range(vregs):
            own[j, pl.ds(ch, height, stride=8), :] = pieces[j]
    lane = lanes_of((8 * height, 128))
    to_west = jnp.zeros((8 * height, 128), F32)
    to_east = jnp.zeros((8 * height, 128), F32)
    for l in range(levels):
        here = (lane >= 32 * l) & (lane < 32 * (l + 1))
        to_west = jnp.where(here, own[l], to_west)
        to_east = jnp.where(here, own[l + 1], to_east)
    lane = lanes_of((rows, 128))
    first = jnp.zeros((rows, 128), F32)
    last = jnp.zeros((rows, 128), F32)
    for f in range(3):
        ref = field(f)
        for l in range(levels):
            n = f * levels + l
            first = jnp.where(lane == n, pltpu.roll(ref[l, :, 0:128], n, 1), first)
            last = jnp.where(lane == n, pltpu.roll(ref[l, :, cols - 128 :], n + 1, 1), last)
    tall = 8 * height
    east, north = heads_up("lon"), heads_up("lat")
    cells = jnp.where(east, to_east, to_west)
    to_lon[...] = jnp.concatenate([cells] + halves(jnp.where(east, last, first)), 0).astype(BF16)
    line = [jnp.where(north, field(f)[:, rows - 1, :], field(f)[:, 0, :]) for f in range(3)]
    line = [part[:, 128 * j : 128 * (j + 1)] for j in range(cols // 128) for part in line]
    edges[...] = jnp.concatenate(line, 0)


def merge_kernel(own, got, other, edges, full, message):
    vregs, tall = own.shape[:2]
    levels, deep = vregs - 1, 8 * HALO
    ahead, north = heads_up("lon"), heads_up("lat")
    near, far = (ref[...].astype(F32)[0:tall] for ref in (got, other))
    right, left = jnp.where(ahead, near, far), jnp.where(ahead, far, near)
    lane = lanes_of((tall, 128))
    pieces = []
    for j in range(vregs):
        value = own[j]
        if j < levels:
            at = 32 * j + SIDE
            value = jnp.where((lane >= at - HALO) & (lane < at), left, value)
        if j > 0:
            at = 32 * (j - 1) + SIDE
            value = jnp.where((lane >= at) & (lane < at + HALO), right, value)
        full[j] = value
        pieces.append(jnp.where(north, value[tall - deep :], value[:deep]))
    pieces.append(jnp.zeros((-deep * vregs % 16, 128), F32))
    message[...] = jnp.concatenate(pieces + halves(edges[...]), 0).astype(BF16)


def closure_kernel(
    scale, total_rows,
    full, got, other, wf, wm, wb, wl, wlt,
    force, *rest,
):
    nlat = lax.axis_size("lat")
    sends, (mine, xf, xb, h1, h2, yl, gb, d2, pf, packed) = rest[: nlat - 1], rest[nlat - 1 :]
    vregs = full.shape[0]
    height = full.shape[1] // 8
    wide = 128 * vregs
    span = height + 2 * HALO
    first_row = lax.axis_index("lat") * height

    def inside(row):
        at = first_row + row
        return jnp.where((at >= 0) & (at < total_rows), F32(1.0), F32(0.0))

    deep = 8 * HALO
    north = heads_up("lat")
    got, other = got[...].astype(F32), other[...].astype(F32)
    for j in range(vregs):
        near, far = got[deep * j : deep * (j + 1)], other[deep * j : deep * (j + 1)]
        above, below = jnp.where(north, near, far), jnp.where(north, far, near)
        xf[:, 128 * j : 128 * (j + 1)] = jnp.concatenate([below, full[j], above], 0)

    sub = subs_of((8, wide))
    lane = lanes_of((1, wide))
    within = lane % (128 + 2 * SIDE)
    tile = (within >= SIDE) & (within < SIDE + 128)
    tile_f = jnp.where(tile, F32(1.0), F32(0.0))
    tile_b = tile_f.astype(BF16)

    def window(ref, row, rows, step):
        return ref[step * row : step * (row + rows), :]

    def quad(get, row, left):
        return get(row) if left <= 2 else jnp.concatenate([get(row), get(row + 2)], 1)

    for r in range(span):
        x = window(xf, r, 1, 8)
        one = jnp.where(sub < 4, pltpu.roll(pltpu.roll(x, 1, 1), 4, 0), x)
        two = pltpu.roll(pltpu.roll(x, wide - 1, 1), 4, 0)
        xb[16 * r : 16 * (r + 1), :] = jnp.concatenate([one, two], 0).astype(BF16)

    step = wf.shape[0] // 128
    for q in range(0, height + 8, step):
        pre = dot(wf[...], window(xb, q, step + 2, 16))
        for i in range(step):
            h = (jnp.tanh(pre[128 * i : 128 * (i + 1)]) * inside(q + i - 4)).astype(BF16)
            for m in range(2):
                h1[m, 64 * (q + i) : 64 * (q + i + 1), :] = h[64 * m : 64 * (m + 1)]

    def columns(y, rr, t, sign):
        part = [y[192 * rr + 64 * b : 192 * rr + 64 * (b + 1), wide * t : wide * (t + 1)] for b in range(3)]
        return pltpu.roll(part[0], sign % wide, 1) + part[1] + pltpu.roll(part[2], -sign % wide, 1)

    rows = height + 6
    for p in range(0, rows, 4):
        for m in range(2):
            y = dot(wm[m], quad(lambda r: h1[m, 64 * r : 64 * (r + 4), :], p, rows - p))
            for i in range(min(4, rows - p)):
                h = jnp.tanh(columns(y, i % 2, i // 2, 1)) * inside(p + i - 3)
                at = 128 * (p + i) + 64 * m
                h2[at : at + 64, :] = h.astype(BF16)
        for i in range(p, min(p + 4, rows), 2):
            yl[72 * i : 72 * (i + 2), :] = dot(wl[...], window(h2, i, 2, 128))

    for s in range(height + 4):
        z = sum(yl[72 * (s + a) + 24 * a : 72 * (s + a) + 24 * (a + 1), :] for a in range(3))
        pred = pltpu.roll(z[0:8], 1, 1) + z[8:16] + pltpu.roll(z[16:24], wide - 1, 1)
        goal = window(xf, s + 3, 1, 8)
        g = ((pred - goal) * scale * inside(s - 2)).astype(BF16).astype(F32)
        one = jnp.where(sub < 4, pltpu.roll(g, wide - 1, 1), pltpu.roll(g, 4, 0))
        two = pltpu.roll(g, 1, 1)
        gb[16 * s : 16 * (s + 1), :] = jnp.concatenate([one, two], 0).astype(BF16)
        if 2 <= s < height + 2:
            both = pred + pltpu.roll(pred, 6, 0)
            pf[2 * (s - 2) : 2 * (s - 1), :] = both[0:2]
    force[...] = pf[...].astype(BF16)

    for u in range(height + 2):
        hidden = window(h2, u + 2, 1, 128).astype(F32)
        d = dot(wlt[...], window(gb, u, 3, 16)) * (1.0 - hidden * hidden) * inside(u - 1)
        for m in range(2):
            d2[m, 64 * u : 64 * (u + 1), :] = d[64 * m : 64 * (m + 1)].astype(BF16)

    sum_l = sum_f = None
    sum_m = [None, None]

    def add(total, term):
        return term if total is None else total + term

    for j in range(0, height, 4):
        left = height - j
        g = quad(lambda r: window(gb, r + 1, 4, 16) * tile_b, j, left)
        sum_l = add(sum_l, dot_nt(g, quad(lambda r: window(h2, r + 3, 2, 128), j, left)))
        d1 = [[None, None] for _ in range(4)]
        for m in range(2):
            y = dot(wb[m], quad(lambda r: d2[m, 64 * r : 64 * (r + 4), :], j, left))
            for i in range(4):
                hidden = h1[m, 64 * (j + i + 4) : 64 * (j + i + 5), :].astype(F32)
                d = columns(y, i % 2, i // 2, -1) * (1.0 - hidden * hidden) * tile_f
                d1[i][m] = d.astype(BF16)

            def moved(r):
                pieces = []
                for i in range(2):
                    d = d2[m, 64 * (r + i + 1) : 64 * (r + i + 2), :] * tile_b
                    pieces += [pltpu.roll(d, wide - 1, 1), d, pltpu.roll(d, 1, 1)]
                return jnp.concatenate(pieces, 0)

            rhs = quad(lambda r: h1[m, 64 * (r + 3) : 64 * (r + 7), :], j, left)
            sum_m[m] = add(sum_m[m], dot_nt(quad(moved, j, left), rhs))
        x = quad(lambda r: window(xb, r + 4, 4, 16), j, left)
        sum_f = add(sum_f, dot_nt(x, quad(lambda r: jnp.concatenate(d1[r - j] + d1[r - j + 1], 0), j, left)))
    gl = sum_l[0:48, 0:128] + sum_l[16:64, 128:256]
    gf = sum_f[0:48, 0:128] + sum_f[16:64, 128:256]
    gm = [t[0:192, 0:192] + t[192:384, 64:256] for t in sum_m]
    for m in range(2):
        packed[192 * m : 192 * (m + 1), :] = gm[m][:, 0:128]
    packed[384:576, :] = jnp.concatenate([gm[0][:, 128:192], gm[1][:, 128:192]], 1)
    pieces = [gf[16 * a : 16 * a + 12, :] for a in range(3)]
    last = jnp.where(lanes_of(gl.shape) < 64, gl, pltpu.roll(gl, 46, 0))
    pieces += [last[16 * s + 4 * b : 16 * s + 4 * b + 2] for s in range(3) for b in range(3)]
    pieces.append(jnp.zeros((packed.shape[0] - 576 - 54, 128), F32))
    packed[576:, :] = jnp.concatenate(pieces, 0)
    part = packed.shape[0] // nlat
    me = lax.axis_index("lat")
    for k, ref in enumerate((mine, *sends)):
        value = packed[pl.ds(pl.multiple_of((me ^ k) * part, 8), part), :]
        ref[...] = value if k == 0 else encode(value)


def tree_sum(values):
    while len(values) > 1:
        values = [sum(values[i : i + 2][1:], values[i]) for i in range(0, len(values), 2)]
    return values[0]


def sum_kernel(*refs):
    parts, out = refs[:-1], refs[-1]
    out[...] = encode(tree_sum([ref[...] if ref.dtype == F32 else decode(ref) for ref in parts]))


def finish_kernel(*refs):
    nlat = lax.axis_size("lat")
    parts, (first, middle, last, packed) = refs[:nlat], refs[nlat:]
    part = parts[0].shape[0] - GROUP
    me = lax.axis_index("lat")
    for k, ref in enumerate(parts):
        packed[pl.ds(pl.multiple_of((me ^ k) * part, 8), part), :] = decode(ref)
    for m in range(2):
        for b in range(3):
            two = packed[192 * m + 64 * b : 192 * m + 64 * (b + 1), :]
            third = packed[384 + 64 * b : 384 + 64 * (b + 1), :]
            middle[m, b] = two[:, 0:64]
            middle[m, 3 + b] = two[:, 64:128]
            middle[m, 6 + b] = third[:, 64 * m : 64 * (m + 1)]
    rows = packed[576:640, :]
    for m in range(2):
        for k in range(9):
            for c in range(3):
                first[k, c, m : m + 1] = rows[4 * k + c : 4 * k + c + 1, 64 * m : 64 * (m + 1)]
            at = 36 + 2 * (3 * (2 - k // 3) + k % 3)
            last[m, k] = rows[at : at + 2, 64 * m : 64 * (m + 1)]


def ocean_kernel(
    total_rows, members,
    velo, temp, land, mine, other, got_lon, other_lon, got_lat, other_lat,
    velo_next, temp_next,
):
    levels, rows, cols = temp.shape

    def whole(ref, at, size):
        value = ref[...].astype(F32)
        return value[at : at + size] + value[at + size : at + 2 * size]

    ahead = heads_up("lon")
    near, far = (whole(ref, ref.shape[0] - 2 * rows, rows) for ref in (got_lon, other_lon))
    ceast, cwest = jnp.where(ahead, near, far), jnp.where(ahead, far, near)
    ahead = heads_up("lat")
    lines = 3 * levels * (cols // 128)
    near, far = (whole(ref, ref.shape[0] - 2 * lines, lines) for ref in (got_lat, other_lat))
    near, far = (
        jnp.concatenate([x[3 * levels * j : 3 * levels * (j + 1)] for j in range(cols // 128)], 1) for x in (near, far)
    )
    rnorth, rsouth = jnp.where(ahead, near, far), jnp.where(ahead, far, near)
    height, width = rows // COARSE, cols // COARSE
    row = subs_of((rows, cols))
    lane = lanes_of((rows, cols))
    ids = (lax.axis_index("lat") * rows + subs_of((rows, 128))).astype(F32)
    coriolis = jnp.sin(F32(-math.pi / 2) + F32(math.pi) * (ids + 0.5) / F32(total_rows))
    coriolis = jnp.concatenate([coriolis] * (cols // 128), 1)
    wet = land[...].astype(F32) * 0.1
    up = [
        jnp.where(lanes_of((rows, 2 * height)) == subs_of((rows, 2 * height)) // COARSE * 2 + o, F32(1.0), F32(0.0)).astype(BF16)
        for o in range(2)
    ]
    tall = [[dot(u, ref[...]).astype(BF16) for ref in (mine, other)] for u in up]
    spread_k = subs_of((256, cols))
    spread_i = lanes_of((256, cols)) // COARSE

    def neighbours(q, n):
        east = jnp.where(lane == cols - 1, ceast[:, n : n + 1], pltpu.roll(q, cols - 1, 1))
        west = jnp.where(lane == 0, cwest[:, n : n + 1], pltpu.roll(q, 1, 1))
        north = jnp.where(row == rows - 1, rnorth[n : n + 1], pltpu.roll(q, rows - 1, 0))
        south = jnp.where(row == 0, rsouth[n : n + 1], pltpu.roll(q, 1, 0))
        return east, west, north, south

    cum_x = cum_y = None
    for l in range(levels):
        u, v, t = velo[0, l], velo[1, l], temp[l]
        ue, uw, un, us = neighbours(u, l)
        ve, vw, vn, vs = neighbours(v, levels + l)
        te, tw, tn, ts = neighbours(t, 2 * levels + l)
        dx, dy = te - tw, tn - ts
        cum_x = dx if cum_x is None else cum_x + dx
        cum_y = dy if cum_y is None else cum_y + dy
        spread = jnp.where(spread_k == spread_i + (32 * l + SIDE), F32(1.0), F32(0.0)).astype(BF16)
        f = []
        for o in range(2):
            total = None
            for part in tall[o]:
                term = dot(part[:, 128 * l : 128 * (l + 2)], spread)
                total = term if total is None else total + term
            f.append(total * (1.0 / members))
        lap_u = ue + uw + un + us - 4.0 * u
        lap_v = ve + vw + vn + vs - 4.0 * v
        lap_t = te + tw + tn + ts - 4.0 * t
        velo_next[0, l] = u + wet * (coriolis * v + 0.25 * cum_x + 0.5 * lap_u + f[0])
        velo_next[1, l] = v + wet * (0.25 * cum_y - coriolis * u + 0.5 * lap_v + f[1])
        temp_next[l] = t + wet * (0.3 * lap_t - 0.5 * (u * dx + v * dy))


def weights_kernel(first, middle, last, wf, wm, wb, wl, wlt):
    hid = middle.shape[-1]

    def slide(pieces, copies):
        zero = jnp.zeros_like(pieces[0])
        return [jnp.concatenate([zero] * r + pieces + [zero] * (copies - 1 - r), 1) for r in range(copies)]

    for m in range(2):
        for b in range(3):
            taps = [middle[m, 3 * a + b] for a in range(3)]
            turned = jnp.concatenate([t.astype(F32) for t in taps[::-1]], 0).T.astype(BF16)
            turned = [turned[:, hid * s : hid * (s + 1)] for s in range(3)]
            for ref, pieces in ((wm, taps), (wb, turned)):
                for r, block in enumerate(slide(pieces, 2)):
                    at = hid * (3 * r + b)
                    ref[m, at : at + hid, :] = block
    zero = jnp.zeros((1, 2 * hid), F32)
    rows = []
    for a in range(3):
        for b in range(4):
            for c in range(4):
                if b < 3 and c < 3:
                    w = first[3 * a + b, c].astype(F32)
                    rows.append(jnp.concatenate([w[0:1], w[1:2]], 1))
                else:
                    rows.append(zero)
    turned = jnp.concatenate(rows + [zero] * (2 * hid - 48), 0).T
    for r in range(H1_ROWS):
        wf[2 * hid * r : 2 * hid * (r + 1), :] = pltpu.roll(turned, 16 * r, 1).astype(BF16)[:, : wf.shape[1]]
    zero = jnp.zeros((2, hid), F32)
    block = []
    for k in range(9):
        w = [last[m, k].astype(F32) for m in range(2)]
        tops = [jnp.concatenate([w[0], zero], 1), jnp.concatenate([zero, w[1]], 1)]
        block.append(jnp.concatenate(tops + [jnp.zeros((4, 2 * hid), F32)], 0))
    for r, rows in enumerate(slide([jnp.concatenate(block, 0)], 2)):
        wl[72 * r : 72 * (r + 1), :] = rows.astype(BF16)
    rows = [block[3 * (2 - s) + b][0:4] if b < 3 else jnp.zeros((4, 2 * hid), F32) for s in range(3) for b in range(4)]
    wlt[...] = jnp.concatenate(rows, 0).T.astype(BF16)


def pairs_of(lat=None, lon=None):
    sizes = [lax.axis_size(name) for name in ("lat", "lon", "mem")]
    pairs = []
    for index in itertools.product(*(range(n) for n in sizes)):
        place = list(index)
        if lat is not None:
            place[0] += 1 if (index[0] + lat[index[2]]) % 2 == 0 else -1
        if lon is not None:
            place[1] += 1 if (index[1] + lon[index[2]]) % 2 == 0 else -1
            place[1] %= sizes[1]
        if 0 <= place[0] < sizes[0]:
            pairs.append(tuple((i[0] * sizes[1] + i[1]) * sizes[2] + i[2] for i in (index, place)))
    return pairs


def swap(value, pairs):
    got = lax.ppermute(value, ("lat", "lon", "mem"), pairs)
    return got, swap_cores(got)


def swap_cores(value):
    return lax.ppermute(value, "mem", [(i, i ^ 1) for i in range(lax.axis_size("mem"))])


def partner(value, axis, k):
    return lax.ppermute(value, axis, [(i, i ^ k) for i in range(lax.axis_size(axis))])


def per_device(velo, temp, land, target, w_first, w_middle, w_last):
    levels, rows, cols = temp.shape
    height, width = rows // COARSE, cols // COARSE
    wide = levels * (width + 2 * SIDE)
    vregs = wide // 128
    members = w_first.shape[0] * lax.axis_size("mem")
    nlat, nlon = lax.axis_size("lat"), lax.axis_size("lon")
    total_coarse = height * nlat
    count = 2.0 * levels * total_coarse * width * nlon
    params = pltpu.CompilerParams(vmem_limit_bytes=VMEM_LIMIT)
    vm = pltpu.VMEM

    def f32(*shape):
        return jax.ShapeDtypeStruct(shape, F32)

    def bf16(*shape):
        return jax.ShapeDtypeStruct(shape, BF16)

    hid = w_middle.shape[-1]
    hbm = pl.BlockSpec(memory_space=pltpu.HBM)
    deep, tall = 8 * HALO, 8 * height
    core = (0, 1)
    own, to_lon, edges = pl.pallas_call(
        coarse_kernel,
        in_specs=[hbm, hbm, hbm],
        out_shape=(
            vm((vregs, tall, 128), F32),
            vm((tall + 2 * rows, 128), BF16),
            vm((3 * levels * (cols // 128), 128), F32),
        ),
        scratch_shapes=[
            vm(velo.shape, F32),
            vm(temp.shape, F32),
            vm(target.shape, BF16),
            vm((cols // 128, levels * rows, 128), F32),
            pltpu.SemaphoreType.DMA((4,)),
        ],
        compiler_params=pltpu.CompilerParams(vmem_limit_bytes=COARSE_LIMIT),
        name="coarse",
    )(velo, temp, target)
    got_lon, other_lon = swap(to_lon, pairs_of(lon=core))
    full, to_lat = pl.pallas_call(
        merge_kernel,
        out_shape=(f32(vregs, tall, 128), bf16(-(-deep * vregs // 16) * 16 + 2 * edges.shape[0], 128)),
        compiler_params=params,
        name="merge",
    )(own, got_lon, other_lon, edges)
    got_lat, other_lat = swap(to_lat, pairs_of(lat=core))

    weights = pl.pallas_call(
        weights_kernel,
        out_shape=(
            bf16(H1_ROWS * 2 * hid, 16 * (H1_ROWS + 2)),
            bf16(2, 6 * hid, 4 * hid),
            bf16(2, 6 * hid, 4 * hid),
            bf16(144, 4 * hid),
            bf16(2 * hid, 48),
        ),
        cost_estimate=pl.CostEstimate(flops=10**7, bytes_accessed=4 * 10**6, transcendentals=0),
        compiler_params=params,
        name="weights",
    )(jnp.transpose(w_first, (1, 3, 0, 2)), w_middle, w_last)
    total = -(-630 // (GROUP * nlat)) * GROUP * nlat
    part = total // nlat
    force, *sends, mine = pl.pallas_call(
        functools.partial(closure_kernel, 2.0 / count, total_coarse),
        out_shape=(
            bf16(2 * height, wide),
            *[jax.ShapeDtypeStruct((part + GROUP, 128), jnp.int16)] * (nlat - 1),
            f32(part, 128),
        ),
        scratch_shapes=[
            vm((8 * (height + 2 * HALO), wide), F32),
            vm((16 * (height + 2 * HALO), wide), BF16),
            vm((2, 64 * (height + 8), wide), BF16),
            vm((128 * (height + 6), wide), BF16),
            vm((72 * (height + 6), wide), F32),
            vm((16 * (height + 4), wide), BF16),
            vm((2, 64 * (height + 2), wide), BF16),
            vm((2 * height, wide), F32),
            vm((total, 128), F32),
        ],
        compiler_params=params,
        name="closure",
    )(full, got_lat, other_lat, *weights)

    parts = [partner(value, "lat", k + 1) for k, value in enumerate(sends)]
    other = swap_cores(force)
    velo_next, temp_next = pl.pallas_call(
        functools.partial(ocean_kernel, rows * nlat, members),
        out_shape=(jax.ShapeDtypeStruct(velo.shape, F32), jax.ShapeDtypeStruct(temp.shape, F32)),
        cost_estimate=pl.CostEstimate(flops=10**8, bytes_accessed=4 * 10**6, transcendentals=0),
        compiler_params=params,
        name="ocean",
    )(velo, temp, land, force, other, got_lon, other_lon, got_lat, other_lat)

    def add_up(values, name):
        return pl.pallas_call(
            sum_kernel,
            out_shape=jax.ShapeDtypeStruct((part + GROUP, 128), jnp.int16),
            compiler_params=params,
            name=name,
        )(*values)

    summed = add_up([mine, *parts], "sum_lat")
    summed = add_up([summed] + [partner(summed, "lon", k) for k in range(1, nlon)], "sum_lon")
    parts = [summed] + [partner(summed, "lat", k) for k in range(1, nlat)]
    members_here, taps, _, inputs = w_first.shape
    first, middle, last = pl.pallas_call(
        finish_kernel,
        out_shape=(f32(taps, inputs, members_here, hid), f32(*w_middle.shape), f32(*w_last.shape)),
        scratch_shapes=[vm((total, 128), F32)],
        compiler_params=params,
        name="finish",
    )(*parts)
    return (velo_next, temp_next, jnp.transpose(first, (2, 0, 3, 1)), middle, last)


def solution(mesh):
    return jax.shard_map(
        per_device,
        mesh=mesh,
        in_specs=(
            P(None, None, "lat", "lon"),
            P(None, "lat", "lon"),
            P("lat", "lon"),
            P(None, None, "lat", "lon"),
            P("mem", None, None, None),
            P("mem", None, None, None),
            P("mem", None, None, None),
        ),
        out_specs=(
            P(None, None, "lat", "lon"),
            P(None, "lat", "lon"),
            P("mem", None, None, None),
            P("mem", None, None, None),
            P("mem", None, None, None),
        ),
        check_vma=False,
    )
```

```python
import functools
import itertools
import math

import jax
import jax.numpy as jnp
from jax import lax
from jax.experimental import pallas as pl
from jax.experimental.pallas import tpu as pltpu
from jax.sharding import PartitionSpec as P

COARSE = 4
HALO = 5
GROUP = 16
LEVELS = 32000.0
H1_ROWS = 4
SIDE = 16
F32 = jnp.float32
BF16 = jnp.bfloat16
HIGH = lax.Precision.HIGHEST
VMEM_LIMIT = 32 * 1024 * 1024
COARSE_LIMIT = 64 * 1024 * 1024 - 512 * 1024


def dot(a, b, **kw):
    return jnp.dot(a, b, preferred_element_type=F32, **kw)


def dot_nt(a, b):
    return lax.dot_general(a, b, (((1,), (1,)), ((), ())), preferred_element_type=F32)


def lanes_of(shape):
    return lax.broadcasted_iota(jnp.int32, shape, len(shape) - 1)


def subs_of(shape):
    return lax.broadcasted_iota(jnp.int32, shape, len(shape) - 2)


def heads_up(axis):
    return (lax.axis_index(axis) + lax.axis_index("mem")) % 2 == 0


def north_and_south(got, other):
    ahead, place = heads_up("lat"), lax.axis_index("lat")
    north, south = jnp.where(ahead, got, other), jnp.where(ahead, other, got)
    return jnp.where(place < lax.axis_size("lat") - 1, north, 0.0), jnp.where(place > 0, south, 0.0)


def halves(x):
    high = x.astype(BF16).astype(F32)
    return [high, x - high]


def encode(x):
    coded, exponents = [], []
    for at in range(0, x.shape[0], GROUP):
        part = x[at : at + GROUP]
        most = jnp.max(jnp.abs(part), axis=0, keepdims=True)
        exponent = jnp.ceil(jnp.log2(jnp.maximum(most, 1e-30)))
        coded.append(jnp.round(part * (jnp.exp2(-exponent) * LEVELS)))
        exponents.append(exponent)
    exponents.append(jnp.zeros((GROUP - len(exponents), x.shape[1]), F32))
    return jnp.concatenate(coded + exponents, 0).astype(jnp.int32).astype(jnp.int16)


def decode(ref):
    value = ref[...].astype(jnp.int32).astype(F32)
    rows = value.shape[0] - GROUP
    scale = jnp.exp2(value[rows:]) * (1.0 / LEVELS)
    pieces = [value[at : at + GROUP] * scale[i : i + 1] for i, at in enumerate(range(0, rows, GROUP))]
    return jnp.concatenate(pieces, 0)


def coarse_kernel(
    velo_hbm, temp_hbm, target_hbm, own, to_lon, edges, velo, temp, target, fine, sems
):
    copies = [
        pltpu.make_async_copy(velo_hbm.at[0], velo.at[0], sems.at[0]),
        pltpu.make_async_copy(velo_hbm.at[1], velo.at[1], sems.at[1]),
        pltpu.make_async_copy(temp_hbm, temp, sems.at[2]),
        pltpu.make_async_copy(target_hbm, target, sems.at[3]),
    ]
    for copy in copies:
        copy.start()
    levels, rows, cols = temp.shape
    height, width = rows // COARSE, cols // COARSE
    vregs = levels + 1
    pool_r = subs_of((cols, width)) // COARSE
    pool = jnp.where(pool_r == lanes_of((cols, width)), F32(1.0 / COARSE**2), F32(0.0))

    def field(f):
        return temp if f == 2 else velo.at[f]

    means = []
    for f in range(3):
        copies[f].wait()
        ref = field(f)
        pieces = []
        for j in range(cols // 128):
            fine[j] = ref[:, :, 128 * j : 128 * (j + 1)].reshape(levels * rows, 128)
            part = None
            for s in range(COARSE):
                piece = fine[j, pl.ds(s, levels * height, stride=COARSE), :]
                part = piece if part is None else part + piece
            pieces.append(part)
        means.append(jnp.concatenate(pieces, 1))
    mean = dot(jnp.concatenate(means, 0), pool, precision=HIGH)
    mean = mean.astype(BF16).astype(F32)

    copies[3].wait()
    lane = lanes_of((height, 128))

    def place(tiles):
        pieces = []
        for j in range(vregs):
            value = jnp.zeros((height, 128), F32)
            if j < levels:
                moved = pltpu.roll(tiles[j], 32 * j + SIDE, 1)
                value = jnp.where(lane >= 32 * j + SIDE, moved, value)
            if j > 0:
                moved = pltpu.roll(tiles[j - 1], 32 * (j - 1) + SIDE, 1)
                value = jnp.where(lane < 32 * (j - 1) + SIDE, moved, value)
            pieces.append(value)
        return pieces

    for ch in range(8):
        if ch < 4:
            tiles = [target[ch % 2, l].astype(F32) for l in range(levels)]
        elif ch < 7:
            base = (ch - 4) * levels * height
            tiles = [mean[base + l * height : base + (l + 1) * height] for l in range(levels)]
        if ch < 7:
            pieces = place(tiles)
        else:
            pieces = [jnp.zeros((height, 128), F32)] * vregs
        for j in range(vregs):
            own[j, pl.ds(ch, height, stride=8), :] = pieces[j]
    lane = lanes_of((8 * height, 128))
    to_west = jnp.zeros((8 * height, 128), F32)
    to_east = jnp.zeros((8 * height, 128), F32)
    for l in range(levels):
        here = (lane >= 32 * l) & (lane < 32 * (l + 1))
        to_west = jnp.where(here, own[l], to_west)
        to_east = jnp.where(here, own[l + 1], to_east)
    lane = lanes_of((rows, 128))
    first = jnp.zeros((rows, 128), F32)
    last = jnp.zeros((rows, 128), F32)
    for f in range(3):
        ref = field(f)
        for l in range(levels):
            n = f * levels + l
            first = jnp.where(lane == n, pltpu.roll(ref[l, :, 0:128], n, 1), first)
            last = jnp.where(lane == n, pltpu.roll(ref[l, :, cols - 128 :], n + 1, 1), last)
    tall = 8 * height
    east = heads_up("lon")
    cells = jnp.where(east, to_east, to_west)
    to_lon[...] = jnp.concatenate([cells] + halves(jnp.where(east, last, first)), 0).astype(BF16)
    for i, row in enumerate((rows - 1, 0)):
        line = [field(f)[:, row, 128 * j : 128 * (j + 1)] for j in range(cols // 128) for f in range(3)]
        edges[i] = jnp.concatenate(line, 0)


def merge_kernel(own, got, other, edges, full, message):
    vregs, tall = own.shape[:2]
    levels, deep = vregs - 1, 8 * HALO
    ahead = heads_up("lon")
    near, far = (ref[...].astype(F32)[0:tall] for ref in (got, other))
    right, left = jnp.where(ahead, near, far), jnp.where(ahead, far, near)
    lane = lanes_of((tall, 128))
    upper, lower = [], []
    for j in range(vregs):
        value = own[j]
        if j < levels:
            at = 32 * j + SIDE
            value = jnp.where((lane >= at - HALO) & (lane < at), left, value)
        if j > 0:
            at = 32 * (j - 1) + SIDE
            value = jnp.where((lane >= at) & (lane < at + HALO), right, value)
        full[j] = value
        upper.append(value[tall - deep :])
        lower.append(value[:deep])
    pad = [jnp.zeros((-deep * vregs % 16, 128), F32)]
    upper, lower = (jnp.concatenate(x + pad + halves(edges[i]), 0) for i, x in enumerate((upper, lower)))
    message[...] = jnp.where(heads_up("lat"), upper, lower).astype(BF16)


def add(sums, name, term):
    sums[name] = sums[name] + term if name in sums else term


def window(ref, row, rows, step):
    return ref[step * row : step * (row + rows), :]


def quad(get, row, left):
    return get(row) if left <= 2 else jnp.concatenate([get(row), get(row + 2)], 1)


def taps(ref, m, row):
    return jnp.concatenate([ref[b, m, 64 * row : 64 * (row + 4), :] for b in range(3)], 0)


def inner_lanes(wide):
    within = lanes_of((1, wide)) % (128 + 2 * SIDE)
    return jnp.where((within >= SIDE) & (within < SIDE + 128), F32(1.0), F32(0.0))


def closure_kernel(
    scale, total_rows,
    full, got, other, wf, wm, wl, wlt,
    force, *rest,
):
    nlat = lax.axis_size("lat")
    sends, (mine, xb, inner, d2, xf, h1, h2, yl, gb, pf, packed) = rest[: nlat - 1], rest[nlat - 1 :]
    vregs = full.shape[0]
    height = full.shape[1] // 8
    wide = 128 * vregs
    span = height + 2 * HALO
    first_row = lax.axis_index("lat") * height

    def inside(row):
        at = first_row + row
        return jnp.where((at >= 0) & (at < total_rows), F32(1.0), F32(0.0))

    deep = 8 * HALO
    got, other = got[...].astype(F32), other[...].astype(F32)
    for j in range(vregs):
        above, below = north_and_south(got[deep * j : deep * (j + 1)], other[deep * j : deep * (j + 1)])
        xf[:, 128 * j : 128 * (j + 1)] = jnp.concatenate([below, full[j], above], 0)

    sub = subs_of((8, wide))
    tile_b = inner_lanes(wide).astype(BF16)

    for r in range(span):
        x = window(xf, r, 1, 8)
        one = jnp.where(sub < 4, pltpu.roll(pltpu.roll(x, 1, 1), 4, 0), x)
        two = pltpu.roll(pltpu.roll(x, wide - 1, 1), 4, 0)
        xb[16 * r : 16 * (r + 1), :] = jnp.concatenate([one, two], 0).astype(BF16)

    def shifts(x, m, at, ref):
        for b in range(3):
            moved = x if b == 1 else pltpu.roll(x, (1 - b) % wide, 1)
            ref[b, m, 64 * at : 64 * (at + 1), :] = moved

    step = wf.shape[0] // 128

    def make_h1(q):
        pre = dot(wf[...], window(xb, q, step + 2, 16))
        for i in range(step):
            h = (jnp.tanh(pre[128 * i : 128 * (i + 1)]) * inside(q + i - 4)).astype(BF16)
            for m in range(2):
                part = h[64 * m : 64 * (m + 1)]
                shifts(part, m, q + i, h1)
                if 4 <= q + i < height + 4:
                    inner[m, 64 * (q + i - 4) : 64 * (q + i - 3), :] = part

    rows = height + 6

    def make_h2(p):
        for m in range(2):
            y = dot(wm[m], quad(lambda r: taps(h1, m, r), p, rows - p))
            for i in range(min(4, rows - p)):
                pre = y[64 * (i % 2) : 64 * (i % 2 + 1), wide * (i // 2) : wide * (i // 2 + 1)]
                h = jnp.tanh(pre) * inside(p + i - 3)
                at = 128 * (p + i) + 64 * m
                h2[at : at + 64, :] = h.astype(BF16)
        for i in range(p, min(p + 4, rows), 2):
            yl[72 * i : 72 * (i + 2), :] = dot(wl[...], window(h2, i, 2, 128))

    def make_g3(s):
        z = sum(yl[72 * (s + a) + 24 * a : 72 * (s + a) + 24 * (a + 1), :] for a in range(3))
        pred = pltpu.roll(z[0:8], 1, 1) + z[8:16] + pltpu.roll(z[16:24], wide - 1, 1)
        goal = window(xf, s + 3, 1, 8)
        g = ((pred - goal) * scale * inside(s - 2)).astype(BF16).astype(F32)
        one = jnp.where(sub < 4, pltpu.roll(g, wide - 1, 1), pltpu.roll(g, 4, 0))
        two = pltpu.roll(g, 1, 1)
        gb[16 * s : 16 * (s + 1), :] = jnp.concatenate([one, two], 0).astype(BF16)
        if 2 <= s < height + 2:
            both = pred + pltpu.roll(pred, 6, 0)
            pf[2 * (s - 2) : 2 * (s - 1), :] = both[0:2]

    def make_d2(u):
        hidden = window(h2, u + 2, 1, 128).astype(F32)
        d = dot(wlt[...], window(gb, u, 3, 16)) * (1.0 - hidden * hidden) * inside(u - 1)
        for m in range(2):
            shifts(d[64 * m : 64 * (m + 1)].astype(BF16), m, u, d2)

    sums = {}

    def make_grads(j):
        left = height - j
        g = quad(lambda r: window(gb, r + 1, 4, 16) * tile_b, j, left)
        add(sums, "l", dot_nt(g, quad(lambda r: window(h2, r + 3, 2, 128), j, left)))
        for m in range(2):

            def moved(r):
                return jnp.concatenate([d2[b, m, 64 * (r + 1) : 64 * (r + 3), :] for b in (2, 1, 0)], 0)

            rhs = quad(lambda r: h1[1, m, 64 * (r + 3) : 64 * (r + 7), :] * tile_b, j, left)
            add(sums, m, dot_nt(quad(moved, j, left), rhs))

    done = dict.fromkeys(("h1", "h2", "g3", "d2", "d1"), 0)
    while done["d1"] < height:
        if done["d1"] + 6 <= done["d2"]:
            make_grads(done["d1"])
            done["d1"] += 4
        elif done["d2"] < height + 2 and done["d2"] + 3 <= done["g3"]:
            make_d2(done["d2"])
            done["d2"] += 1
        elif done["g3"] < height + 4 and done["g3"] + 3 <= done["h2"]:
            make_g3(done["g3"])
            done["g3"] += 1
        elif done["h2"] < rows and min(done["h2"] + 6, height + 8) <= done["h1"]:
            make_h2(done["h2"])
            done["h2"] = min(done["h2"] + 4, rows)
        else:
            make_h1(done["h1"])
            done["h1"] += step
    force[...] = pf[...].astype(BF16)
    gl = sums["l"][0:48, 0:128] + sums["l"][16:64, 128:256]
    gm = []
    for m in range(2):
        parts = [sums[m][64 * i : 64 * (i + 1)] for i in range(6)]
        gm.append(jnp.concatenate([parts[2 * b][:, 0:192] + parts[2 * b + 1][:, 64:256] for b in range(3)], 0))
    for m in range(2):
        packed[192 * m : 192 * (m + 1), :] = gm[m][:, 0:128]
    packed[384:576, :] = jnp.concatenate([gm[0][:, 128:192], gm[1][:, 128:192]], 1)
    last = jnp.where(lanes_of(gl.shape) < 64, gl, pltpu.roll(gl, 46, 0))
    pieces = [last[16 * s + 4 * b : 16 * s + 4 * b + 2] for s in range(3) for b in range(3)]
    pieces.append(jnp.zeros((packed.shape[0] - 576 - 18, 128), F32))
    packed[576:, :] = jnp.concatenate(pieces, 0)
    part = packed.shape[0] // nlat
    me = lax.axis_index("lat")
    for k, ref in enumerate((mine, *sends)):
        value = packed[pl.ds(pl.multiple_of((me ^ k) * part, 8), part), :]
        ref[...] = value if k == 0 else encode(value)


def first_grad_kernel(xb, inner, d2, wb, out):
    wide = xb.shape[1]
    height = xb.shape[0] // 16 - 2 * HALO
    mask = inner_lanes(wide)
    sums = {}
    for j in range(0, height, 4):
        left = height - j
        d1 = [[None, None] for _ in range(4)]
        for m in range(2):
            y = dot(wb[m], quad(lambda r: taps(d2, m, r), j, left))
            for i in range(4):
                hidden = inner[m, 64 * (j + i) : 64 * (j + i + 1), :].astype(F32)
                pre = y[64 * (i % 2) : 64 * (i % 2 + 1), wide * (i // 2) : wide * (i // 2 + 1)]
                d1[i][m] = (pre * (1.0 - hidden * hidden) * mask).astype(BF16)
        x = quad(lambda r: window(xb, r + 4, 4, 16), j, left)
        add(sums, "f", dot_nt(x, quad(lambda r: jnp.concatenate(d1[r - j] + d1[r - j + 1], 0), j, left)))
    out[...] = sums["f"][0:48, 0:128] + sums["f"][16:64, 128:256]


def tree_sum(values):
    while len(values) > 1:
        values = [sum(values[i : i + 2][1:], values[i]) for i in range(0, len(values), 2)]
    return values[0]


def sum_lat_kernel(mine, first, *refs):
    parts, out = refs[:-1], refs[-1]
    total = tree_sum([mine[...]] + [decode(ref) for ref in parts])
    out[...] = encode(jnp.concatenate([total, first[...]], 0))


def sum_lon_kernel(*refs):
    parts, out = refs[:-1], refs[-1]
    out[...] = encode(tree_sum([decode(ref) for ref in parts]))


def finish_kernel(*refs):
    nlat = lax.axis_size("lat")
    parts, (first, middle, last, packed) = refs[:nlat], refs[nlat:]
    part = packed.shape[0] // nlat
    me = lax.axis_index("lat")
    values = [decode(ref) for ref in parts]
    for k, value in enumerate(values):
        packed[pl.ds(pl.multiple_of((me ^ k) * part, 8), part), :] = value[:part]
    inputs = tree_sum([value[part:] for value in values])
    for m in range(2):
        for b in range(3):
            two = packed[192 * m + 64 * b : 192 * m + 64 * (b + 1), :]
            third = packed[384 + 64 * b : 384 + 64 * (b + 1), :]
            middle[m, b] = two[:, 0:64]
            middle[m, 3 + b] = two[:, 64:128]
            middle[m, 6 + b] = third[:, 64 * m : 64 * (m + 1)]
    rows = packed[576:608, :]
    for m in range(2):
        for k in range(9):
            for c in range(3):
                at = 16 * (k // 3) + 4 * (k % 3) + c
                first[k, c, m : m + 1] = inputs[at : at + 1, 64 * m : 64 * (m + 1)]
            at = 2 * (3 * (2 - k // 3) + k % 3)
            last[m, k] = rows[at : at + 2, 64 * m : 64 * (m + 1)]


def ocean_kernel(
    total_rows, members,
    velo, temp, land, mine, other, got_lon, other_lon, got_lat, other_lat,
    velo_next, temp_next,
):
    levels, rows, cols = temp.shape

    def whole(ref, at, size):
        value = ref[...].astype(F32)
        return value[at : at + size] + value[at + size : at + 2 * size]

    ahead = heads_up("lon")
    near, far = (whole(ref, ref.shape[0] - 2 * rows, rows) for ref in (got_lon, other_lon))
    ceast, cwest = jnp.where(ahead, near, far), jnp.where(ahead, far, near)
    lines = 3 * levels * (cols // 128)
    near, far = (whole(ref, ref.shape[0] - 2 * lines, lines) for ref in (got_lat, other_lat))
    near, far = (
        jnp.concatenate([x[3 * levels * j : 3 * levels * (j + 1)] for j in range(cols // 128)], 1) for x in (near, far)
    )
    rnorth, rsouth = north_and_south(near, far)
    height, width = rows // COARSE, cols // COARSE
    row = subs_of((rows, cols))
    lane = lanes_of((rows, cols))
    ids = (lax.axis_index("lat") * rows + subs_of((rows, 128))).astype(F32)
    coriolis = jnp.sin(F32(-math.pi / 2) + F32(math.pi) * (ids + 0.5) / F32(total_rows))
    coriolis = jnp.concatenate([coriolis] * (cols // 128), 1)
    wet = land[...].astype(F32) * 0.1
    up = [
        jnp.where(lanes_of((rows, 2 * height)) == subs_of((rows, 2 * height)) // COARSE * 2 + o, F32(1.0), F32(0.0)).astype(BF16)
        for o in range(2)
    ]
    tall = [[dot(u, ref[...]).astype(BF16) for ref in (mine, other)] for u in up]
    spread_k = subs_of((256, cols))
    spread_i = lanes_of((256, cols)) // COARSE

    def neighbours(q, n):
        east = jnp.where(lane == cols - 1, ceast[:, n : n + 1], pltpu.roll(q, cols - 1, 1))
        west = jnp.where(lane == 0, cwest[:, n : n + 1], pltpu.roll(q, 1, 1))
        north = jnp.where(row == rows - 1, rnorth[n : n + 1], pltpu.roll(q, rows - 1, 0))
        south = jnp.where(row == 0, rsouth[n : n + 1], pltpu.roll(q, 1, 0))
        return east, west, north, south

    cum_x = cum_y = None
    for l in range(levels):
        u, v, t = velo[0, l], velo[1, l], temp[l]
        ue, uw, un, us = neighbours(u, l)
        ve, vw, vn, vs = neighbours(v, levels + l)
        te, tw, tn, ts = neighbours(t, 2 * levels + l)
        dx, dy = te - tw, tn - ts
        cum_x = dx if cum_x is None else cum_x + dx
        cum_y = dy if cum_y is None else cum_y + dy
        spread = jnp.where(spread_k == spread_i + (32 * l + SIDE), F32(1.0), F32(0.0)).astype(BF16)
        f = []
        for o in range(2):
            total = None
            for part in tall[o]:
                term = dot(part[:, 128 * l : 128 * (l + 2)], spread)
                total = term if total is None else total + term
            f.append(total * (1.0 / members))
        lap_u = ue + uw + un + us - 4.0 * u
        lap_v = ve + vw + vn + vs - 4.0 * v
        lap_t = te + tw + tn + ts - 4.0 * t
        velo_next[0, l] = u + wet * (coriolis * v + 0.25 * cum_x + 0.5 * lap_u + f[0])
        velo_next[1, l] = v + wet * (0.25 * cum_y - coriolis * u + 0.5 * lap_v + f[1])
        temp_next[l] = t + wet * (0.3 * lap_t - 0.5 * (u * dx + v * dy))


def weights_kernel(first_hbm, middle_hbm, last_hbm, wf, wm, wb, wl, wlt, first, middle, last, sems):
    hid = middle.shape[-1]
    pairs = ((first_hbm, first), (middle_hbm, middle), (last_hbm, last))
    copies = [pltpu.make_async_copy(*pair, sems.at[i]) for i, pair in enumerate(pairs)]
    for copy in copies:
        copy.start()
    for copy in copies:
        copy.wait()

    def slide(pieces, copies):
        zero = jnp.zeros_like(pieces[0])
        return [jnp.concatenate([zero] * r + pieces + [zero] * (copies - 1 - r), 1) for r in range(copies)]

    for m in range(2):
        for b in range(3):
            taps = [middle[m, 3 * a + b] for a in range(3)]
            turned = jnp.concatenate([t.astype(F32) for t in taps[::-1]], 0).T.astype(BF16)
            turned = [turned[:, hid * s : hid * (s + 1)] for s in range(3)]
            for ref, pieces, at in ((wm, taps, b), (wb, turned, 2 - b)):
                for r, block in enumerate(slide(pieces, 2)):
                    ref[m, hid * r : hid * (r + 1), 4 * hid * at : 4 * hid * (at + 1)] = block
    zero = jnp.zeros((1, 2 * hid), F32)
    rows = []
    for a in range(3):
        for b in range(4):
            for c in range(4):
                if b < 3 and c < 3:
                    w = first[3 * a + b, c].astype(F32)
                    rows.append(jnp.concatenate([w[0:1], w[1:2]], 1))
                else:
                    rows.append(zero)
    turned = jnp.concatenate(rows + [zero] * (2 * hid - 48), 0).T
    for r in range(H1_ROWS):
        wf[2 * hid * r : 2 * hid * (r + 1), :] = pltpu.roll(turned, 16 * r, 1).astype(BF16)[:, : wf.shape[1]]
    zero = jnp.zeros((2, hid), F32)
    block = []
    for k in range(9):
        w = [last[m, k].astype(F32) for m in range(2)]
        tops = [jnp.concatenate([w[0], zero], 1), jnp.concatenate([zero, w[1]], 1)]
        block.append(jnp.concatenate(tops + [jnp.zeros((4, 2 * hid), F32)], 0))
    for r, rows in enumerate(slide([jnp.concatenate(block, 0)], 2)):
        wl[72 * r : 72 * (r + 1), :] = rows.astype(BF16)
    rows = [block[3 * (2 - s) + b][0:4] if b < 3 else jnp.zeros((4, 2 * hid), F32) for s in range(3) for b in range(4)]
    wlt[...] = jnp.concatenate(rows, 0).T.astype(BF16)


def pairs_of(lat=None, lon=None):
    sizes = [lax.axis_size(name) for name in ("lat", "lon", "mem")]
    pairs = []
    for index in itertools.product(*(range(n) for n in sizes)):
        place = list(index)
        if lat is not None:
            place[0] += 1 if (index[0] + lat[index[2]]) % 2 == 0 else -1
            place[0] %= sizes[0]
        if lon is not None:
            place[1] += 1 if (index[1] + lon[index[2]]) % 2 == 0 else -1
            place[1] %= sizes[1]
        pairs.append(tuple((i[0] * sizes[1] + i[1]) * sizes[2] + i[2] for i in (index, place)))
    return pairs


def swap_cores(value):
    return lax.ppermute(value, "mem", [(i, i ^ 1) for i in range(lax.axis_size("mem"))])


def partner(value, axis, k):
    return lax.ppermute(value, axis, [(i, i ^ k) for i in range(lax.axis_size(axis))])


def per_device(velo, temp, land, target, w_first, w_middle, w_last):
    levels, rows, cols = temp.shape
    height, width = rows // COARSE, cols // COARSE
    wide = levels * (width + 2 * SIDE)
    vregs = wide // 128
    members = w_first.shape[0] * lax.axis_size("mem")
    nlat, nlon = lax.axis_size("lat"), lax.axis_size("lon")
    total_coarse = height * nlat
    count = 2.0 * levels * total_coarse * width * nlon
    params = pltpu.CompilerParams(vmem_limit_bytes=VMEM_LIMIT)
    vm = pltpu.VMEM

    def f32(*shape):
        return jax.ShapeDtypeStruct(shape, F32)

    def bf16(*shape):
        return jax.ShapeDtypeStruct(shape, BF16)

    hid = w_middle.shape[-1]
    hbm = pl.BlockSpec(memory_space=pltpu.HBM)
    deep, tall = 8 * HALO, 8 * height
    core = (0, 1)
    own, to_lon, edges = pl.pallas_call(
        coarse_kernel,
        in_specs=[hbm, hbm, hbm],
        out_shape=(
            vm((vregs, tall, 128), F32),
            vm((tall + 2 * rows, 128), BF16),
            vm((2, 3 * levels * (cols // 128), 128), F32),
        ),
        scratch_shapes=[
            vm(velo.shape, F32),
            vm(temp.shape, F32),
            vm(target.shape, BF16),
            vm((cols // 128, levels * rows, 128), F32),
            pltpu.SemaphoreType.DMA((4,)),
        ],
        compiler_params=pltpu.CompilerParams(vmem_limit_bytes=COARSE_LIMIT),
        name="coarse",
    )(velo, temp, target)
    everywhere = ("lat", "lon", "mem")
    got_lon = lax.ppermute(to_lon, everywhere, pairs_of(lon=core))
    kept_in_hbm = (pltpu.with_memory_space_constraint(w, pltpu.HBM) for w in (jnp.transpose(w_first, (1, 3, 0, 2)), w_middle, w_last))
    weights = pl.pallas_call(
        weights_kernel,
        in_specs=[hbm, hbm, hbm],
        out_shape=(
            bf16(H1_ROWS * 2 * hid, 16 * (H1_ROWS + 2)),
            bf16(2, 2 * hid, 12 * hid),
            bf16(2, 2 * hid, 12 * hid),
            bf16(144, 4 * hid),
            bf16(2 * hid, 48),
        ),
        scratch_shapes=[
            vm((w_first.shape[1], w_first.shape[3], w_first.shape[0], hid), BF16),
            vm(w_middle.shape, BF16),
            vm(w_last.shape, BF16),
            pltpu.SemaphoreType.DMA((3,)),
        ],
        cost_estimate=pl.CostEstimate(flops=10**8, bytes_accessed=4 * 10**6, transcendentals=0),
        compiler_params=params,
        name="weights",
    )(*kept_in_hbm)
    other_lon = swap_cores(got_lon)
    message = bf16(-(-deep * vregs // 16) * 16 + 2 * edges.shape[1], 128)
    full, to_lat = pl.pallas_call(
        merge_kernel,
        out_shape=(f32(vregs, tall, 128), message),
        compiler_params=params,
        name="merge",
    )(own, got_lon, other_lon, edges)
    got_lat = lax.ppermute(to_lat, everywhere, pairs_of(lat=core))
    got_lat, weights = lax.optimization_barrier((got_lat, weights))
    other_lat = swap_cores(got_lat)

    total = -(-594 // (GROUP * nlat)) * GROUP * nlat
    part = total // nlat
    coded = jax.ShapeDtypeStruct((part + GROUP, 128), jnp.int16)
    wf, wm, wb, wl, wlt = weights
    force, *rest = pl.pallas_call(
        functools.partial(closure_kernel, 2.0 / count, total_coarse),
        out_shape=(
            bf16(2 * height, wide),
            *[coded] * (nlat - 1),
            f32(part, 128),
            vm((16 * (height + 2 * HALO), wide), BF16),
            vm((2, 64 * height, wide), BF16),
            vm((3, 2, 64 * (height + 2), wide), BF16),
        ),
        scratch_shapes=[
            vm((8 * (height + 2 * HALO), wide), F32),
            vm((3, 2, 64 * (height + 8), wide), BF16),
            vm((128 * (height + 6), wide), BF16),
            vm((72 * (height + 6), wide), F32),
            vm((16 * (height + 4), wide), BF16),
            vm((2 * height, wide), F32),
            vm((total, 128), F32),
        ],
        compiler_params=params,
        name="closure",
    )(full, got_lat, other_lat, wf, wm, wl, wlt)
    sends, (mine, *kept) = rest[: nlat - 1], rest[nlat - 1 :]

    other = swap_cores(force)
    parts = [partner(value, "lat", k + 1) for k, value in enumerate(sends)]
    first = pl.pallas_call(
        first_grad_kernel,
        out_shape=f32(48, 128),
        cost_estimate=pl.CostEstimate(flops=2 * 10**9, bytes_accessed=4 * 10**6, transcendentals=0),
        compiler_params=params,
        name="first_grad",
    )(*kept, wb)
    def add_up(kernel, values, name):
        return pl.pallas_call(
            kernel,
            out_shape=jax.ShapeDtypeStruct((part + 48 + GROUP, 128), jnp.int16),
            compiler_params=params,
            name=name,
        )(*values)

    parts, other = lax.optimization_barrier((parts, other))
    summed = add_up(sum_lat_kernel, [mine, first, *parts], "sum_lat")
    velo_next, temp_next = pl.pallas_call(
        functools.partial(ocean_kernel, rows * nlat, members),
        out_shape=(jax.ShapeDtypeStruct(velo.shape, F32), jax.ShapeDtypeStruct(temp.shape, F32)),
        cost_estimate=pl.CostEstimate(flops=10**8, bytes_accessed=4 * 10**6, transcendentals=0),
        compiler_params=params,
        name="ocean",
    )(velo, temp, land, force, other, got_lon, other_lon, got_lat, other_lat)
    parts = [summed] + [partner(summed, "lon", k) for k in range(1, nlon)]
    parts, velo_next, temp_next = lax.optimization_barrier((parts, velo_next, temp_next))
    summed = add_up(sum_lon_kernel, parts, "sum_lon")
    parts = [summed] + [partner(summed, "lat", k) for k in range(1, nlat)]
    members_here, taps, _, inputs = w_first.shape
    first, middle, last = pl.pallas_call(
        finish_kernel,
        out_shape=(f32(taps, inputs, members_here, hid), f32(*w_middle.shape), f32(*w_last.shape)),
        scratch_shapes=[vm((total, 128), F32)],
        compiler_params=params,
        name="finish",
    )(*parts)
    return (velo_next, temp_next, jnp.transpose(first, (2, 0, 3, 1)), middle, last)


def solution(mesh):
    return jax.shard_map(
        per_device,
        mesh=mesh,
        in_specs=(
            P(None, None, "lat", "lon"),
            P(None, "lat", "lon"),
            P("lat", "lon"),
            P(None, None, "lat", "lon"),
            P("mem", None, None, None),
            P("mem", None, None, None),
            P("mem", None, None, None),
        ),
        out_specs=(
            P(None, None, "lat", "lon"),
            P(None, "lat", "lon"),
            P("mem", None, None, None),
            P("mem", None, None, None),
            P("mem", None, None, None),
        ),
        check_vma=False,
    )
```

```python
import functools
import itertools
import math

import jax
import jax.numpy as jnp
from jax import lax
from jax.experimental import pallas as pl
from jax.experimental.pallas import tpu as pltpu
from jax.sharding import PartitionSpec as P

COARSE = 4
HALO = 5
PACKED = 3 * HALO + 4
GROUP = 16
LEVELS = 32000.0
H1_ROWS = 4
SIDE = 16
F32 = jnp.float32
BF16 = jnp.bfloat16
HIGH = lax.Precision.HIGHEST
VMEM_LIMIT = 32 * 1024 * 1024
COARSE_LIMIT = 60 * 1024 * 1024


def dot(a, b, **kw):
    return jnp.dot(a, b, preferred_element_type=F32, **kw)


def dot_nt(a, b):
    return lax.dot_general(a, b, (((1,), (1,)), ((), ())), preferred_element_type=F32)


def lanes_of(shape):
    return lax.broadcasted_iota(jnp.int32, shape, len(shape) - 1)


def subs_of(shape):
    return lax.broadcasted_iota(jnp.int32, shape, len(shape) - 2)


def heads_up(axis):
    return (lax.axis_index(axis) + lax.axis_index("mem")) % 2 == 0


def north_and_south(got, other):
    ahead, place = heads_up("lat"), lax.axis_index("lat")
    north, south = jnp.where(ahead, got, other), jnp.where(ahead, other, got)
    return jnp.where(place < lax.axis_size("lat") - 1, north, 0.0), jnp.where(place > 0, south, 0.0)


def halves(x):
    high = x.astype(BF16).astype(F32)
    return [high, x - high]


def encode(x):
    coded, exponents = [], []
    for at in range(0, x.shape[0], GROUP):
        part = x[at : at + GROUP]
        most = jnp.max(jnp.abs(part), axis=0, keepdims=True)
        exponent = jnp.ceil(jnp.log2(jnp.maximum(most, 1e-30)))
        coded.append(jnp.round(part * (jnp.exp2(-exponent) * LEVELS)))
        exponents.append(exponent)
    exponents.append(jnp.zeros((GROUP - len(exponents), x.shape[1]), F32))
    return jnp.concatenate(coded + exponents, 0).astype(jnp.int32).astype(jnp.int16)


def decode(ref):
    value = ref[...].astype(jnp.int32).astype(F32)
    rows = value.shape[0] - GROUP
    scale = jnp.exp2(value[rows:]) * (1.0 / LEVELS)
    pieces = [value[at : at + GROUP] * scale[i : i + 1] for i, at in enumerate(range(0, rows, GROUP))]
    return jnp.concatenate(pieces, 0)


def coarse_kernel(
    velo_hbm, temp_hbm, target_hbm, *refs
):
    from_hbm, (own, to_lon, edges, *weights), (velo, temp, target, fine, sems) = refs[:3], refs[3:9], refs[9:]
    copies = [
        pltpu.make_async_copy(velo_hbm.at[0], velo.at[0], sems.at[0]),
        pltpu.make_async_copy(velo_hbm.at[1], velo.at[1], sems.at[1]),
        pltpu.make_async_copy(temp_hbm, temp, sems.at[2]),
        pltpu.make_async_copy(target_hbm, target, sems.at[3]),
        *(pltpu.make_async_copy(*pair, sems.at[4 + i]) for i, pair in enumerate(zip(from_hbm, weights))),
    ]
    for copy in copies:
        copy.start()
    levels, rows, cols = temp.shape
    height, width = rows // COARSE, cols // COARSE
    vregs = levels + 1
    pool_r = subs_of((cols, width)) // COARSE
    pool = jnp.where(pool_r == lanes_of((cols, width)), F32(1.0 / COARSE**2), F32(0.0))

    def field(f):
        return temp if f == 2 else velo.at[f]

    means = []
    for f in range(3):
        copies[f].wait()
        ref = field(f)
        pieces = []
        for j in range(cols // 128):
            fine[j] = ref[:, :, 128 * j : 128 * (j + 1)].reshape(levels * rows, 128)
            part = None
            for s in range(COARSE):
                piece = fine[j, pl.ds(s, levels * height, stride=COARSE), :]
                part = piece if part is None else part + piece
            pieces.append(part)
        means.append(jnp.concatenate(pieces, 1))
    mean = dot(jnp.concatenate(means, 0), pool, precision=HIGH)
    mean = mean.astype(BF16).astype(F32)

    copies[3].wait()
    lane = lanes_of((height, 128))

    def place(tiles):
        pieces = []
        for j in range(vregs):
            value = jnp.zeros((height, 128), F32)
            if j < levels:
                moved = pltpu.roll(tiles[j], 32 * j + SIDE, 1)
                value = jnp.where(lane >= 32 * j + SIDE, moved, value)
            if j > 0:
                moved = pltpu.roll(tiles[j - 1], 32 * (j - 1) + SIDE, 1)
                value = jnp.where(lane < 32 * (j - 1) + SIDE, moved, value)
            pieces.append(value)
        return pieces

    for ch in range(8):
        if ch < 4:
            tiles = [target[ch % 2, l].astype(F32) for l in range(levels)]
        elif ch < 7:
            base = (ch - 4) * levels * height
            tiles = [mean[base + l * height : base + (l + 1) * height] for l in range(levels)]
        if ch < 7:
            pieces = place(tiles)
        else:
            pieces = [jnp.zeros((height, 128), F32)] * vregs
        for j in range(vregs):
            own[j, pl.ds(ch, height, stride=8), :] = pieces[j]
    lane = lanes_of((8 * height, 128))
    to_west = jnp.zeros((8 * height, 128), F32)
    to_east = jnp.zeros((8 * height, 128), F32)
    for l in range(levels):
        here = (lane >= 32 * l) & (lane < 32 * (l + 1))
        to_west = jnp.where(here, own[l], to_west)
        to_east = jnp.where(here, own[l + 1], to_east)
    lane = lanes_of((rows, 128))
    first = jnp.zeros((rows, 128), F32)
    last = jnp.zeros((rows, 128), F32)
    for f in range(3):
        ref = field(f)
        for l in range(levels):
            n = f * levels + l
            first = jnp.where(lane == n, pltpu.roll(ref[l, :, 0:128], n, 1), first)
            last = jnp.where(lane == n, pltpu.roll(ref[l, :, cols - 128 :], n + 1, 1), last)
    tall = 8 * height
    east = heads_up("lon")
    cells = jnp.where(east, to_east, to_west)
    to_lon[...] = jnp.concatenate([cells] + halves(jnp.where(east, last, first)), 0).astype(BF16)
    for i, row in enumerate((rows - 1, 0)):
        line = [field(f)[:, row, 128 * j : 128 * (j + 1)] for j in range(cols // 128) for f in range(3)]
        edges[i] = jnp.concatenate(line, 0)
    for copy in copies[4:]:
        copy.wait()


def merge_kernel(own, got, other, edges, full, message):
    vregs, tall = own.shape[:2]
    levels = vregs - 1
    ahead = heads_up("lon")
    near, far = (ref[...].astype(F32)[0:tall] for ref in (got, other))
    right, left = jnp.where(ahead, near, far), jnp.where(ahead, far, near)
    lane = lanes_of((tall, 128))
    upper, lower = [], []
    for j in range(vregs):
        value = own[j]
        if j < levels:
            at = 32 * j + SIDE
            value = jnp.where((lane >= at - HALO) & (lane < at), left, value)
        if j > 0:
            at = 32 * (j - 1) + SIDE
            value = jnp.where((lane >= at) & (lane < at + HALO), right, value)
        full[j] = value
        last = tall // 8
        for pieces, first, goals in ((upper, last - HALO, (last - 2, last - 1)), (lower, 0, (0, 1))):
            pieces += [value[8 * r + 4 : 8 * r + 7] for r in range(first, first + HALO)]
            pieces += [value[8 * r : 8 * r + 2] for r in goals]
    pad = [jnp.zeros((-PACKED * vregs % 16, 128), F32)]
    upper, lower = (jnp.concatenate(x + pad + halves(edges[i]), 0) for i, x in enumerate((upper, lower)))
    message[...] = jnp.where(heads_up("lat"), upper, lower).astype(BF16)


def unpack(message, j, goal_rows):
    at = PACKED * j
    rows = []
    for i in range(HALO):
        goal = jnp.zeros((2, 128), F32)
        if i in goal_rows:
            start = at + 3 * HALO + 2 * goal_rows.index(i)
            goal = message[start : start + 2]
        rows += [goal, goal, message[at + 3 * i : at + 3 * (i + 1)], jnp.zeros((1, 128), F32)]
    return jnp.concatenate(rows, 0)


def add(sums, name, term):
    sums[name] = sums[name] + term if name in sums else term


def window(ref, row, rows, step):
    return ref[step * row : step * (row + rows), :]


def quad(get, row, left):
    return get(row) if left <= 2 else jnp.concatenate([get(row), get(row + 2)], 1)


def taps(ref, m, row):
    return jnp.concatenate([ref[b, m, 64 * row : 64 * (row + 4), :] for b in range(3)], 0)


def columns_around(x):
    wide = x.shape[1]
    return [pltpu.roll(x, 1, 1), x, pltpu.roll(x, wide - 1, 1)]


def spread_columns(x):
    wide = x.shape[1]
    one = jnp.where(subs_of(x.shape) < 4, pltpu.roll(pltpu.roll(x, 1, 1), 4, 0), x)
    two = pltpu.roll(pltpu.roll(x, wide - 1, 1), 4, 0)
    return jnp.concatenate([one, two], 0).astype(BF16)


def inner_kernel(full, wf, wm, h1, h2, xb):
    vregs, height = full.shape[0], full.shape[1] // 8
    wide = 128 * vregs
    for r in range(height):
        x = jnp.concatenate([full[j, 8 * r : 8 * (r + 1), :] for j in range(vregs)], 1)
        xb[16 * r : 16 * (r + 1), :] = spread_columns(x)
    half = (height - 2) // 2
    y = dot(wf[0 : 128 * half, 0 : 16 * (half + 2)], jnp.concatenate([window(xb, r, half + 2, 16) for r in (0, half)], 1))
    for i in range(2 * half):
        t = i // half
        h = jnp.tanh(y[128 * (i - t * half) : 128 * (i - t * half + 1), wide * t : wide * (t + 1)]).astype(BF16)
        for m in range(2):
            for b, moved in enumerate(columns_around(h[64 * m : 64 * (m + 1)])):
                h1[b, m, 64 * i : 64 * (i + 1), :] = moved
    for p in range(0, height - 4, 4):
        for m in range(2):
            y = dot(wm[m], quad(lambda r: taps(h1, m, r), p, 4))
            for i in range(4):
                pre = y[64 * (i % 2) : 64 * (i % 2 + 1), wide * (i // 2) : wide * (i // 2 + 1)]
                at = 128 * (p + i) + 64 * m
                h2[at : at + 64, :] = jnp.tanh(pre).astype(BF16)


def inner_lanes(wide):
    within = lanes_of((1, wide)) % (128 + 2 * SIDE)
    return jnp.where((within >= SIDE) & (within < SIDE + 128), F32(1.0), F32(0.0))


def closure_kernel(
    scale, total_rows,
    full, got, other, h1_inner, h2_inner, wf, wm, wl, wlt,
    force, *rest,
):
    nlat = lax.axis_size("lat")
    sends, (mine, xb, inner, h2, gb, d2, xf, h1, yl, pf, packed) = rest[: nlat - 1], rest[nlat - 1 :]
    vregs = full.shape[0]
    height = full.shape[1] // 8
    wide = 128 * vregs
    span = height + 2 * HALO
    first_row = lax.axis_index("lat") * height

    def inside(row):
        at = first_row + row
        return jnp.where((at >= 0) & (at < total_rows), F32(1.0), F32(0.0))

    north, south = north_and_south(got[...].astype(F32), other[...].astype(F32))
    for j in range(vregs):
        above, below = unpack(north, j, (0, 1)), unpack(south, j, (HALO - 2, HALO - 1))
        xf[:, 128 * j : 128 * (j + 1)] = jnp.concatenate([below, full[j], above], 0)

    sub = subs_of((8, wide))
    tile_b = inner_lanes(wide).astype(BF16)

    for r in range(span):
        xb[16 * r : 16 * (r + 1), :] = spread_columns(window(xf, r, 1, 8))

    known = range(5, height + 3)

    def h1_row(b, m, i):
        ref, at = (h1_inner, i - known[0]) if i in known else (h1, i)
        return ref[b, m, 64 * at : 64 * (at + 1), :]

    def make_h1(starts, count):
        weights = wf[0 : 128 * count, 0 : 16 * (count + 2)]
        y = dot(weights, jnp.concatenate([window(xb, r, count + 2, 16) for r in starts], 1))
        for t, start in enumerate(starts):
            for i in range(count):
                pre = y[128 * i : 128 * (i + 1), wide * t : wide * (t + 1)]
                h = (jnp.tanh(pre) * inside(start + i - 4)).astype(BF16)
                for m in range(2):
                    at = 64 * (start + i)
                    for b, moved in enumerate(columns_around(h[64 * m : 64 * (m + 1)])):
                        h1[b, m, at : at + 64, :] = moved

    def h1_rows(b, m, row):
        return jnp.concatenate([h1_row(b, m, row + i) for i in range(4)], 0)

    rows = height + 6
    h2[128 * 5 : 128 * (height + 1), :] = h2_inner[...]

    def make_h2(starts, count):
        for m in range(2):
            windows = [jnp.concatenate([h1_rows(b, m, r) for b in range(3)], 0) for r in starts]
            y = dot(wm[m, 0 : 64 * count, :], jnp.concatenate(windows, 1))
            for t, start in enumerate(starts):
                for i in range(count):
                    pre = y[64 * i : 64 * (i + 1), wide * t : wide * (t + 1)]
                    h = jnp.tanh(pre) * inside(start + i - 3)
                    at = 128 * (start + i) + 64 * m
                    h2[at : at + 64, :] = h.astype(BF16)

    def make_yl(p):
        y = dot(wl[...], quad(lambda r: window(h2, r, 2, 128), p, rows - p))
        for t in range(y.shape[1] // wide):
            at = 32 * (p + 2 * t)
            yl[at : at + 64, :] = y[:, wide * t : wide * (t + 1)]

    def make_g3(s):
        z = 0.0
        for pair in ((s, s + 2) if s % 2 == 0 else (s - 1, s + 1)):
            at = 32 * pair + 16 * (s + 2 - pair)
            z = z + yl[at : at + 16, :]
        pred = pltpu.roll(z[0:8], 1, 1) + pltpu.roll(z[0:8], 4, 0) + pltpu.roll(z[8:16], wide - 1, 1)
        goal = window(xf, s + 3, 1, 8)
        g = ((pred - goal) * scale * inside(s - 2)).astype(BF16).astype(F32)
        one = jnp.where(sub < 4, pltpu.roll(g, wide - 1, 1), pltpu.roll(g, 4, 0))
        two = pltpu.roll(g, 1, 1)
        gb[16 * s : 16 * (s + 1), :] = jnp.concatenate([one, two], 0).astype(BF16)
        if 2 <= s < height + 2:
            both = pred + pltpu.roll(pred, 6, 0)
            pf[2 * (s - 2) : 2 * (s - 1), :] = both[0:2]

    def make_d2(u):
        y = dot(wlt[...], jnp.concatenate([window(gb, r, 3, 16) for r in (u, u + 1)], 1))
        for t in range(2):
            hidden = window(h2, u + t + 2, 1, 128).astype(F32)
            d = y[:, wide * t : wide * (t + 1)] * (1.0 - hidden * hidden) * inside(u + t - 1)
            for m in range(2):
                for b, moved in enumerate(columns_around(d[64 * m : 64 * (m + 1)].astype(BF16))):
                    d2[b, m, 64 * (u + t) : 64 * (u + t + 1), :] = moved

    sums = {}

    def make_grads(j):
        left = height - j
        for m in range(2):

            def moved(r):
                return jnp.concatenate([d2[b, m, 64 * (r + 1) : 64 * (r + 3), :] for b in (2, 1, 0)], 0)

            rhs = quad(lambda r: h1_rows(1, m, r + 3) * tile_b, j, left)
            add(sums, m, dot_nt(quad(moved, j, left), rhs))

    make_h1((0, height + 4), 4)
    make_h1((4, height + 3), 1)
    make_h2((0, 2), 2)
    make_h2((4, height + 1), 1)
    for p in range(0, height, 4):
        make_yl(p)
    make_h2((height + 2, height + 4), 2)
    for p in range(height, rows, 4):
        make_yl(p)
    for m in range(2):
        for r in range(height):
            inner[m, 64 * r : 64 * (r + 1), :] = h1_row(1, m, r + 4)
    for r in range(height + 4):
        make_g3(r)
    for u in range(0, height + 2, 2):
        make_d2(u)
    for j in range(0, height, 4):
        make_grads(j)
    force[...] = pf[...].astype(BF16)
    gm = []
    for m in range(2):
        parts = [sums[m][64 * i : 64 * (i + 1)] for i in range(6)]
        gm.append(jnp.concatenate([parts[2 * b][:, 0:192] + parts[2 * b + 1][:, 64:256] for b in range(3)], 0))
    for m in range(2):
        packed[192 * m : 192 * (m + 1), :] = gm[m][:, 0:128]
    packed[384:576, :] = jnp.concatenate([gm[0][:, 128:192], gm[1][:, 128:192]], 1)
    if packed.shape[0] > 576:
        packed[576:, :] = jnp.zeros((packed.shape[0] - 576, 128), F32)
    part = packed.shape[0] // nlat
    me = lax.axis_index("lat")
    for k, ref in enumerate((mine, *sends)):
        value = packed[pl.ds(pl.multiple_of((me ^ k) * part, 8), part), :]
        ref[...] = value if k == 0 else encode(value)


def outer_grads_kernel(xb, inner, h2, gb, d2, wb, out):
    wide = xb.shape[1]
    height = xb.shape[0] // 16 - 2 * HALO
    mask = inner_lanes(wide)
    sums = {}
    for j in range(0, height, 4):
        left = height - j
        g = quad(lambda r: window(gb, r + 1, 4, 16) * mask.astype(BF16), j, left)
        add(sums, "l", dot_nt(g, quad(lambda r: window(h2, r + 3, 2, 128), j, left)))
        d1 = [[None, None] for _ in range(4)]
        for m in range(2):
            y = dot(wb[m], quad(lambda r: taps(d2, m, r), j, left))
            for i in range(4):
                hidden = inner[m, 64 * (j + i) : 64 * (j + i + 1), :].astype(F32)
                pre = y[64 * (i % 2) : 64 * (i % 2 + 1), wide * (i // 2) : wide * (i // 2 + 1)]
                d1[i][m] = (pre * (1.0 - hidden * hidden) * mask).astype(BF16)
        x = quad(lambda r: window(xb, r + 4, 4, 16), j, left)
        add(sums, "f", dot_nt(x, quad(lambda r: jnp.concatenate(d1[r - j] + d1[r - j + 1], 0), j, left)))
    first, last = (sums[name][0:48, 0:128] + sums[name][16:64, 128:256] for name in "fl")
    last = jnp.where(lanes_of(last.shape) < 64, last, pltpu.roll(last, 46, 0))
    places = [(a, b) for a in range(3) for b in range(3)]
    pieces = [first[16 * a + 4 * b : 16 * a + 4 * b + 3] for a, b in places]
    pieces += [last[16 * a + 4 * b : 16 * a + 4 * b + 2] for a, b in places]
    out[...] = jnp.concatenate(pieces + [jnp.zeros((3, 128), F32)], 0)


def tree_sum(values):
    while len(values) > 1:
        values = [sum(values[i : i + 2][1:], values[i]) for i in range(0, len(values), 2)]
    return values[0]


def sum_lat_kernel(mine, outer, *refs):
    parts, out = refs[:-1], refs[-1]
    total = tree_sum([mine[...]] + [decode(ref) for ref in parts])
    out[...] = encode(jnp.concatenate([total, outer[...]], 0))


def sum_lon_kernel(*refs):
    parts, out = refs[:-1], refs[-1]
    out[...] = encode(tree_sum([decode(ref) for ref in parts]))


def finish_kernel(*refs):
    nlat = lax.axis_size("lat")
    parts, (first, middle, last, packed) = refs[:nlat], refs[nlat:]
    part = packed.shape[0] // nlat
    me = lax.axis_index("lat")
    values = [decode(ref) for ref in parts]
    for k, value in enumerate(values):
        packed[pl.ds(pl.multiple_of((me ^ k) * part, 8), part), :] = value[:part]
    outer = tree_sum([value[part:] for value in values])
    for m in range(2):
        for b in range(3):
            two = packed[192 * m + 64 * b : 192 * m + 64 * (b + 1), :]
            third = packed[384 + 64 * b : 384 + 64 * (b + 1), :]
            middle[m, b] = two[:, 0:64]
            middle[m, 3 + b] = two[:, 64:128]
            middle[m, 6 + b] = third[:, 64 * m : 64 * (m + 1)]
    for m in range(2):
        for k in range(9):
            for c in range(3):
                at = 3 * k + c
                first[k, c, m : m + 1] = outer[at : at + 1, 64 * m : 64 * (m + 1)]
            at = 27 + 2 * (3 * (2 - k // 3) + k % 3)
            last[m, k] = outer[at : at + 2, 64 * m : 64 * (m + 1)]


def ocean_kernel(
    total_rows, members,
    velo, temp, land, mine, other, got_lon, other_lon, got_lat, other_lat,
    velo_next, temp_next,
):
    levels, rows, cols = temp.shape

    def whole(ref, at, size):
        value = ref[...].astype(F32)
        return value[at : at + size] + value[at + size : at + 2 * size]

    ahead = heads_up("lon")
    near, far = (whole(ref, ref.shape[0] - 2 * rows, rows) for ref in (got_lon, other_lon))
    ceast, cwest = jnp.where(ahead, near, far), jnp.where(ahead, far, near)
    lines = 3 * levels * (cols // 128)
    near, far = (whole(ref, ref.shape[0] - 2 * lines, lines) for ref in (got_lat, other_lat))
    near, far = (
        jnp.concatenate([x[3 * levels * j : 3 * levels * (j + 1)] for j in range(cols // 128)], 1) for x in (near, far)
    )
    rnorth, rsouth = north_and_south(near, far)
    height, width = rows // COARSE, cols // COARSE
    row = subs_of((rows, cols))
    lane = lanes_of((rows, cols))
    ids = (lax.axis_index("lat") * rows + subs_of((rows, 128))).astype(F32)
    coriolis = jnp.sin(F32(-math.pi / 2) + F32(math.pi) * (ids + 0.5) / F32(total_rows))
    coriolis = jnp.concatenate([coriolis] * (cols // 128), 1)
    wet = land[...].astype(F32) * 0.1
    up = [
        jnp.where(lanes_of((rows, 2 * height)) == subs_of((rows, 2 * height)) // COARSE * 2 + o, F32(1.0), F32(0.0)).astype(BF16)
        for o in range(2)
    ]
    tall = [[dot(u, ref[...]).astype(BF16) for ref in (mine, other)] for u in up]
    spread_k = subs_of((256, cols))
    spread_i = lanes_of((256, cols)) // COARSE

    def neighbours(q, n):
        east = jnp.where(lane == cols - 1, ceast[:, n : n + 1], pltpu.roll(q, cols - 1, 1))
        west = jnp.where(lane == 0, cwest[:, n : n + 1], pltpu.roll(q, 1, 1))
        north = jnp.where(row == rows - 1, rnorth[n : n + 1], pltpu.roll(q, rows - 1, 0))
        south = jnp.where(row == 0, rsouth[n : n + 1], pltpu.roll(q, 1, 0))
        return east, west, north, south

    cum_x = cum_y = None
    for l in range(levels):
        u, v, t = velo[0, l], velo[1, l], temp[l]
        ue, uw, un, us = neighbours(u, l)
        ve, vw, vn, vs = neighbours(v, levels + l)
        te, tw, tn, ts = neighbours(t, 2 * levels + l)
        dx, dy = te - tw, tn - ts
        cum_x = dx if cum_x is None else cum_x + dx
        cum_y = dy if cum_y is None else cum_y + dy
        spread = jnp.where(spread_k == spread_i + (32 * l + SIDE), F32(1.0), F32(0.0)).astype(BF16)
        f = []
        for o in range(2):
            total = None
            for part in tall[o]:
                term = dot(part[:, 128 * l : 128 * (l + 2)], spread)
                total = term if total is None else total + term
            f.append(total * (1.0 / members))
        lap_u = ue + uw + un + us - 4.0 * u
        lap_v = ve + vw + vn + vs - 4.0 * v
        lap_t = te + tw + tn + ts - 4.0 * t
        velo_next[0, l] = u + wet * (coriolis * v + 0.25 * cum_x + 0.5 * lap_u + f[0])
        velo_next[1, l] = v + wet * (0.25 * cum_y - coriolis * u + 0.5 * lap_v + f[1])
        temp_next[l] = t + wet * (0.3 * lap_t - 0.5 * (u * dx + v * dy))


def weights_kernel(first, middle, last, wf, wm, wb, wl, wlt):
    hid = middle.shape[-1]

    def slide(pieces, copies):
        zero = jnp.zeros_like(pieces[0])
        return [jnp.concatenate([zero] * r + pieces + [zero] * (copies - 1 - r), 1) for r in range(copies)]

    for m in range(2):
        for b in range(3):
            taps = [middle[m, 3 * a + b] for a in range(3)]
            turned = jnp.concatenate([t.astype(F32) for t in taps[::-1]], 0).T.astype(BF16)
            turned = [turned[:, hid * s : hid * (s + 1)] for s in range(3)]
            for ref, pieces, at in ((wm, taps, b), (wb, turned, 2 - b)):
                for r, block in enumerate(slide(pieces, 2)):
                    ref[m, hid * r : hid * (r + 1), 4 * hid * at : 4 * hid * (at + 1)] = block
    zero = jnp.zeros((1, 2 * hid), F32)
    rows = []
    for a in range(3):
        for b in range(4):
            for c in range(4):
                if b < 3 and c < 3:
                    w = first[3 * a + b, c].astype(F32)
                    rows.append(jnp.concatenate([w[0:1], w[1:2]], 1))
                else:
                    rows.append(zero)
    turned = jnp.concatenate(rows + [zero] * (2 * hid - 48), 0).T
    for r in range(H1_ROWS):
        wf[2 * hid * r : 2 * hid * (r + 1), :] = pltpu.roll(turned, 16 * r, 1).astype(BF16)[:, : wf.shape[1]]
    zero = jnp.zeros((2, hid), F32)
    by_row = []
    for a in range(3):
        rows = []
        for b in range(3):
            w = [last[m, 3 * a + b].astype(F32) for m in range(2)]
            rows += [jnp.concatenate([w[0], zero], 1), jnp.concatenate([zero, w[1]], 1)]
        by_row.append(jnp.concatenate(rows + [jnp.zeros((4, 2 * hid), F32)], 0))
    none = jnp.zeros((16, 2 * hid), F32)
    for e in range(-1, 3):
        taps = [by_row[r - e + 1] if abs(r - e) <= 1 else none for r in range(2)]
        wl[16 * (e + 1) : 16 * (e + 2), :] = jnp.concatenate(taps, 1).astype(BF16)
    wlt[...] = jnp.concatenate(by_row[::-1], 0).T.astype(BF16)


def pairs_of(lat=None, lon=None):
    sizes = [lax.axis_size(name) for name in ("lat", "lon", "mem")]
    pairs = []
    for index in itertools.product(*(range(n) for n in sizes)):
        place = list(index)
        if lat is not None:
            place[0] += 1 if (index[0] + lat[index[2]]) % 2 == 0 else -1
            place[0] %= sizes[0]
        if lon is not None:
            place[1] += 1 if (index[1] + lon[index[2]]) % 2 == 0 else -1
            place[1] %= sizes[1]
        pairs.append(tuple((i[0] * sizes[1] + i[1]) * sizes[2] + i[2] for i in (index, place)))
    return pairs


def swap_cores(value):
    return lax.ppermute(value, "mem", [(i, i ^ 1) for i in range(lax.axis_size("mem"))])


def partner(value, axis, k):
    return lax.ppermute(value, axis, [(i, i ^ k) for i in range(lax.axis_size(axis))])


def per_device(velo, temp, land, target, w_first, w_middle, w_last):
    levels, rows, cols = temp.shape
    height, width = rows // COARSE, cols // COARSE
    wide = levels * (width + 2 * SIDE)
    vregs = wide // 128
    members = w_first.shape[0] * lax.axis_size("mem")
    nlat, nlon = lax.axis_size("lat"), lax.axis_size("lon")
    total_coarse = height * nlat
    count = 2.0 * levels * total_coarse * width * nlon
    params = pltpu.CompilerParams(vmem_limit_bytes=VMEM_LIMIT)
    vm = pltpu.VMEM

    def f32(*shape):
        return jax.ShapeDtypeStruct(shape, F32)

    def bf16(*shape):
        return jax.ShapeDtypeStruct(shape, BF16)

    hid = w_middle.shape[-1]
    hbm = pl.BlockSpec(memory_space=pltpu.HBM)
    tall = 8 * height
    core = (0, 1)
    raw = (jnp.transpose(w_first, (1, 3, 0, 2)), w_middle, w_last)
    own, to_lon, edges, *raw = pl.pallas_call(
        coarse_kernel,
        in_specs=[hbm] * 6,
        out_shape=(
            vm((vregs, tall, 128), F32),
            vm((tall + 2 * rows, 128), BF16),
            vm((2, 3 * levels * (cols // 128), 128), F32),
            *(vm(w.shape, BF16) for w in raw),
        ),
        scratch_shapes=[
            vm(velo.shape, F32),
            vm(temp.shape, F32),
            vm(target.shape, BF16),
            vm((cols // 128, levels * rows, 128), F32),
            pltpu.SemaphoreType.DMA((7,)),
        ],
        compiler_params=pltpu.CompilerParams(vmem_limit_bytes=COARSE_LIMIT),
        name="coarse",
    )(velo, temp, target, *raw)
    everywhere = ("lat", "lon", "mem")
    got_lon = lax.ppermute(to_lon, everywhere, pairs_of(lon=core))
    weights = pl.pallas_call(
        weights_kernel,
        out_shape=(
            bf16(H1_ROWS * 2 * hid, 16 * (H1_ROWS + 2)),
            bf16(2, 2 * hid, 12 * hid),
            bf16(2, 2 * hid, 12 * hid),
            bf16(64, 4 * hid),
            bf16(2 * hid, 48),
        ),
        cost_estimate=pl.CostEstimate(flops=10**8, bytes_accessed=4 * 10**6, transcendentals=0),
        compiler_params=params,
        name="weights",
    )(*raw)
    other_lon = swap_cores(got_lon)
    message = bf16(-(-PACKED * vregs // 16) * 16 + 2 * edges.shape[1], 128)
    full, to_lat = pl.pallas_call(
        merge_kernel,
        out_shape=(f32(vregs, tall, 128), message),
        compiler_params=params,
        name="merge",
    )(own, got_lon, other_lon, edges)
    got_lat = lax.ppermute(to_lat, everywhere, pairs_of(lat=core))
    wf, wm, wb, wl, wlt = weights
    tops = pl.pallas_call(
        inner_kernel,
        out_shape=(vm((3, 2, 64 * (height - 2), wide), BF16), vm((128 * (height - 4), wide), BF16)),
        scratch_shapes=[vm((16 * height, wide), BF16)],
        cost_estimate=pl.CostEstimate(flops=10**9, bytes_accessed=4 * 10**6, transcendentals=0),
        compiler_params=params,
        name="inner",
    )(full, wf, wm)
    got_lat, tops, weights = lax.optimization_barrier((got_lat, tops, (wf, wm, wb, wl, wlt)))
    other_lat = swap_cores(got_lat)

    total = -(-576 // (GROUP * nlat)) * GROUP * nlat
    part = total // nlat
    coded = jax.ShapeDtypeStruct((part + GROUP, 128), jnp.int16)
    wf, wm, wb, wl, wlt = weights
    force, *rest = pl.pallas_call(
        functools.partial(closure_kernel, 2.0 / count, total_coarse),
        out_shape=(
            bf16(2 * height, wide),
            *[coded] * (nlat - 1),
            f32(part, 128),
            vm((16 * (height + 2 * HALO), wide), BF16),
            vm((2, 64 * height, wide), BF16),
            vm((128 * (height + 6), wide), BF16),
            vm((16 * (height + 4), wide), BF16),
            vm((3, 2, 64 * (height + 2), wide), BF16),
        ),
        scratch_shapes=[
            vm((8 * (height + 2 * HALO), wide), F32),
            vm((3, 2, 64 * (height + 8), wide), BF16),
            vm((32 * (height + 6), wide), F32),
            vm((2 * height, wide), F32),
            vm((total, 128), F32),
        ],
        compiler_params=params,
        name="closure",
    )(full, got_lat, other_lat, *tops, wf, wm, wl, wlt)
    sends, (mine, *kept) = rest[: nlat - 1], rest[nlat - 1 :]

    other = swap_cores(force)
    parts = [partner(sends[k - 1], "lat", k) for k in reversed(range(1, nlat))][::-1]
    outer = pl.pallas_call(
        outer_grads_kernel,
        out_shape=f32(48, 128),
        cost_estimate=pl.CostEstimate(flops=2 * 10**9, bytes_accessed=4 * 10**6, transcendentals=0),
        compiler_params=params,
        name="outer_grads",
    )(*kept, wb)
    def add_up(kernel, values, name):
        return pl.pallas_call(
            kernel,
            out_shape=jax.ShapeDtypeStruct((part + 48 + GROUP, 128), jnp.int16),
            compiler_params=params,
            name=name,
        )(*values)

    parts, other = lax.optimization_barrier((parts, other))
    summed = add_up(sum_lat_kernel, [mine, outer, *parts], "sum_lat")
    velo_next, temp_next = pl.pallas_call(
        functools.partial(ocean_kernel, rows * nlat, members),
        out_shape=(jax.ShapeDtypeStruct(velo.shape, F32), jax.ShapeDtypeStruct(temp.shape, F32)),
        cost_estimate=pl.CostEstimate(flops=10**8, bytes_accessed=4 * 10**6, transcendentals=0),
        compiler_params=params,
        name="ocean",
    )(velo, temp, land, force, other, got_lon, other_lon, got_lat, other_lat)
    parts = [summed] + [partner(summed, "lon", k) for k in range(1, nlon)]
    parts, velo_next, temp_next = lax.optimization_barrier((parts, velo_next, temp_next))
    summed = add_up(sum_lon_kernel, parts, "sum_lon")
    parts = [summed] + [partner(summed, "lat", k) for k in range(1, nlat)]
    members_here, taps, _, inputs = w_first.shape
    first, middle, last = pl.pallas_call(
        finish_kernel,
        out_shape=(f32(taps, inputs, members_here, hid), f32(*w_middle.shape), f32(*w_last.shape)),
        scratch_shapes=[vm((total, 128), F32)],
        compiler_params=params,
        name="finish",
    )(*parts)
    return (velo_next, temp_next, jnp.transpose(first, (2, 0, 3, 1)), middle, last)


def solution(mesh):
    return jax.shard_map(
        per_device,
        mesh=mesh,
        in_specs=(
            P(None, None, "lat", "lon"),
            P(None, "lat", "lon"),
            P("lat", "lon"),
            P(None, None, "lat", "lon"),
            P("mem", None, None, None),
            P("mem", None, None, None),
            P("mem", None, None, None),
        ),
        out_specs=(
            P(None, None, "lat", "lon"),
            P(None, "lat", "lon"),
            P("mem", None, None, None),
            P("mem", None, None, None),
            P("mem", None, None, None),
        ),
        check_vma=False,
    )
```

```python
import functools
import itertools
import math

import jax
import jax.numpy as jnp
from jax import lax
from jax.experimental import pallas as pl
from jax.experimental.pallas import tpu as pltpu
from jax.sharding import PartitionSpec as P

COARSE = 4
HALO = 5
PACKED = 3 * HALO + 4
GROUP = 16
LEVELS = 32000.0
H1_ROWS = 4
SIDE = 16
F32 = jnp.float32
BF16 = jnp.bfloat16
VMEM_LIMIT = 32 * 1024 * 1024
COARSE_LIMIT = 60 * 1024 * 1024


def dot(a, b, **kw):
    return jnp.dot(a, b, preferred_element_type=F32, **kw)


def dot_nt(a, b):
    return lax.dot_general(a, b, (((1,), (1,)), ((), ())), preferred_element_type=F32)


def lanes_of(shape):
    return lax.broadcasted_iota(jnp.int32, shape, len(shape) - 1)


def subs_of(shape):
    return lax.broadcasted_iota(jnp.int32, shape, len(shape) - 2)


def heads_up(axis):
    return (lax.axis_index(axis) + lax.axis_index("mem")) % 2 == 0


def north_and_south(got, other):
    ahead, place = heads_up("lat"), lax.axis_index("lat")
    north, south = jnp.where(ahead, got, other), jnp.where(ahead, other, got)
    return jnp.where(place < lax.axis_size("lat") - 1, north, 0.0), jnp.where(place > 0, south, 0.0)


def halves(x):
    high = x.astype(BF16).astype(F32)
    return [high, x - high]


def encode(x):
    coded, exponents = [], []
    for at in range(0, x.shape[0], GROUP):
        part = x[at : at + GROUP]
        most = jnp.max(jnp.abs(part), axis=0, keepdims=True)
        exponent = jnp.ceil(jnp.log2(jnp.maximum(most, 1e-30)))
        coded.append(jnp.round(part * (jnp.exp2(-exponent) * LEVELS)))
        exponents.append(exponent)
    exponents.append(jnp.zeros((GROUP - len(exponents), x.shape[1]), F32))
    return jnp.concatenate(coded + exponents, 0).astype(jnp.int32).astype(jnp.int16)


def decode(ref):
    value = ref[...].astype(jnp.int32).astype(F32)
    rows = value.shape[0] - GROUP
    scale = jnp.exp2(value[rows:]) * (1.0 / LEVELS)
    pieces = [value[at : at + GROUP] * scale[i : i + 1] for i, at in enumerate(range(0, rows, GROUP))]
    return jnp.concatenate(pieces, 0)


def row_sums(ref, fine, spans):
    levels, rows, _ = ref.shape
    for j, span in enumerate(spans):
        fine[j] = ref[:, :, span].reshape(levels * rows, 128)
    step = levels * rows // COARSE
    return [
        sum(fine[j, pl.ds(s, step, stride=COARSE), :] for s in range(COARSE)) for j in range(len(spans))
    ]


def pool_columns(x):
    cols = x.shape[1]
    here = subs_of((cols, 128)) // COARSE == lanes_of((cols, 128))
    pool = jnp.where(here, F32(1.0 / COARSE**2), F32(0.0)).astype(BF16)
    high, rest = halves(x)
    terms = jnp.concatenate([high] + halves(rest), 0).astype(BF16)
    y = dot(terms, pool)
    size = x.shape[0]
    return ((y[2 * size :] + y[size : 2 * size]) + y[:size]).astype(BF16).astype(F32)


def edge_kernel(velo_hbm, temp_hbm, target_hbm, *refs):
    from_hbm, (to_lon, velo, temp, target, *weights), (fine, cells, sems) = refs[:3], refs[3:10], refs[10:]
    levels, rows, cols = temp.shape
    height = rows // COARSE
    pairs = [(velo_hbm.at[0], velo.at[0]), (velo_hbm.at[1], velo.at[1]), (temp_hbm, temp), (target_hbm, target)]
    pairs += zip(from_hbm, weights)
    copies = [pltpu.make_async_copy(*pair, sems.at[i]) for i, pair in enumerate(pairs)]
    for copy in copies:
        copy.start()
    spans = (slice(0, 128), slice(cols - 128, cols))
    sums = []
    for f in range(3):
        copies[f].wait()
        sums += row_sums(temp if f == 2 else velo.at[f], fine, spans)
    mean = pool_columns(jnp.concatenate(sums, 0))
    copies[3].wait()
    lane = lanes_of((height, 128))
    cells[...] = jnp.zeros_like(cells)
    for side in range(2):
        begin = SIDE - HALO * side
        for ch in range(7):
            total = jnp.zeros((height, 128), F32)
            for l in range(levels):
                if ch < 4:
                    x, shift = target[ch % 2, l].astype(F32), SIDE
                else:
                    at = ((2 * (ch - 4) + side) * levels + l) * height
                    x, shift = mean[at : at + height], SIDE if side == 0 else SIDE - 128 // COARSE
                at = 32 * l + begin
                total = jnp.where((lane >= at) & (lane < at + HALO), pltpu.roll(x, (32 * l + shift) % 128, 1), total)
            cells[side, pl.ds(ch, height, stride=8), :] = total
    lane = lanes_of((rows, 128))
    first = jnp.zeros((rows, 128), F32)
    last = jnp.zeros((rows, 128), F32)
    for f in range(3):
        ref = temp if f == 2 else velo.at[f]
        for l in range(levels):
            n = f * levels + l
            first = jnp.where(lane == n, pltpu.roll(ref[l, :, 0:128], n, 1), first)
            last = jnp.where(lane == n, pltpu.roll(ref[l, :, cols - 128 :], n + 1, 1), last)
    west, east = (jnp.concatenate([cells[i]] + halves(x), 0) for i, x in enumerate((first, last)))
    to_lon[...] = jnp.where(heads_up("lon"), east, west).astype(BF16)
    for copy in copies[4:]:
        copy.wait()


def coarse_kernel(velo, temp, target, own, edges, fine):
    levels, rows, cols = temp.shape
    height, width = rows // COARSE, cols // COARSE
    vregs = levels + 1
    spans = [slice(128 * j, 128 * (j + 1)) for j in range(cols // 128)]

    def field(f):
        return temp if f == 2 else velo.at[f]

    mean = pool_columns(jnp.concatenate([jnp.concatenate(row_sums(field(f), fine, spans), 1) for f in range(3)], 0))
    lane = lanes_of((height, 128))

    def place(tiles):
        pieces = []
        for j in range(vregs):
            value = jnp.zeros((height, 128), F32)
            if j < levels:
                moved = pltpu.roll(tiles[j], 32 * j + SIDE, 1)
                value = jnp.where(lane >= 32 * j + SIDE, moved, value)
            if j > 0:
                moved = pltpu.roll(tiles[j - 1], 32 * (j - 1) + SIDE, 1)
                value = jnp.where(lane < 32 * (j - 1) + SIDE, moved, value)
            pieces.append(value)
        return pieces

    for ch in range(8):
        if ch < 4:
            tiles = [target[ch % 2, l].astype(F32) for l in range(levels)]
        elif ch < 7:
            base = (ch - 4) * levels * height
            tiles = [mean[base + l * height : base + (l + 1) * height] for l in range(levels)]
        if ch < 7:
            pieces = place(tiles)
        else:
            pieces = [jnp.zeros((height, 128), F32)] * vregs
        for j in range(vregs):
            own[j, pl.ds(ch, height, stride=8), :] = pieces[j]
    for i, row in enumerate((rows - 1, 0)):
        line = [field(f)[:, row, 128 * j : 128 * (j + 1)] for j in range(cols // 128) for f in range(3)]
        edges[i] = jnp.concatenate(line, 0)


def merge_kernel(own, got, other, edges, full, message):
    vregs, tall = own.shape[:2]
    levels = vregs - 1
    ahead = heads_up("lon")
    near, far = (ref[...].astype(F32)[0:tall] for ref in (got, other))
    right, left = jnp.where(ahead, near, far), jnp.where(ahead, far, near)
    lane = lanes_of((tall, 128))
    upper, lower = [], []
    for j in range(vregs):
        value = own[j]
        if j < levels:
            at = 32 * j + SIDE
            value = jnp.where((lane >= at - HALO) & (lane < at), left, value)
        if j > 0:
            at = 32 * (j - 1) + SIDE
            value = jnp.where((lane >= at) & (lane < at + HALO), right, value)
        full[j] = value
        last = tall // 8
        for pieces, first, goals in ((upper, last - HALO, (last - 2, last - 1)), (lower, 0, (0, 1))):
            pieces += [value[8 * r + 4 : 8 * r + 7] for r in range(first, first + HALO)]
            pieces += [value[8 * r : 8 * r + 2] for r in goals]
    pad = [jnp.zeros((-PACKED * vregs % 16, 128), F32)]
    upper, lower = (jnp.concatenate(x + pad + halves(edges[i]), 0) for i, x in enumerate((upper, lower)))
    message[...] = jnp.where(heads_up("lat"), upper, lower).astype(BF16)


def unpack(message, j, goal_rows):
    at = PACKED * j
    rows = []
    for i in range(HALO):
        goal = jnp.zeros((2, 128), F32)
        if i in goal_rows:
            start = at + 3 * HALO + 2 * goal_rows.index(i)
            goal = message[start : start + 2]
        rows += [goal, goal, message[at + 3 * i : at + 3 * (i + 1)], jnp.zeros((1, 128), F32)]
    return jnp.concatenate(rows, 0)


def add(sums, name, term):
    sums[name] = sums[name] + term if name in sums else term


def window(ref, row, rows, step):
    return ref[step * row : step * (row + rows), :]


def quad(get, row, left):
    return get(row) if left <= 2 else jnp.concatenate([get(row), get(row + 2)], 1)


def taps(ref, m, row):
    return jnp.concatenate([ref[b, m, 64 * row : 64 * (row + 4), :] for b in range(3)], 0)


def columns_around(x):
    wide = x.shape[1]
    return [pltpu.roll(x, 1, 1), x, pltpu.roll(x, wide - 1, 1)]


def spread_columns(x):
    wide = x.shape[1]
    one = jnp.where(subs_of(x.shape) < 4, pltpu.roll(pltpu.roll(x, 1, 1), 4, 0), x)
    two = pltpu.roll(pltpu.roll(x, wide - 1, 1), 4, 0)
    return jnp.concatenate([one, two], 0).astype(BF16)


def inner_kernel(full, wf, wm, h1, h2, xb):
    vregs, height = full.shape[0], full.shape[1] // 8
    wide = 128 * vregs
    for r in range(height):
        x = jnp.concatenate([full[j, 8 * r : 8 * (r + 1), :] for j in range(vregs)], 1)
        xb[16 * r : 16 * (r + 1), :] = spread_columns(x)
    half = (height - 2) // 2
    y = dot(wf[0 : 128 * half, 0 : 16 * (half + 2)], jnp.concatenate([window(xb, r, half + 2, 16) for r in (0, half)], 1))
    for i in range(2 * half):
        t = i // half
        h = jnp.tanh(y[128 * (i - t * half) : 128 * (i - t * half + 1), wide * t : wide * (t + 1)]).astype(BF16)
        for m in range(2):
            for b, moved in enumerate(columns_around(h[64 * m : 64 * (m + 1)])):
                h1[b, m, 64 * i : 64 * (i + 1), :] = moved
    for p in range(0, height - 4, 4):
        for m in range(2):
            y = dot(wm[m], quad(lambda r: taps(h1, m, r), p, 4))
            for i in range(4):
                pre = y[64 * (i % 2) : 64 * (i % 2 + 1), wide * (i // 2) : wide * (i // 2 + 1)]
                at = 128 * (p + i) + 64 * m
                h2[at : at + 64, :] = jnp.tanh(pre).astype(BF16)


def inner_lanes(wide):
    within = lanes_of((1, wide)) % (128 + 2 * SIDE)
    return jnp.where((within >= SIDE) & (within < SIDE + 128), F32(1.0), F32(0.0))


def closure_kernel(
    scale, total_rows,
    full, got, other, h1_inner, h2_inner, wf, wm, wl, wlt,
    force, *rest,
):
    nlat = lax.axis_size("lat")
    sends, (mine, xb, inner, h2, gb, d2, xf, h1, yl, pf, packed) = rest[: nlat - 1], rest[nlat - 1 :]
    vregs = full.shape[0]
    height = full.shape[1] // 8
    wide = 128 * vregs
    span = height + 2 * HALO
    first_row = lax.axis_index("lat") * height

    def inside(row):
        at = first_row + row
        return jnp.where((at >= 0) & (at < total_rows), F32(1.0), F32(0.0))

    north, south = north_and_south(got[...].astype(F32), other[...].astype(F32))
    for j in range(vregs):
        above, below = unpack(north, j, (0, 1)), unpack(south, j, (HALO - 2, HALO - 1))
        xf[:, 128 * j : 128 * (j + 1)] = jnp.concatenate([below, full[j], above], 0)

    sub = subs_of((8, wide))
    tile_b = inner_lanes(wide).astype(BF16)

    for r in range(span):
        xb[16 * r : 16 * (r + 1), :] = spread_columns(window(xf, r, 1, 8))

    known = range(5, height + 3)

    def h1_row(b, m, i):
        ref, at = (h1_inner, i - known[0]) if i in known else (h1, i)
        return ref[b, m, 64 * at : 64 * (at + 1), :]

    def make_h1(starts, count):
        weights = wf[0 : 128 * count, 0 : 16 * (count + 2)]
        y = dot(weights, jnp.concatenate([window(xb, r, count + 2, 16) for r in starts], 1))
        for t, start in enumerate(starts):
            for i in range(count):
                pre = y[128 * i : 128 * (i + 1), wide * t : wide * (t + 1)]
                h = (jnp.tanh(pre) * inside(start + i - 4)).astype(BF16)
                for m in range(2):
                    at = 64 * (start + i)
                    for b, moved in enumerate(columns_around(h[64 * m : 64 * (m + 1)])):
                        h1[b, m, at : at + 64, :] = moved

    def h1_rows(b, m, row):
        return jnp.concatenate([h1_row(b, m, row + i) for i in range(4)], 0)

    rows = height + 6
    h2[128 * 5 : 128 * (height + 1), :] = h2_inner[...]

    def make_h2(starts, count):
        for m in range(2):
            windows = [jnp.concatenate([h1_rows(b, m, r) for b in range(3)], 0) for r in starts]
            y = dot(wm[m, 0 : 64 * count, :], jnp.concatenate(windows, 1))
            for t, start in enumerate(starts):
                for i in range(count):
                    pre = y[64 * i : 64 * (i + 1), wide * t : wide * (t + 1)]
                    h = jnp.tanh(pre) * inside(start + i - 3)
                    at = 128 * (start + i) + 64 * m
                    h2[at : at + 64, :] = h.astype(BF16)

    def make_yl(p):
        y = dot(wl[...], quad(lambda r: window(h2, r, 2, 128), p, rows - p))
        for t in range(y.shape[1] // wide):
            at = 32 * (p + 2 * t)
            yl[at : at + 64, :] = y[:, wide * t : wide * (t + 1)]

    def make_g3(s):
        z = 0.0
        for pair in ((s, s + 2) if s % 2 == 0 else (s - 1, s + 1)):
            at = 32 * pair + 16 * (s + 2 - pair)
            z = z + yl[at : at + 16, :]
        pred = pltpu.roll(z[0:8], 1, 1) + pltpu.roll(z[0:8], 4, 0) + pltpu.roll(z[8:16], wide - 1, 1)
        goal = window(xf, s + 3, 1, 8)
        g = ((pred - goal) * scale * inside(s - 2)).astype(BF16).astype(F32)
        one = jnp.where(sub < 4, pltpu.roll(g, wide - 1, 1), pltpu.roll(g, 4, 0))
        two = pltpu.roll(g, 1, 1)
        gb[16 * s : 16 * (s + 1), :] = jnp.concatenate([one, two], 0).astype(BF16)
        if 2 <= s < height + 2:
            both = pred + pltpu.roll(pred, 6, 0)
            pf[2 * (s - 2) : 2 * (s - 1), :] = both[0:2]

    def make_d2(u):
        y = dot(wlt[...], jnp.concatenate([window(gb, r, 3, 16) for r in (u, u + 1)], 1))
        for t in range(2):
            hidden = window(h2, u + t + 2, 1, 128).astype(F32)
            d = y[:, wide * t : wide * (t + 1)] * (1.0 - hidden * hidden) * inside(u + t - 1)
            for m in range(2):
                for b, moved in enumerate(columns_around(d[64 * m : 64 * (m + 1)].astype(BF16))):
                    d2[b, m, 64 * (u + t) : 64 * (u + t + 1), :] = moved

    sums = {}

    def make_grads(j):
        left = height - j
        for m in range(2):

            def moved(r):
                return jnp.concatenate([d2[b, m, 64 * (r + 1) : 64 * (r + 3), :] for b in (2, 1, 0)], 0)

            rhs = quad(lambda r: h1_rows(1, m, r + 3) * tile_b, j, left)
            add(sums, m, dot_nt(quad(moved, j, left), rhs))

    make_h1((0, height + 4), 4)
    make_h1((4, height + 3), 1)
    make_h2((0, 2), 2)
    make_h2((4, height + 1), 1)
    for p in range(0, height, 4):
        make_yl(p)
    make_h2((height + 2, height + 4), 2)
    for p in range(height, rows, 4):
        make_yl(p)
    for m in range(2):
        for r in range(height):
            inner[m, 64 * r : 64 * (r + 1), :] = h1_row(1, m, r + 4)
    for r in range(height + 4):
        make_g3(r)
    for u in range(0, height + 2, 2):
        make_d2(u)
    for j in range(0, height, 4):
        make_grads(j)
    force[...] = pf[...].astype(BF16)
    gm = []
    for m in range(2):
        parts = [sums[m][64 * i : 64 * (i + 1)] for i in range(6)]
        gm.append(jnp.concatenate([parts[2 * b][:, 0:192] + parts[2 * b + 1][:, 64:256] for b in range(3)], 0))
    for m in range(2):
        packed[192 * m : 192 * (m + 1), :] = gm[m][:, 0:128]
    packed[384:576, :] = jnp.concatenate([gm[0][:, 128:192], gm[1][:, 128:192]], 1)
    if packed.shape[0] > 576:
        packed[576:, :] = jnp.zeros((packed.shape[0] - 576, 128), F32)
    part = packed.shape[0] // nlat
    me = lax.axis_index("lat")
    for k, ref in enumerate((mine, *sends)):
        value = packed[pl.ds(pl.multiple_of((me ^ k) * part, 8), part), :]
        ref[...] = value if k == 0 else encode(value)


def outer_grads_kernel(xb, inner, h2, gb, d2, wb, out):
    wide = xb.shape[1]
    height = xb.shape[0] // 16 - 2 * HALO
    mask = inner_lanes(wide)
    sums = {}
    for j in range(0, height, 4):
        left = height - j
        g = quad(lambda r: window(gb, r + 1, 4, 16) * mask.astype(BF16), j, left)
        add(sums, "l", dot_nt(g, quad(lambda r: window(h2, r + 3, 2, 128), j, left)))
        d1 = [[None, None] for _ in range(4)]
        for m in range(2):
            y = dot(wb[m], quad(lambda r: taps(d2, m, r), j, left))
            for i in range(4):
                hidden = inner[m, 64 * (j + i) : 64 * (j + i + 1), :].astype(F32)
                pre = y[64 * (i % 2) : 64 * (i % 2 + 1), wide * (i // 2) : wide * (i // 2 + 1)]
                d1[i][m] = (pre * (1.0 - hidden * hidden) * mask).astype(BF16)
        x = quad(lambda r: window(xb, r + 4, 4, 16), j, left)
        add(sums, "f", dot_nt(x, quad(lambda r: jnp.concatenate(d1[r - j] + d1[r - j + 1], 0), j, left)))
    first, last = (sums[name][0:48, 0:128] + sums[name][16:64, 128:256] for name in "fl")
    last = jnp.where(lanes_of(last.shape) < 64, last, pltpu.roll(last, 46, 0))
    places = [(a, b) for a in range(3) for b in range(3)]
    pieces = [first[16 * a + 4 * b : 16 * a + 4 * b + 3] for a, b in places]
    pieces += [last[16 * a + 4 * b : 16 * a + 4 * b + 2] for a, b in places]
    out[...] = jnp.concatenate(pieces + [jnp.zeros((3, 128), F32)], 0)


def tree_sum(values):
    while len(values) > 1:
        values = [sum(values[i : i + 2][1:], values[i]) for i in range(0, len(values), 2)]
    return values[0]


def sum_lat_kernel(mine, outer, *refs):
    parts, out = refs[:-1], refs[-1]
    total = tree_sum([mine[...]] + [decode(ref) for ref in parts])
    out[...] = encode(jnp.concatenate([total, outer[...]], 0))


def sum_lon_kernel(*refs):
    parts, out = refs[:-1], refs[-1]
    out[...] = encode(tree_sum([decode(ref) for ref in parts]))


def finish_kernel(*refs):
    nlat = lax.axis_size("lat")
    parts, (first, middle, last, packed) = refs[:nlat], refs[nlat:]
    part = packed.shape[0] // nlat
    me = lax.axis_index("lat")
    values = [decode(ref) for ref in parts]
    for k, value in enumerate(values):
        packed[pl.ds(pl.multiple_of((me ^ k) * part, 8), part), :] = value[:part]
    outer = tree_sum([value[part:] for value in values])
    for m in range(2):
        for b in range(3):
            two = packed[192 * m + 64 * b : 192 * m + 64 * (b + 1), :]
            third = packed[384 + 64 * b : 384 + 64 * (b + 1), :]
            middle[m, b] = two[:, 0:64]
            middle[m, 3 + b] = two[:, 64:128]
            middle[m, 6 + b] = third[:, 64 * m : 64 * (m + 1)]
    for m in range(2):
        for k in range(9):
            for c in range(3):
                at = 3 * k + c
                first[k, c, m : m + 1] = outer[at : at + 1, 64 * m : 64 * (m + 1)]
            at = 27 + 2 * (3 * (2 - k // 3) + k % 3)
            last[m, k] = outer[at : at + 2, 64 * m : 64 * (m + 1)]


def ocean_kernel(
    total_rows, members,
    velo, temp, land, mine, other, got_lon, other_lon, got_lat, other_lat,
    velo_next, temp_next,
):
    levels, rows, cols = temp.shape

    def whole(ref, at, size):
        value = ref[...].astype(F32)
        return value[at : at + size] + value[at + size : at + 2 * size]

    ahead = heads_up("lon")
    near, far = (whole(ref, ref.shape[0] - 2 * rows, rows) for ref in (got_lon, other_lon))
    ceast, cwest = jnp.where(ahead, near, far), jnp.where(ahead, far, near)
    lines = 3 * levels * (cols // 128)
    near, far = (whole(ref, ref.shape[0] - 2 * lines, lines) for ref in (got_lat, other_lat))
    near, far = (
        jnp.concatenate([x[3 * levels * j : 3 * levels * (j + 1)] for j in range(cols // 128)], 1) for x in (near, far)
    )
    rnorth, rsouth = north_and_south(near, far)
    height, width = rows // COARSE, cols // COARSE
    row = subs_of((rows, cols))
    lane = lanes_of((rows, cols))
    ids = (lax.axis_index("lat") * rows + subs_of((rows, 128))).astype(F32)
    coriolis = jnp.sin(F32(-math.pi / 2) + F32(math.pi) * (ids + 0.5) / F32(total_rows))
    coriolis = jnp.concatenate([coriolis] * (cols // 128), 1)
    wet = land[...].astype(F32) * 0.1
    up = [
        jnp.where(lanes_of((rows, 2 * height)) == subs_of((rows, 2 * height)) // COARSE * 2 + o, F32(1.0), F32(0.0)).astype(BF16)
        for o in range(2)
    ]
    tall = [[dot(u, ref[...]).astype(BF16) for ref in (mine, other)] for u in up]
    spread_k = subs_of((256, cols))
    spread_i = lanes_of((256, cols)) // COARSE

    def neighbours(q, n):
        east = jnp.where(lane == cols - 1, ceast[:, n : n + 1], pltpu.roll(q, cols - 1, 1))
        west = jnp.where(lane == 0, cwest[:, n : n + 1], pltpu.roll(q, 1, 1))
        north = jnp.where(row == rows - 1, rnorth[n : n + 1], pltpu.roll(q, rows - 1, 0))
        south = jnp.where(row == 0, rsouth[n : n + 1], pltpu.roll(q, 1, 0))
        return east, west, north, south

    cum_x = cum_y = None
    for l in range(levels):
        u, v, t = velo[0, l], velo[1, l], temp[l]
        ue, uw, un, us = neighbours(u, l)
        ve, vw, vn, vs = neighbours(v, levels + l)
        te, tw, tn, ts = neighbours(t, 2 * levels + l)
        dx, dy = te - tw, tn - ts
        cum_x = dx if cum_x is None else cum_x + dx
        cum_y = dy if cum_y is None else cum_y + dy
        spread = jnp.where(spread_k == spread_i + (32 * l + SIDE), F32(1.0), F32(0.0)).astype(BF16)
        f = []
        for o in range(2):
            total = None
            for part in tall[o]:
                term = dot(part[:, 128 * l : 128 * (l + 2)], spread)
                total = term if total is None else total + term
            f.append(total * (1.0 / members))
        lap_u = ue + uw + un + us - 4.0 * u
        lap_v = ve + vw + vn + vs - 4.0 * v
        lap_t = te + tw + tn + ts - 4.0 * t
        velo_next[0, l] = u + wet * (coriolis * v + 0.25 * cum_x + 0.5 * lap_u + f[0])
        velo_next[1, l] = v + wet * (0.25 * cum_y - coriolis * u + 0.5 * lap_v + f[1])
        temp_next[l] = t + wet * (0.3 * lap_t - 0.5 * (u * dx + v * dy))


def weights_kernel(first, middle, last, wf, wm, wb, wl, wlt):
    hid = middle.shape[-1]

    def slide(pieces, copies):
        zero = jnp.zeros_like(pieces[0])
        return [jnp.concatenate([zero] * r + pieces + [zero] * (copies - 1 - r), 1) for r in range(copies)]

    for m in range(2):
        for b in range(3):
            taps = [middle[m, 3 * a + b] for a in range(3)]
            turned = jnp.concatenate([t.astype(F32) for t in taps[::-1]], 0).T.astype(BF16)
            turned = [turned[:, hid * s : hid * (s + 1)] for s in range(3)]
            for ref, pieces, at in ((wm, taps, b), (wb, turned, 2 - b)):
                for r, block in enumerate(slide(pieces, 2)):
                    ref[m, hid * r : hid * (r + 1), 4 * hid * at : 4 * hid * (at + 1)] = block
    zero = jnp.zeros((1, 2 * hid), F32)
    rows = []
    for a in range(3):
        for b in range(4):
            for c in range(4):
                if b < 3 and c < 3:
                    w = first[3 * a + b, c].astype(F32)
                    rows.append(jnp.concatenate([w[0:1], w[1:2]], 1))
                else:
                    rows.append(zero)
    turned = jnp.concatenate(rows + [zero] * (2 * hid - 48), 0).T
    for r in range(H1_ROWS):
        wf[2 * hid * r : 2 * hid * (r + 1), :] = pltpu.roll(turned, 16 * r, 1).astype(BF16)[:, : wf.shape[1]]
    zero = jnp.zeros((2, hid), F32)
    by_row = []
    for a in range(3):
        rows = []
        for b in range(3):
            w = [last[m, 3 * a + b].astype(F32) for m in range(2)]
            rows += [jnp.concatenate([w[0], zero], 1), jnp.concatenate([zero, w[1]], 1)]
        by_row.append(jnp.concatenate(rows + [jnp.zeros((4, 2 * hid), F32)], 0))
    none = jnp.zeros((16, 2 * hid), F32)
    for e in range(-1, 3):
        taps = [by_row[r - e + 1] if abs(r - e) <= 1 else none for r in range(2)]
        wl[16 * (e + 1) : 16 * (e + 2), :] = jnp.concatenate(taps, 1).astype(BF16)
    wlt[...] = jnp.concatenate(by_row[::-1], 0).T.astype(BF16)


def pairs_of(lat=None, lon=None):
    sizes = [lax.axis_size(name) for name in ("lat", "lon", "mem")]
    pairs = []
    for index in itertools.product(*(range(n) for n in sizes)):
        place = list(index)
        if lat is not None:
            place[0] += 1 if (index[0] + lat[index[2]]) % 2 == 0 else -1
            place[0] %= sizes[0]
        if lon is not None:
            place[1] += 1 if (index[1] + lon[index[2]]) % 2 == 0 else -1
            place[1] %= sizes[1]
        pairs.append(tuple((i[0] * sizes[1] + i[1]) * sizes[2] + i[2] for i in (index, place)))
    return pairs


def swap_cores(value):
    return lax.ppermute(value, "mem", [(i, i ^ 1) for i in range(lax.axis_size("mem"))])


def partner(value, axis, k):
    return lax.ppermute(value, axis, [(i, i ^ k) for i in range(lax.axis_size(axis))])


def per_device(velo, temp, land, target, w_first, w_middle, w_last):
    levels, rows, cols = temp.shape
    height, width = rows // COARSE, cols // COARSE
    wide = levels * (width + 2 * SIDE)
    vregs = wide // 128
    members = w_first.shape[0] * lax.axis_size("mem")
    nlat, nlon = lax.axis_size("lat"), lax.axis_size("lon")
    total_coarse = height * nlat
    count = 2.0 * levels * total_coarse * width * nlon
    params = pltpu.CompilerParams(vmem_limit_bytes=VMEM_LIMIT)
    vm = pltpu.VMEM

    def f32(*shape):
        return jax.ShapeDtypeStruct(shape, F32)

    def bf16(*shape):
        return jax.ShapeDtypeStruct(shape, BF16)

    hid = w_middle.shape[-1]
    hbm = pl.BlockSpec(memory_space=pltpu.HBM)
    tall = 8 * height
    core = (0, 1)
    raw = (jnp.transpose(w_first, (1, 3, 0, 2)), w_middle, w_last)
    to_lon, velo, temp, target, *raw = pl.pallas_call(
        edge_kernel,
        in_specs=[hbm] * 6,
        out_shape=(
            vm((tall + 2 * rows, 128), BF16),
            vm(velo.shape, F32),
            vm(temp.shape, F32),
            vm(target.shape, BF16),
            *(vm(w.shape, BF16) for w in raw),
        ),
        scratch_shapes=[
            vm((2, levels * rows, 128), F32),
            vm((2, tall, 128), F32),
            pltpu.SemaphoreType.DMA((7,)),
        ],
        compiler_params=pltpu.CompilerParams(vmem_limit_bytes=COARSE_LIMIT),
        name="edge",
    )(velo, temp, target, *raw)
    everywhere = ("lat", "lon", "mem")
    got_lon = lax.ppermute(to_lon, everywhere, pairs_of(lon=core))
    own, edges = pl.pallas_call(
        coarse_kernel,
        out_shape=(vm((vregs, tall, 128), F32), vm((2, 3 * levels * (cols // 128), 128), F32)),
        scratch_shapes=[vm((cols // 128, levels * rows, 128), F32)],
        cost_estimate=pl.CostEstimate(flops=5 * 10**8, bytes_accessed=2 * 10**6, transcendentals=0),
        compiler_params=params,
        name="coarse",
    )(velo, temp, target)
    got_lon, own, edges = lax.optimization_barrier((got_lon, own, edges))
    weights = pl.pallas_call(
        weights_kernel,
        out_shape=(
            bf16(H1_ROWS * 2 * hid, 16 * (H1_ROWS + 2)),
            bf16(2, 2 * hid, 12 * hid),
            bf16(2, 2 * hid, 12 * hid),
            bf16(64, 4 * hid),
            bf16(2 * hid, 48),
        ),
        cost_estimate=pl.CostEstimate(flops=10**8, bytes_accessed=4 * 10**6, transcendentals=0),
        compiler_params=params,
        name="weights",
    )(*raw)
    other_lon = swap_cores(got_lon)
    message = bf16(-(-PACKED * vregs // 16) * 16 + 2 * edges.shape[1], 128)
    full, to_lat = pl.pallas_call(
        merge_kernel,
        out_shape=(f32(vregs, tall, 128), message),
        compiler_params=params,
        name="merge",
    )(own, got_lon, other_lon, edges)
    got_lat = lax.ppermute(to_lat, everywhere, pairs_of(lat=core))
    wf, wm, wb, wl, wlt = weights
    tops = pl.pallas_call(
        inner_kernel,
        out_shape=(vm((3, 2, 64 * (height - 2), wide), BF16), vm((128 * (height - 4), wide), BF16)),
        scratch_shapes=[vm((16 * height, wide), BF16)],
        cost_estimate=pl.CostEstimate(flops=10**9, bytes_accessed=4 * 10**6, transcendentals=0),
        compiler_params=params,
        name="inner",
    )(full, wf, wm)
    got_lat, tops, weights = lax.optimization_barrier((got_lat, tops, (wf, wm, wb, wl, wlt)))
    other_lat = swap_cores(got_lat)

    total = -(-576 // (GROUP * nlat)) * GROUP * nlat
    part = total // nlat
    coded = jax.ShapeDtypeStruct((part + GROUP, 128), jnp.int16)
    wf, wm, wb, wl, wlt = weights
    force, *rest = pl.pallas_call(
        functools.partial(closure_kernel, 2.0 / count, total_coarse),
        out_shape=(
            bf16(2 * height, wide),
            *[coded] * (nlat - 1),
            f32(part, 128),
            vm((16 * (height + 2 * HALO), wide), BF16),
            vm((2, 64 * height, wide), BF16),
            vm((128 * (height + 6), wide), BF16),
            vm((16 * (height + 4), wide), BF16),
            vm((3, 2, 64 * (height + 2), wide), BF16),
        ),
        scratch_shapes=[
            vm((8 * (height + 2 * HALO), wide), F32),
            vm((3, 2, 64 * (height + 8), wide), BF16),
            vm((32 * (height + 6), wide), F32),
            vm((2 * height, wide), F32),
            vm((total, 128), F32),
        ],
        compiler_params=params,
        name="closure",
    )(full, got_lat, other_lat, *tops, wf, wm, wl, wlt)
    sends, (mine, *kept) = rest[: nlat - 1], rest[nlat - 1 :]

    other = swap_cores(force)
    parts = [partner(sends[k - 1], "lat", k) for k in reversed(range(1, nlat))][::-1]
    outer = pl.pallas_call(
        outer_grads_kernel,
        out_shape=f32(48, 128),
        cost_estimate=pl.CostEstimate(flops=2 * 10**9, bytes_accessed=4 * 10**6, transcendentals=0),
        compiler_params=params,
        name="outer_grads",
    )(*kept, wb)
    def add_up(kernel, values, name):
        return pl.pallas_call(
            kernel,
            out_shape=jax.ShapeDtypeStruct((part + 48 + GROUP, 128), jnp.int16),
            compiler_params=params,
            name=name,
        )(*values)

    parts, other = lax.optimization_barrier((parts, other))
    summed = add_up(sum_lat_kernel, [mine, outer, *parts], "sum_lat")
    velo_next, temp_next = pl.pallas_call(
        functools.partial(ocean_kernel, rows * nlat, members),
        out_shape=(jax.ShapeDtypeStruct(velo.shape, F32), jax.ShapeDtypeStruct(temp.shape, F32)),
        cost_estimate=pl.CostEstimate(flops=10**8, bytes_accessed=4 * 10**6, transcendentals=0),
        compiler_params=params,
        name="ocean",
    )(velo, temp, land, force, other, got_lon, other_lon, got_lat, other_lat)
    parts = [summed] + [partner(summed, "lon", k) for k in range(1, nlon)]
    parts, velo_next, temp_next = lax.optimization_barrier((parts, velo_next, temp_next))
    summed = add_up(sum_lon_kernel, parts, "sum_lon")
    parts = [summed] + [partner(summed, "lat", k) for k in range(1, nlat)]
    members_here, taps, _, inputs = w_first.shape
    first, middle, last = pl.pallas_call(
        finish_kernel,
        out_shape=(f32(taps, inputs, members_here, hid), f32(*w_middle.shape), f32(*w_last.shape)),
        scratch_shapes=[vm((total, 128), F32)],
        compiler_params=params,
        name="finish",
    )(*parts)
    return (velo_next, temp_next, jnp.transpose(first, (2, 0, 3, 1)), middle, last)


def solution(mesh):
    return jax.shard_map(
        per_device,
        mesh=mesh,
        in_specs=(
            P(None, None, "lat", "lon"),
            P(None, "lat", "lon"),
            P("lat", "lon"),
            P(None, None, "lat", "lon"),
            P("mem", None, None, None),
            P("mem", None, None, None),
            P("mem", None, None, None),
        ),
        out_specs=(
            P(None, None, "lat", "lon"),
            P(None, "lat", "lon"),
            P("mem", None, None, None),
            P("mem", None, None, None),
            P("mem", None, None, None),
        ),
        check_vma=False,
    )
```

```python
import functools
import itertools
import math

import jax
import jax.numpy as jnp
from jax import lax
from jax.experimental import pallas as pl
from jax.experimental.pallas import tpu as pltpu
from jax.sharding import PartitionSpec as P

COARSE = 4
HALO = 5
PACKED = 3 * HALO + 4
GROUP = 16
LEVELS = 32000.0
H1_ROWS = 4
SIDE = 16
F32 = jnp.float32
BF16 = jnp.bfloat16
VMEM_LIMIT = 32 * 1024 * 1024
COARSE_LIMIT = 60 * 1024 * 1024


def dot(a, b, **kw):
    return jnp.dot(a, b, preferred_element_type=F32, **kw)


def dot_nt(a, b):
    return lax.dot_general(a, b, (((1,), (1,)), ((), ())), preferred_element_type=F32)


def lanes_of(shape):
    return lax.broadcasted_iota(jnp.int32, shape, len(shape) - 1)


def subs_of(shape):
    return lax.broadcasted_iota(jnp.int32, shape, len(shape) - 2)


def heads_up(axis):
    return (lax.axis_index(axis) + lax.axis_index("mem")) % 2 == 0


def north_and_south(got, other):
    ahead, place = heads_up("lat"), lax.axis_index("lat")
    north, south = jnp.where(ahead, got, other), jnp.where(ahead, other, got)
    return jnp.where(place < lax.axis_size("lat") - 1, north, 0.0), jnp.where(place > 0, south, 0.0)


def halves(x):
    high = x.astype(BF16).astype(F32)
    return [high, x - high]


def encode(x):
    coded, exponents = [], []
    for at in range(0, x.shape[0], GROUP):
        part = x[at : at + GROUP]
        most = jnp.max(jnp.abs(part), axis=0, keepdims=True)
        exponent = jnp.ceil(jnp.log2(jnp.maximum(most, 1e-30)))
        coded.append(jnp.round(part * (jnp.exp2(-exponent) * LEVELS)))
        exponents.append(exponent)
    exponents.append(jnp.zeros((GROUP - len(exponents), x.shape[1]), F32))
    return jnp.concatenate(coded + exponents, 0).astype(jnp.int32).astype(jnp.int16)


def decode(ref):
    value = ref[...].astype(jnp.int32).astype(F32)
    rows = value.shape[0] - GROUP
    scale = jnp.exp2(value[rows:]) * (1.0 / LEVELS)
    pieces = [value[at : at + GROUP] * scale[i : i + 1] for i, at in enumerate(range(0, rows, GROUP))]
    return jnp.concatenate(pieces, 0)


def row_sums(ref, fine, spans):
    levels, rows, _ = ref.shape
    for j, span in enumerate(spans):
        fine[j] = ref[:, :, span].reshape(levels * rows, 128)
    step = levels * rows // COARSE
    return [
        sum(fine[j, pl.ds(s, step, stride=COARSE), :] for s in range(COARSE)) for j in range(len(spans))
    ]


def pool_columns(x):
    cols = x.shape[1]
    here = subs_of((cols, 128)) // COARSE == lanes_of((cols, 128))
    pool = jnp.where(here, F32(1.0 / COARSE**2), F32(0.0)).astype(BF16)
    high, rest = halves(x)
    terms = jnp.concatenate([high] + halves(rest), 0).astype(BF16)
    y = dot(terms, pool)
    size = x.shape[0]
    return ((y[2 * size :] + y[size : 2 * size]) + y[:size]).astype(BF16).astype(F32)


def edge_kernel(velo_hbm, temp_hbm, target_hbm, *refs):
    from_hbm, (to_lon, velo, temp, target, *weights), (fine, cells, sems) = refs[:3], refs[3:10], refs[10:]
    levels, rows, cols = temp.shape
    height = rows // COARSE
    pairs = [(velo_hbm.at[0], velo.at[0]), (velo_hbm.at[1], velo.at[1]), (temp_hbm, temp), (target_hbm, target)]
    pairs += zip(from_hbm, weights)
    copies = [pltpu.make_async_copy(*pair, sems.at[i]) for i, pair in enumerate(pairs)]
    for copy in copies:
        copy.start()
    spans = (slice(0, 128), slice(cols - 128, cols))
    sums = []
    for f in range(3):
        copies[f].wait()
        sums += row_sums(temp if f == 2 else velo.at[f], fine, spans)
    mean = pool_columns(jnp.concatenate(sums, 0))
    copies[3].wait()
    lane = lanes_of((height, 128))
    cells[...] = jnp.zeros_like(cells)
    for side in range(2):
        begin = SIDE - HALO * side
        for ch in range(7):
            total = jnp.zeros((height, 128), F32)
            for l in range(levels):
                if ch < 4:
                    x, shift = target[ch % 2, l].astype(F32), SIDE
                else:
                    at = ((2 * (ch - 4) + side) * levels + l) * height
                    x, shift = mean[at : at + height], SIDE if side == 0 else SIDE - 128 // COARSE
                at = 32 * l + begin
                total = jnp.where((lane >= at) & (lane < at + HALO), pltpu.roll(x, (32 * l + shift) % 128, 1), total)
            cells[side, pl.ds(ch, height, stride=8), :] = total
    lane = lanes_of((rows, 128))
    first = jnp.zeros((rows, 128), F32)
    last = jnp.zeros((rows, 128), F32)
    for f in range(3):
        ref = temp if f == 2 else velo.at[f]
        for l in range(levels):
            n = f * levels + l
            first = jnp.where(lane == n, pltpu.roll(ref[l, :, 0:128], n, 1), first)
            last = jnp.where(lane == n, pltpu.roll(ref[l, :, cols - 128 :], n + 1, 1), last)
    west, east = (jnp.concatenate([cells[i]] + halves(x), 0) for i, x in enumerate((first, last)))
    to_lon[...] = jnp.where(heads_up("lon"), east, west).astype(BF16)
    for copy in copies[4:]:
        copy.wait()


def coarse_kernel(velo, temp, target, own, edges, fine):
    levels, rows, cols = temp.shape
    height, width = rows // COARSE, cols // COARSE
    vregs = levels + 1
    spans = [slice(128 * j, 128 * (j + 1)) for j in range(cols // 128)]

    def field(f):
        return temp if f == 2 else velo.at[f]

    mean = pool_columns(jnp.concatenate([jnp.concatenate(row_sums(field(f), fine, spans), 1) for f in range(3)], 0))
    lane = lanes_of((height, 128))

    def place(tiles):
        pieces = []
        for j in range(vregs):
            value = jnp.zeros((height, 128), F32)
            if j < levels:
                moved = pltpu.roll(tiles[j], 32 * j + SIDE, 1)
                value = jnp.where(lane >= 32 * j + SIDE, moved, value)
            if j > 0:
                moved = pltpu.roll(tiles[j - 1], 32 * (j - 1) + SIDE, 1)
                value = jnp.where(lane < 32 * (j - 1) + SIDE, moved, value)
            pieces.append(value)
        return pieces

    for ch in range(8):
        if ch < 4:
            tiles = [target[ch % 2, l].astype(F32) for l in range(levels)]
        elif ch < 7:
            base = (ch - 4) * levels * height
            tiles = [mean[base + l * height : base + (l + 1) * height] for l in range(levels)]
        if ch < 7:
            pieces = place(tiles)
        else:
            pieces = [jnp.zeros((height, 128), F32)] * vregs
        for j in range(vregs):
            own[j, pl.ds(ch, height, stride=8), :] = pieces[j]
    for i, row in enumerate((rows - 1, 0)):
        line = [field(f)[:, row, 128 * j : 128 * (j + 1)] for j in range(cols // 128) for f in range(3)]
        edges[i] = jnp.concatenate(line, 0)


def merge_kernel(own, got, other, edges, full, message):
    vregs, tall = own.shape[:2]
    levels = vregs - 1
    ahead = heads_up("lon")
    near, far = (ref[...].astype(F32)[0:tall] for ref in (got, other))
    right, left = jnp.where(ahead, near, far), jnp.where(ahead, far, near)
    lane = lanes_of((tall, 128))
    upper, lower = [], []
    for j in range(vregs):
        value = own[j]
        if j < levels:
            at = 32 * j + SIDE
            value = jnp.where((lane >= at - HALO) & (lane < at), left, value)
        if j > 0:
            at = 32 * (j - 1) + SIDE
            value = jnp.where((lane >= at) & (lane < at + HALO), right, value)
        full[j] = value
        last = tall // 8
        for pieces, first, goals in ((upper, last - HALO, (last - 2, last - 1)), (lower, 0, (0, 1))):
            pieces += [value[8 * r + 4 : 8 * r + 7] for r in range(first, first + HALO)]
            pieces += [value[8 * r : 8 * r + 2] for r in goals]
    pad = [jnp.zeros((-PACKED * vregs % 16, 128), F32)]
    upper, lower = (jnp.concatenate(x + pad + halves(edges[i]), 0) for i, x in enumerate((upper, lower)))
    message[...] = jnp.where(heads_up("lat"), upper, lower).astype(BF16)


def unpack(message, j, goal_rows):
    at = PACKED * j
    rows = []
    for i in range(HALO):
        goal = jnp.zeros((2, 128), F32)
        if i in goal_rows:
            start = at + 3 * HALO + 2 * goal_rows.index(i)
            goal = message[start : start + 2]
        rows += [goal, goal, message[at + 3 * i : at + 3 * (i + 1)], jnp.zeros((1, 128), F32)]
    return jnp.concatenate(rows, 0)


def add(sums, name, term):
    sums[name] = sums[name] + term if name in sums else term


def window(ref, row, rows, step):
    return ref[step * row : step * (row + rows), :]


def quad(get, row, left):
    return get(row) if left <= 2 else jnp.concatenate([get(row), get(row + 2)], 1)


def taps(ref, m, row):
    return jnp.concatenate([ref[b, m, 64 * row : 64 * (row + 4), :] for b in range(3)], 0)


def columns_around(x):
    wide = x.shape[1]
    return [pltpu.roll(x, 1, 1), x, pltpu.roll(x, wide - 1, 1)]


def spread_columns(x):
    wide = x.shape[1]
    one = jnp.where(subs_of(x.shape) < 4, pltpu.roll(pltpu.roll(x, 1, 1), 4, 0), x)
    two = pltpu.roll(pltpu.roll(x, wide - 1, 1), 4, 0)
    return jnp.concatenate([one, two], 0).astype(BF16)


def inner_kernel(full, wf, wm, h1, h2, xb):
    vregs, height = full.shape[0], full.shape[1] // 8
    wide = 128 * vregs
    for r in range(height):
        x = jnp.concatenate([full[j, 8 * r : 8 * (r + 1), :] for j in range(vregs)], 1)
        xb[16 * r : 16 * (r + 1), :] = spread_columns(x)
    half = (height - 2) // 2
    y = dot(wf[0 : 128 * half, 0 : 16 * (half + 2)], jnp.concatenate([window(xb, r, half + 2, 16) for r in (0, half)], 1))
    for i in range(2 * half):
        t = i // half
        h = jnp.tanh(y[128 * (i - t * half) : 128 * (i - t * half + 1), wide * t : wide * (t + 1)]).astype(BF16)
        for m in range(2):
            for b, moved in enumerate(columns_around(h[64 * m : 64 * (m + 1)])):
                h1[b, m, 64 * i : 64 * (i + 1), :] = moved
    for p in range(0, height - 4, 4):
        for m in range(2):
            y = dot(wm[m], quad(lambda r: taps(h1, m, r), p, 4))
            for i in range(4):
                pre = y[64 * (i % 2) : 64 * (i % 2 + 1), wide * (i // 2) : wide * (i // 2 + 1)]
                at = 128 * (p + i) + 64 * m
                h2[at : at + 64, :] = jnp.tanh(pre).astype(BF16)


def inner_lanes(wide):
    within = lanes_of((1, wide)) % (128 + 2 * SIDE)
    return jnp.where((within >= SIDE) & (within < SIDE + 128), F32(1.0), F32(0.0))


def closure_kernel(
    scale, total_rows,
    full, got, other, h1_inner, h2_inner, xb_inner, wf, wm, wl, wlt,
    force, *rest,
):
    nlat = lax.axis_size("lat")
    sends, (mine, xb, inner, h2, gb, d2, xf, h1, yl, pf, packed) = rest[: nlat - 1], rest[nlat - 1 :]
    vregs = full.shape[0]
    height = full.shape[1] // 8
    wide = 128 * vregs
    span = height + 2 * HALO
    first_row = lax.axis_index("lat") * height

    def inside(row):
        at = first_row + row
        return jnp.where((at >= 0) & (at < total_rows), F32(1.0), F32(0.0))

    north, south = north_and_south(got[...].astype(F32), other[...].astype(F32))
    for j in range(vregs):
        above, below = unpack(north, j, (0, 1)), unpack(south, j, (HALO - 2, HALO - 1))
        xf[:, 128 * j : 128 * (j + 1)] = jnp.concatenate([below, full[j], above], 0)

    sub = subs_of((8, wide))
    tile_b = inner_lanes(wide).astype(BF16)

    xb[16 * HALO : 16 * (HALO + height), :] = xb_inner[...]
    for r in (*range(HALO), *range(HALO + height, span)):
        xb[16 * r : 16 * (r + 1), :] = spread_columns(window(xf, r, 1, 8))

    known = range(5, height + 3)

    def h1_row(b, m, i):
        ref, at = (h1_inner, i - known[0]) if i in known else (h1, i)
        return ref[b, m, 64 * at : 64 * (at + 1), :]

    def make_h1(starts, count):
        weights = wf[0 : 128 * count, 0 : 16 * (count + 2)]
        y = dot(weights, jnp.concatenate([window(xb, r, count + 2, 16) for r in starts], 1))
        for t, start in enumerate(starts):
            for i in range(count):
                pre = y[128 * i : 128 * (i + 1), wide * t : wide * (t + 1)]
                h = (jnp.tanh(pre) * inside(start + i - 4)).astype(BF16)
                for m in range(2):
                    at = 64 * (start + i)
                    for b, moved in enumerate(columns_around(h[64 * m : 64 * (m + 1)])):
                        h1[b, m, at : at + 64, :] = moved

    def h1_rows(b, m, row):
        return jnp.concatenate([h1_row(b, m, row + i) for i in range(4)], 0)

    rows = height + 6
    h2[128 * 5 : 128 * (height + 1), :] = h2_inner[...]

    def make_h2(starts, count):
        for m in range(2):
            windows = [jnp.concatenate([h1_rows(b, m, r) for b in range(3)], 0) for r in starts]
            y = dot(wm[m, 0 : 64 * count, :], jnp.concatenate(windows, 1))
            for t, start in enumerate(starts):
                for i in range(count):
                    pre = y[64 * i : 64 * (i + 1), wide * t : wide * (t + 1)]
                    h = jnp.tanh(pre) * inside(start + i - 3)
                    at = 128 * (start + i) + 64 * m
                    h2[at : at + 64, :] = h.astype(BF16)

    def make_yl(p):
        y = dot(wl[...], quad(lambda r: window(h2, r, 2, 128), p, rows - p))
        for t in range(y.shape[1] // wide):
            at = 32 * (p + 2 * t)
            yl[at : at + 64, :] = y[:, wide * t : wide * (t + 1)]

    def make_g3(s):
        z = 0.0
        for pair in ((s, s + 2) if s % 2 == 0 else (s - 1, s + 1)):
            at = 32 * pair + 16 * (s + 2 - pair)
            z = z + yl[at : at + 16, :]
        pred = pltpu.roll(z[0:8], 1, 1) + pltpu.roll(z[0:8], 4, 0) + pltpu.roll(z[8:16], wide - 1, 1)
        goal = window(xf, s + 3, 1, 8)
        g = ((pred - goal) * scale * inside(s - 2)).astype(BF16).astype(F32)
        one = jnp.where(sub < 4, pltpu.roll(g, wide - 1, 1), pltpu.roll(g, 4, 0))
        two = pltpu.roll(g, 1, 1)
        gb[16 * s : 16 * (s + 1), :] = jnp.concatenate([one, two], 0).astype(BF16)
        if 2 <= s < height + 2:
            both = pred + pltpu.roll(pred, 6, 0)
            pf[2 * (s - 2) : 2 * (s - 1), :] = both[0:2]

    def make_d2(u):
        y = dot(wlt[...], jnp.concatenate([window(gb, r, 3, 16) for r in (u, u + 1)], 1))
        for t in range(2):
            hidden = window(h2, u + t + 2, 1, 128).astype(F32)
            d = y[:, wide * t : wide * (t + 1)] * (1.0 - hidden * hidden) * inside(u + t - 1)
            for m in range(2):
                for b, moved in enumerate(columns_around(d[64 * m : 64 * (m + 1)].astype(BF16))):
                    d2[b, m, 64 * (u + t) : 64 * (u + t + 1), :] = moved

    sums = {}

    def make_grads(j):
        left = height - j
        for m in range(2):

            def moved(r):
                return jnp.concatenate([d2[b, m, 64 * (r + 1) : 64 * (r + 3), :] for b in (2, 1, 0)], 0)

            rhs = quad(lambda r: h1_rows(1, m, r + 3) * tile_b, j, left)
            add(sums, m, dot_nt(quad(moved, j, left), rhs))

    make_h1((0, height + 4), 4)
    make_h1((4, height + 3), 1)
    make_h2((0, 2), 2)
    make_h2((4, height + 1), 1)
    for p in range(0, height, 4):
        make_yl(p)
    make_h2((height + 2, height + 4), 2)
    for p in range(height, rows, 4):
        make_yl(p)
    for m in range(2):
        for r in range(height):
            inner[m, 64 * r : 64 * (r + 1), :] = h1_row(1, m, r + 4)
    for r in range(height + 4):
        make_g3(r)
    for u in range(0, height + 2, 2):
        make_d2(u)
    for j in range(0, height, 4):
        make_grads(j)
    force[...] = pf[...].astype(BF16)
    gm = []
    for m in range(2):
        parts = [sums[m][64 * i : 64 * (i + 1)] for i in range(6)]
        gm.append(jnp.concatenate([parts[2 * b][:, 0:192] + parts[2 * b + 1][:, 64:256] for b in range(3)], 0))
    for m in range(2):
        packed[192 * m : 192 * (m + 1), :] = gm[m][:, 0:128]
    packed[384:576, :] = jnp.concatenate([gm[0][:, 128:192], gm[1][:, 128:192]], 1)
    if packed.shape[0] > 576:
        packed[576:, :] = jnp.zeros((packed.shape[0] - 576, 128), F32)
    part = packed.shape[0] // nlat
    me = lax.axis_index("lat")
    for k, ref in enumerate((mine, *sends)):
        value = packed[pl.ds(pl.multiple_of((me ^ k) * part, 8), part), :]
        ref[...] = value if k == 0 else encode(value)


def outer_grads_kernel(xb, inner, h2, gb, d2, wb, out):
    wide = xb.shape[1]
    height = xb.shape[0] // 16 - 2 * HALO
    mask = inner_lanes(wide)
    sums = {}
    for j in range(0, height, 4):
        left = height - j
        g = quad(lambda r: window(gb, r + 1, 4, 16) * mask.astype(BF16), j, left)
        add(sums, "l", dot_nt(g, quad(lambda r: window(h2, r + 3, 2, 128), j, left)))
        d1 = [[None, None] for _ in range(4)]
        for m in range(2):
            y = dot(wb[m], quad(lambda r: taps(d2, m, r), j, left))
            for i in range(4):
                hidden = inner[m, 64 * (j + i) : 64 * (j + i + 1), :].astype(F32)
                pre = y[64 * (i % 2) : 64 * (i % 2 + 1), wide * (i // 2) : wide * (i // 2 + 1)]
                d1[i][m] = (pre * (1.0 - hidden * hidden) * mask).astype(BF16)
        x = quad(lambda r: window(xb, r + 4, 4, 16), j, left)
        add(sums, "f", dot_nt(x, quad(lambda r: jnp.concatenate(d1[r - j] + d1[r - j + 1], 0), j, left)))
    first, last = (sums[name][0:48, 0:128] + sums[name][16:64, 128:256] for name in "fl")
    last = jnp.where(lanes_of(last.shape) < 64, last, pltpu.roll(last, 46, 0))
    places = [(a, b) for a in range(3) for b in range(3)]
    pieces = [first[16 * a + 4 * b : 16 * a + 4 * b + 3] for a, b in places]
    pieces += [last[16 * a + 4 * b : 16 * a + 4 * b + 2] for a, b in places]
    out[...] = jnp.concatenate(pieces + [jnp.zeros((3, 128), F32)], 0)


def tree_sum(values):
    while len(values) > 1:
        values = [sum(values[i : i + 2][1:], values[i]) for i in range(0, len(values), 2)]
    return values[0]


def sum_lat_kernel(mine, outer, *refs):
    parts, out = refs[:-1], refs[-1]
    total = tree_sum([mine[...]] + [decode(ref) for ref in parts])
    out[...] = encode(jnp.concatenate([total, outer[...]], 0))


def sum_lon_kernel(*refs):
    parts, out = refs[:-1], refs[-1]
    out[...] = encode(tree_sum([decode(ref) for ref in parts]))


def finish_kernel(*refs):
    nlat = lax.axis_size("lat")
    parts, (first, middle, last, packed) = refs[:nlat], refs[nlat:]
    part = packed.shape[0] // nlat
    me = lax.axis_index("lat")
    values = [decode(ref) for ref in parts]
    for k, value in enumerate(values):
        packed[pl.ds(pl.multiple_of((me ^ k) * part, 8), part), :] = value[:part]
    outer = tree_sum([value[part:] for value in values])
    for m in range(2):
        for b in range(3):
            two = packed[192 * m + 64 * b : 192 * m + 64 * (b + 1), :]
            third = packed[384 + 64 * b : 384 + 64 * (b + 1), :]
            middle[m, b] = two[:, 0:64]
            middle[m, 3 + b] = two[:, 64:128]
            middle[m, 6 + b] = third[:, 64 * m : 64 * (m + 1)]
    for m in range(2):
        for k in range(9):
            for c in range(3):
                at = 3 * k + c
                first[k, c, m : m + 1] = outer[at : at + 1, 64 * m : 64 * (m + 1)]
            at = 27 + 2 * (3 * (2 - k // 3) + k % 3)
            last[m, k] = outer[at : at + 2, 64 * m : 64 * (m + 1)]


def ocean_kernel(
    total_rows, members,
    velo, temp, land, mine, other, got_lon, other_lon, got_lat, other_lat,
    velo_next, temp_next,
):
    levels, rows, cols = temp.shape

    def whole(ref, at, size):
        value = ref[...].astype(F32)
        return value[at : at + size] + value[at + size : at + 2 * size]

    ahead = heads_up("lon")
    near, far = (whole(ref, ref.shape[0] - 2 * rows, rows) for ref in (got_lon, other_lon))
    ceast, cwest = jnp.where(ahead, near, far), jnp.where(ahead, far, near)
    lines = 3 * levels * (cols // 128)
    near, far = (whole(ref, ref.shape[0] - 2 * lines, lines) for ref in (got_lat, other_lat))
    near, far = (
        jnp.concatenate([x[3 * levels * j : 3 * levels * (j + 1)] for j in range(cols // 128)], 1) for x in (near, far)
    )
    rnorth, rsouth = north_and_south(near, far)
    height, width = rows // COARSE, cols // COARSE
    row = subs_of((rows, cols))
    lane = lanes_of((rows, cols))
    ids = (lax.axis_index("lat") * rows + subs_of((rows, 128))).astype(F32)
    coriolis = jnp.sin(F32(-math.pi / 2) + F32(math.pi) * (ids + 0.5) / F32(total_rows))
    coriolis = jnp.concatenate([coriolis] * (cols // 128), 1)
    wet = land[...].astype(F32) * 0.1
    up = [
        jnp.where(lanes_of((rows, 2 * height)) == subs_of((rows, 2 * height)) // COARSE * 2 + o, F32(1.0), F32(0.0)).astype(BF16)
        for o in range(2)
    ]
    tall = [[dot(u, ref[...]).astype(BF16) for ref in (mine, other)] for u in up]
    spread_k = subs_of((256, cols))
    spread_i = lanes_of((256, cols)) // COARSE

    def neighbours(q, n):
        east = jnp.where(lane == cols - 1, ceast[:, n : n + 1], pltpu.roll(q, cols - 1, 1))
        west = jnp.where(lane == 0, cwest[:, n : n + 1], pltpu.roll(q, 1, 1))
        north = jnp.where(row == rows - 1, rnorth[n : n + 1], pltpu.roll(q, rows - 1, 0))
        south = jnp.where(row == 0, rsouth[n : n + 1], pltpu.roll(q, 1, 0))
        return east, west, north, south

    cum_x = cum_y = None
    for l in range(levels):
        u, v, t = velo[0, l], velo[1, l], temp[l]
        ue, uw, un, us = neighbours(u, l)
        ve, vw, vn, vs = neighbours(v, levels + l)
        te, tw, tn, ts = neighbours(t, 2 * levels + l)
        dx, dy = te - tw, tn - ts
        cum_x = dx if cum_x is None else cum_x + dx
        cum_y = dy if cum_y is None else cum_y + dy
        spread = jnp.where(spread_k == spread_i + (32 * l + SIDE), F32(1.0), F32(0.0)).astype(BF16)
        f = []
        for o in range(2):
            total = None
            for part in tall[o]:
                term = dot(part[:, 128 * l : 128 * (l + 2)], spread)
                total = term if total is None else total + term
            f.append(total * (1.0 / members))
        lap_u = ue + uw + un + us - 4.0 * u
        lap_v = ve + vw + vn + vs - 4.0 * v
        lap_t = te + tw + tn + ts - 4.0 * t
        velo_next[0, l] = u + wet * (coriolis * v + 0.25 * cum_x + 0.5 * lap_u + f[0])
        velo_next[1, l] = v + wet * (0.25 * cum_y - coriolis * u + 0.5 * lap_v + f[1])
        temp_next[l] = t + wet * (0.3 * lap_t - 0.5 * (u * dx + v * dy))


def weights_kernel(first, middle, last, wf, wm, wb, wl, wlt):
    hid = middle.shape[-1]

    def slide(pieces, copies):
        zero = jnp.zeros_like(pieces[0])
        return [jnp.concatenate([zero] * r + pieces + [zero] * (copies - 1 - r), 1) for r in range(copies)]

    for m in range(2):
        for b in range(3):
            taps = [middle[m, 3 * a + b] for a in range(3)]
            turned = jnp.concatenate([t.astype(F32) for t in taps[::-1]], 0).T.astype(BF16)
            turned = [turned[:, hid * s : hid * (s + 1)] for s in range(3)]
            for ref, pieces, at in ((wm, taps, b), (wb, turned, 2 - b)):
                for r, block in enumerate(slide(pieces, 2)):
                    ref[m, hid * r : hid * (r + 1), 4 * hid * at : 4 * hid * (at + 1)] = block
    zero = jnp.zeros((1, 2 * hid), F32)
    rows = []
    for a in range(3):
        for b in range(4):
            for c in range(4):
                if b < 3 and c < 3:
                    w = first[3 * a + b, c].astype(F32)
                    rows.append(jnp.concatenate([w[0:1], w[1:2]], 1))
                else:
                    rows.append(zero)
    turned = jnp.concatenate(rows + [zero] * (2 * hid - 48), 0).T
    for r in range(H1_ROWS):
        wf[2 * hid * r : 2 * hid * (r + 1), :] = pltpu.roll(turned, 16 * r, 1).astype(BF16)[:, : wf.shape[1]]
    zero = jnp.zeros((2, hid), F32)
    by_row = []
    for a in range(3):
        rows = []
        for b in range(3):
            w = [last[m, 3 * a + b].astype(F32) for m in range(2)]
            rows += [jnp.concatenate([w[0], zero], 1), jnp.concatenate([zero, w[1]], 1)]
        by_row.append(jnp.concatenate(rows + [jnp.zeros((4, 2 * hid), F32)], 0))
    none = jnp.zeros((16, 2 * hid), F32)
    for e in range(-1, 3):
        taps = [by_row[r - e + 1] if abs(r - e) <= 1 else none for r in range(2)]
        wl[16 * (e + 1) : 16 * (e + 2), :] = jnp.concatenate(taps, 1).astype(BF16)
    wlt[...] = jnp.concatenate(by_row[::-1], 0).T.astype(BF16)


def pairs_of(lat=None, lon=None):
    sizes = [lax.axis_size(name) for name in ("lat", "lon", "mem")]
    pairs = []
    for index in itertools.product(*(range(n) for n in sizes)):
        place = list(index)
        if lat is not None:
            place[0] += 1 if (index[0] + lat[index[2]]) % 2 == 0 else -1
            place[0] %= sizes[0]
        if lon is not None:
            place[1] += 1 if (index[1] + lon[index[2]]) % 2 == 0 else -1
            place[1] %= sizes[1]
        pairs.append(tuple((i[0] * sizes[1] + i[1]) * sizes[2] + i[2] for i in (index, place)))
    return pairs


def swap_cores(value):
    return lax.ppermute(value, "mem", [(i, i ^ 1) for i in range(lax.axis_size("mem"))])


def partner(value, axis, k):
    return lax.ppermute(value, axis, [(i, i ^ k) for i in range(lax.axis_size(axis))])


def per_device(velo, temp, land, target, w_first, w_middle, w_last):
    levels, rows, cols = temp.shape
    height, width = rows // COARSE, cols // COARSE
    wide = levels * (width + 2 * SIDE)
    vregs = wide // 128
    members = w_first.shape[0] * lax.axis_size("mem")
    nlat, nlon = lax.axis_size("lat"), lax.axis_size("lon")
    total_coarse = height * nlat
    count = 2.0 * levels * total_coarse * width * nlon
    params = pltpu.CompilerParams(vmem_limit_bytes=VMEM_LIMIT)
    vm = pltpu.VMEM

    def f32(*shape):
        return jax.ShapeDtypeStruct(shape, F32)

    def bf16(*shape):
        return jax.ShapeDtypeStruct(shape, BF16)

    hid = w_middle.shape[-1]
    hbm = pl.BlockSpec(memory_space=pltpu.HBM)
    tall = 8 * height
    core = (0, 1)
    raw = (jnp.transpose(w_first, (1, 3, 0, 2)), w_middle, w_last)
    to_lon, velo, temp, target, *raw = pl.pallas_call(
        edge_kernel,
        in_specs=[hbm] * 6,
        out_shape=(
            vm((tall + 2 * rows, 128), BF16),
            vm(velo.shape, F32),
            vm(temp.shape, F32),
            vm(target.shape, BF16),
            *(vm(w.shape, BF16) for w in raw),
        ),
        scratch_shapes=[
            vm((2, levels * rows, 128), F32),
            vm((2, tall, 128), F32),
            pltpu.SemaphoreType.DMA((7,)),
        ],
        compiler_params=pltpu.CompilerParams(vmem_limit_bytes=COARSE_LIMIT),
        name="edge",
    )(velo, temp, target, *raw)
    everywhere = ("lat", "lon", "mem")
    got_lon = lax.ppermute(to_lon, everywhere, pairs_of(lon=core))
    own, edges = pl.pallas_call(
        coarse_kernel,
        out_shape=(vm((vregs, tall, 128), F32), vm((2, 3 * levels * (cols // 128), 128), F32)),
        scratch_shapes=[vm((cols // 128, levels * rows, 128), F32)],
        cost_estimate=pl.CostEstimate(flops=5 * 10**8, bytes_accessed=2 * 10**6, transcendentals=0),
        compiler_params=params,
        name="coarse",
    )(velo, temp, target)
    got_lon, own, edges = lax.optimization_barrier((got_lon, own, edges))
    weights = pl.pallas_call(
        weights_kernel,
        out_shape=(
            bf16(H1_ROWS * 2 * hid, 16 * (H1_ROWS + 2)),
            bf16(2, 2 * hid, 12 * hid),
            bf16(2, 2 * hid, 12 * hid),
            bf16(64, 4 * hid),
            bf16(2 * hid, 48),
        ),
        cost_estimate=pl.CostEstimate(flops=10**8, bytes_accessed=4 * 10**6, transcendentals=0),
        compiler_params=params,
        name="weights",
    )(*raw)
    other_lon = swap_cores(got_lon)
    message = bf16(-(-PACKED * vregs // 16) * 16 + 2 * edges.shape[1], 128)
    full, to_lat = pl.pallas_call(
        merge_kernel,
        out_shape=(f32(vregs, tall, 128), message),
        compiler_params=params,
        name="merge",
    )(own, got_lon, other_lon, edges)
    got_lat = lax.ppermute(to_lat, everywhere, pairs_of(lat=core))
    wf, wm, wb, wl, wlt = weights
    tops = pl.pallas_call(
        inner_kernel,
        out_shape=(
            vm((3, 2, 64 * (height - 2), wide), BF16),
            vm((128 * (height - 4), wide), BF16),
            vm((16 * height, wide), BF16),
        ),
        cost_estimate=pl.CostEstimate(flops=10**9, bytes_accessed=4 * 10**6, transcendentals=0),
        compiler_params=params,
        name="inner",
    )(full, wf, wm)
    got_lat, tops, weights = lax.optimization_barrier((got_lat, tops, (wf, wm, wb, wl, wlt)))
    other_lat = swap_cores(got_lat)

    total = -(-576 // (GROUP * nlat)) * GROUP * nlat
    part = total // nlat
    coded = jax.ShapeDtypeStruct((part + GROUP, 128), jnp.int16)
    wf, wm, wb, wl, wlt = weights
    force, *rest = pl.pallas_call(
        functools.partial(closure_kernel, 2.0 / count, total_coarse),
        out_shape=(
            bf16(2 * height, wide),
            *[coded] * (nlat - 1),
            f32(part, 128),
            vm((16 * (height + 2 * HALO), wide), BF16),
            vm((2, 64 * height, wide), BF16),
            vm((128 * (height + 6), wide), BF16),
            vm((16 * (height + 4), wide), BF16),
            vm((3, 2, 64 * (height + 2), wide), BF16),
        ),
        scratch_shapes=[
            vm((8 * (height + 2 * HALO), wide), F32),
            vm((3, 2, 64 * (height + 8), wide), BF16),
            vm((32 * (height + 6), wide), F32),
            vm((2 * height, wide), F32),
            vm((total, 128), F32),
        ],
        compiler_params=params,
        name="closure",
    )(full, got_lat, other_lat, *tops, wf, wm, wl, wlt)
    sends, (mine, *kept) = rest[: nlat - 1], rest[nlat - 1 :]

    other = swap_cores(force)
    parts = [partner(sends[k - 1], "lat", k) for k in reversed(range(1, nlat))][::-1]
    outer = pl.pallas_call(
        outer_grads_kernel,
        out_shape=f32(48, 128),
        cost_estimate=pl.CostEstimate(flops=2 * 10**9, bytes_accessed=4 * 10**6, transcendentals=0),
        compiler_params=params,
        name="outer_grads",
    )(*kept, wb)
    def add_up(kernel, values, name):
        return pl.pallas_call(
            kernel,
            out_shape=jax.ShapeDtypeStruct((part + 48 + GROUP, 128), jnp.int16),
            compiler_params=params,
            name=name,
        )(*values)

    parts, other = lax.optimization_barrier((parts, other))
    summed = add_up(sum_lat_kernel, [mine, outer, *parts], "sum_lat")
    velo_next, temp_next = pl.pallas_call(
        functools.partial(ocean_kernel, rows * nlat, members),
        out_shape=(jax.ShapeDtypeStruct(velo.shape, F32), jax.ShapeDtypeStruct(temp.shape, F32)),
        cost_estimate=pl.CostEstimate(flops=10**8, bytes_accessed=4 * 10**6, transcendentals=0),
        compiler_params=params,
        name="ocean",
    )(velo, temp, land, force, other, got_lon, other_lon, got_lat, other_lat)
    parts = [summed] + [partner(summed, "lon", k) for k in range(1, nlon)]
    parts, velo_next, temp_next = lax.optimization_barrier((parts, velo_next, temp_next))
    summed = add_up(sum_lon_kernel, parts, "sum_lon")
    parts = [summed] + [partner(summed, "lat", k) for k in range(1, nlat)]
    members_here, taps, _, inputs = w_first.shape
    first, middle, last = pl.pallas_call(
        finish_kernel,
        out_shape=(f32(taps, inputs, members_here, hid), f32(*w_middle.shape), f32(*w_last.shape)),
        scratch_shapes=[vm((total, 128), F32)],
        compiler_params=params,
        name="finish",
    )(*parts)
    return (velo_next, temp_next, jnp.transpose(first, (2, 0, 3, 1)), middle, last)


def solution(mesh):
    return jax.shard_map(
        per_device,
        mesh=mesh,
        in_specs=(
            P(None, None, "lat", "lon"),
            P(None, "lat", "lon"),
            P("lat", "lon"),
            P(None, None, "lat", "lon"),
            P("mem", None, None, None),
            P("mem", None, None, None),
            P("mem", None, None, None),
        ),
        out_specs=(
            P(None, None, "lat", "lon"),
            P(None, "lat", "lon"),
            P("mem", None, None, None),
            P("mem", None, None, None),
            P("mem", None, None, None),
        ),
        check_vma=False,
    )
```
